32 devices in a mesh: rep: 8 (over z, y), shard: 4 (over x, core).
Axes of the slice: x: 2, y: 2, z: 4, core: 2. Of those that a mesh axis runs over, the one named last changes fastest.
Arguments:
- states: bfloat16 [2, 8192, 768], P(None, ('rep', 'shard')), may hold values from -6 to 6
- cotangent: bfloat16 [2, 8192, 768], P(None, ('rep', 'shard')), may hold values from -6 to 6
- norm1_gain: bfloat16 [768], P('shard'), may hold values from 0.099609375 to 1.8984375
- norm1_bias: bfloat16 [768], P('shard'), may hold values from -3 to 3
- qkv_weight: bfloat16 [768, 2304], P('shard'), may hold values from -0.3125 to 0.3125
- qkv_bias: bfloat16 [2304], P('shard'), may hold values from -3 to 3
- out_weight: bfloat16 [768, 768], P('shard'), may hold values from -0.875 to 0.875
- out_bias: bfloat16 [768], P('shard'), may hold values from -3 to 3
- norm2_gain: bfloat16 [768], P('shard'), may hold values from 0.099609375 to 1.8984375
- norm2_bias: bfloat16 [768], P('shard'), may hold values from -3 to 3
- up_weight: bfloat16 [768, 3072], P('shard'), may hold values from -0.21875 to 0.21875
- up_bias: bfloat16 [3072], P('shard'), may hold values from -3 to 3
- down_weight: bfloat16 [3072, 768], P('shard'), may hold values from -0.109375 to 0.109375
- down_bias: bfloat16 [768], P('shard'), may hold values from -3 to 3
- slot_of_device: int32 [8, 4], P('rep'), may hold values from 0 to 3, as said below
- parent_segment: int32 [8, 4], P('rep'), may hold values from 0 to 1, as said below
Outputs:
- output: bfloat16 [2, 8192, 768], P(None, ('rep', 'shard'))
- states_grad: bfloat16 [2, 8192, 768], P(None, ('rep', 'shard'))
- norm1_gain_grad: float32 [768], P('shard')
- norm1_bias_grad: float32 [768], P('shard')
- qkv_weight_grad: float32 [768, 2304], P('shard')
- qkv_bias_grad: float32 [2304], P('shard')
- out_weight_grad: float32 [768, 768], P('shard')
- out_bias_grad: float32 [768], P('shard')
- norm2_gain_grad: float32 [768], P('shard')
- norm2_bias_grad: float32 [768], P('shard')
- up_weight_grad: float32 [768, 3072], P('shard')
- up_bias_grad: float32 [3072], P('shard')
- down_weight_grad: float32 [3072, 768], P('shard')
- down_bias_grad: float32 [768], P('shard')
The draws below stay inside these ranges and needn't reach their ends.
Inputs may be any that keep to these rules, and one draw needn't show every extreme that they name: `slot_of_device`: each row is an ordering of 0 to 3: entry j is the piece held by device j of the tree's group; pieces below 1 are the trunk's runs in order, piece 1 + b is branch b + 1, piece 2 + l is leaf 1 + 1 + l. `parent_segment`: segment 0 is the trunk and its own parent, segments 1 to 1 are branches with parent 0, segments 1 + 1 to 3 are leaves whose parent is the trunk (0) or one of the branches.
All inputs are finite; a program needn't handle non-finite values.
Results may differ from the reference program's by a relative error of at most 0.022.
Values may be sent and summed in bfloat16 or wider, within the bound.
No kernel may reach another device: no remote copies, remote signals or barrier semaphores. Data moves between devices by JAX's collectives and lax.ppermute only.
A program may use at most 192 MiB of HBM per device.

```python
import math
import jax
import jax.numpy as jnp
from jax import lax

D = 768
HEADS = 12
FF = 3072
POS_DEV = 256
BLOCK = 16
POSITIONS = 8192
N_REP = 8
N_SHARD = 4


def draw_slot_of_device(key, part):
    keys = jax.random.split(jax.random.fold_in(key, 11), N_REP)
    return jax.vmap(lambda single: jax.random.permutation(single, N_SHARD))(keys).astype(jnp.int32)


def draw_parent_segment(key, part):
    n_branch = N_SHARD // 4
    keys = jax.random.split(jax.random.fold_in(key, 23), N_REP)

    def one_tree(single):
        leaves = jax.random.randint(single, (2 * n_branch,), 0, n_branch + 1).astype(jnp.int32)
        return jnp.concatenate([jnp.zeros((n_branch + 1,), jnp.int32), leaves])
    return jax.vmap(one_tree)(keys).astype(jnp.int32)


def level_of(key, shape, cuts, low, largest):
    def one(dim, shards_of):
        steps = jax.random.uniform(jax.random.fold_in(jax.random.fold_in(key, 6), dim), (shards_of,), jnp.float32, low / len(cuts), largest / len(cuts))
        return jnp.repeat(jnp.exp(steps), shape[dim] // shards_of).reshape((-1,) + (1,) * (len(shape) - dim - 1))

    factor_of = one(*cuts[0])
    for cut in cuts[1:]:
        factor_of = factor_of * one(*cut)
    return factor_of


def bell_draw(rng, dims, scale, most, shards=(), held_as=jnp.bfloat16):
    drawn = scale * jax.random.normal(rng, dims, jnp.float32)
    if shards:
        drawn = drawn * level_of(rng, dims, shards, -0.22, 0.18)
    return jnp.clip(drawn, -most, most).astype(held_as)


def setup_inputs(seed: int = 0) -> dict:
    splits = jax.random.split(jax.random.key(seed), 17)
    return {
        "states": bell_draw(splits[0], (2, POSITIONS, D), 1.0, 6.0, ((1, 32),)),
        "cotangent": bell_draw(splits[1], (2, POSITIONS, D), 1.0, 6.0, ((1, 32),)),
        "norm1_gain": jnp.clip(1.0 + 0.18 * jax.random.normal(splits[2], (D,), jnp.float32), 0.099609375, 1.8984375).astype(jnp.bfloat16),
        "norm1_bias": bell_draw(splits[3], (D,), 0.5, 3.0, ((0, 4),)),
        "qkv_weight": bell_draw(splits[4], (D, 3 * D), (D // 2) ** -0.5, 0.3125, ((0, 4),)),
        "qkv_bias": bell_draw(splits[5], (3 * D,), 0.5, 3.0, ((0, 4),)),
        "out_weight": bell_draw(splits[6], (D, D), (D // 16) ** -0.5, 0.875, ((0, 4),)),
        "out_bias": bell_draw(splits[7], (D,), 0.5, 3.0, ((0, 4),)),
        "norm2_gain": jnp.clip(1.0 + 0.18 * jax.random.normal(splits[8], (D,), jnp.float32), 0.099609375, 1.8984375).astype(jnp.bfloat16),
        "norm2_bias": bell_draw(splits[9], (D,), 0.5, 3.0, ((0, 4),)),
        "up_weight": bell_draw(splits[10], (D, FF), D ** -0.5, 0.21875, ((0, 4),)),
        "up_bias": bell_draw(splits[11], (FF,), 0.5, 3.0, ((0, 4),)),
        "down_weight": bell_draw(splits[12], (FF, D), FF ** -0.5, 0.109375, ((0, 4),)),
        "down_bias": bell_draw(splits[13], (D,), 0.5, 3.0, ((0, 4),)),
        "slot_of_device": draw_slot_of_device(jax.random.fold_in(splits[16], 71), 0),
        "parent_segment": draw_parent_segment(jax.random.fold_in(splits[16], 71), 0),
    }


NEG = -1e+30
HIGH = lax.Precision.HIGHEST

@jax.custom_vjp
def low(v):
    return lax.optimization_barrier(v.astype(jnp.bfloat16)).astype(jnp.float32)

@jax.custom_vjp
def low_back(v):
    return v

def low_keep(v):
    return (low(v), None)

def low_pass(kept, grad):
    return (grad,)

def back_keep(v):
    return (v, None)

def back_low(kept, grad):
    return (low(grad),)
low.defvjp(low_keep, low_pass)
low_back.defvjp(back_keep, back_low)

def layer_norm(values, gain, shift):
    center = lax.optimization_barrier(jnp.mean(values, axis=-1, keepdims=True))
    spread = values - center
    variance = lax.optimization_barrier(jnp.mean(spread * spread, axis=-1, keepdims=True))
    return spread * lax.rsqrt(variance + 1e-05) * gain + shift

def gelu_tanh(values):
    return 0.5 * values * (1.0 + jnp.tanh(0.7978845608028654 * (values + 0.044715 * values * values * values)))

def rotate(field, angles):
    half = field.shape[-1] // 2
    cosine = jnp.cos(angles)[:, None, :]
    sine = jnp.sin(angles)[:, None, :]
    first = field[..., :half]
    second = field[..., half:]
    return jnp.concatenate([first * cosine - second * sine, second * cosine + first * sine], axis=-1)

def piece_meta(pieces, n_branch, pos_dev):
    segment = jnp.where(pieces < n_branch, 0, pieces - n_branch + 1).astype(jnp.int32)
    start = jnp.where(pieces < n_branch, pieces * pos_dev, jnp.where(pieces < 2 * n_branch, n_branch * pos_dev, (n_branch + 1) * pos_dev)).astype(jnp.int32)
    return (segment, start)

def lookup(table, index):
    hits = index[..., None] == jnp.arange(table.shape[0], dtype=jnp.int32)
    return lax.optimization_barrier(jnp.sum(jnp.where(hits, table, 0), axis=-1)).astype(jnp.int32)

def allowed_pairs(q_pos, q_copy, q_seg, q_parent, q_grand, k_pos, k_copy, k_seg):
    on_path = (k_seg[None, :] == q_seg[:, None]) | (k_seg[None, :] == q_parent[:, None]) | (k_seg[None, :] == q_grand[:, None])
    q_block = q_pos // BLOCK
    k_block = k_pos // BLOCK
    noisy_ok = (q_copy[:, None] == 0) & (k_copy[None, :] == 0) & (k_block[None, :] == q_block[:, None])
    clean_ok = (k_copy[None, :] == 1) & (k_block[None, :] < q_block[:, None] + q_copy[:, None])
    return on_path & (noisy_ok | clean_ok)

def tree_layer(states, params, slots, parents):
    gain_one, shift_one, w_qkv, b_qkv, w_out, b_out, gain_two, shift_two, w_up, b_up, w_down, b_down = params
    group = states.shape[1]
    rows = 2 * group
    head_dim = D // HEADS
    half = head_dim // 2
    seg_dev, start_dev = piece_meta(slots, N_SHARD // 4, POS_DEV)
    offset = jnp.arange(POS_DEV, dtype=jnp.int32)
    pos_one = (start_dev[:, None] + offset[None, :]).reshape(group)
    seg_one = jnp.broadcast_to(seg_dev[:, None], (N_SHARD, POS_DEV)).reshape(group)
    row_pos = jnp.concatenate([pos_one, pos_one])
    row_seg = jnp.concatenate([seg_one, seg_one])
    row_copy = jnp.concatenate([jnp.zeros((group,), jnp.int32), jnp.ones((group,), jnp.int32)])
    row_parent = lookup(parents, row_seg)
    row_grand = lookup(parents, row_parent)
    inputs = states.reshape(rows, D)
    norm_one = low(layer_norm(inputs, gain_one, shift_one))
    qkv = low_back(jnp.dot(norm_one, w_qkv, precision=HIGH) + b_qkv)
    freq = jnp.exp(-jnp.log(10000.0) * jnp.arange(half, dtype=jnp.float32) / half)
    angles = row_pos.astype(jnp.float32)[:, None] * freq[None, :]
    query = low(rotate(qkv[:, :D].reshape(rows, HEADS, head_dim), angles))
    keys = low(rotate(qkv[:, D:2 * D].reshape(rows, HEADS, head_dim), angles))
    values = low(qkv[:, 2 * D:].reshape(rows, HEADS, head_dim))
    scale = 1.0 / math.sqrt(head_dim)

    def attend(block):
        q_blk, q_pos, q_copy, q_seg, q_parent, q_grand = block
        scores = low_back(jnp.einsum('qhd,khd->hqk', q_blk, keys, precision=HIGH) * scale)
        allowed = allowed_pairs(q_pos, q_copy, q_seg, q_parent, q_grand, row_pos, row_copy, row_seg)
        scores = jnp.where(allowed[None], scores, NEG)
        peak = lax.optimization_barrier(jnp.max(scores, axis=-1, keepdims=True))
        expo = jnp.exp(scores - peak)
        weights = expo / lax.optimization_barrier(jnp.sum(expo, axis=-1, keepdims=True))
        return jnp.einsum('hqk,khd->qhd', low(weights), values, precision=HIGH)
    nblk = rows // POS_DEV
    blocks = (query.reshape(nblk, POS_DEV, HEADS, head_dim), row_pos.reshape(nblk, POS_DEV), row_copy.reshape(nblk, POS_DEV), row_seg.reshape(nblk, POS_DEV), row_parent.reshape(nblk, POS_DEV), row_grand.reshape(nblk, POS_DEV))
    attended = lax.map(jax.checkpoint(attend), blocks).reshape(rows, D)
    attended = low(low_back(attended))
    middle = inputs + low_back(jnp.dot(attended, w_out, precision=HIGH) + b_out)
    norm_two = low(layer_norm(middle, gain_two, shift_two))
    upward = low_back(jnp.dot(norm_two, w_up, precision=HIGH) + b_up)
    hidden = low(gelu_tanh(upward))
    result = middle + low_back(jnp.dot(hidden, w_down, precision=HIGH) + b_down)
    return result.reshape(2, group, D)

def reference(states, cotangent, norm1_gain, norm1_bias, qkv_weight, qkv_bias, out_weight, out_bias, norm2_gain, norm2_bias, up_weight, up_bias, down_weight, down_bias, slot_of_device, parent_segment):
    params = tuple((item.astype(jnp.float32) for item in (norm1_gain, norm1_bias, qkv_weight, qkv_bias, out_weight, out_bias, norm2_gain, norm2_bias, up_weight, up_bias, down_weight, down_bias)))
    group = N_SHARD * POS_DEV
    x_all = states.astype(jnp.float32).reshape(2, N_REP, group, D).transpose(1, 0, 2, 3)
    ct_all = cotangent.astype(jnp.float32).reshape(2, N_REP, group, D).transpose(1, 0, 2, 3)

    def per_tree(carry, item):
        x_tree, ct_tree, slots, parents = item
        result, pull = jax.vjp(lambda field, weights: tree_layer(field, weights, slots, parents), x_tree, params)
        d_field, d_params = pull(ct_tree)
        carry = jax.tree.map(lambda left, right: left + right, carry, d_params)
        return (carry, (result, d_field))
    zeros = tuple((jnp.zeros_like(item) for item in params))
    grads, (results, d_fields) = lax.scan(per_tree, zeros, (x_all, ct_all, slot_of_device, parent_segment))
    output = results.transpose(1, 0, 2, 3).reshape(2, N_REP * group, D).astype(jnp.bfloat16)
    states_grad = d_fields.transpose(1, 0, 2, 3).reshape(2, N_REP * group, D).astype(jnp.bfloat16)
    return (output, states_grad, grads[0], grads[1], grads[2], grads[3], grads[4], grads[5], grads[6], grads[7], grads[8], grads[9], grads[10], grads[11])
```

```python
import functools
import math

import jax
import jax.numpy as jnp
from jax import lax
from jax.experimental import pallas as pl
from jax.experimental.pallas import tpu as pltpu
from jax.sharding import PartitionSpec as P

HEADS = 12
BLOCK = 16
NEG = -1e30
PAIR = 128
F32 = jnp.float32
BF16 = jnp.bfloat16
ANY = pl.BlockSpec(memory_space=pl.ANY)


def params():
    return pltpu.CompilerParams(vmem_limit_bytes=58 * 2**20)


def whole(shape):
    return pl.BlockSpec(shape, lambda *_: (0,) * len(shape))


def place(rel):
    return jnp.where(rel == 3, 0, jnp.where(rel == 0, 3, rel))


ORDER = (3, 1, 2, 0)


def dot(a, b):
    return lax.dot_general(a, b, (((1,), (0,)), ((), ())), preferred_element_type=F32)


def dot_t(a, b):
    return lax.dot_general(a, b, (((1,), (1,)), ((), ())), preferred_element_type=F32)


def t_dot(a, b):
    return lax.dot_general(a, b, (((0,), (0,)), ((), ())), preferred_element_type=F32)


def normed(x):
    spread = x - jnp.mean(x, axis=-1, keepdims=True)
    inv = lax.rsqrt(jnp.mean(spread * spread, axis=-1, keepdims=True) + 1e-05)
    return spread * inv, inv


def norm_back(d, n, inv, gain):
    e = d * gain
    return inv * (
        e - jnp.mean(e, axis=-1, keepdims=True) - n * jnp.mean(e * n, axis=-1, keepdims=True)
    )


def lanes(shape):
    return lax.broadcasted_iota(jnp.int32, shape, len(shape) - 1)


def swap_halves(t):
    return jnp.where((lanes(t.shape) & 63) < 32, pltpu.roll(t, 96, 1), pltpu.roll(t, 32, 1))


def chosen_pieces(meta, n_shard, n_branch, pos_dev):
    me = meta[0]
    mine = meta[2 + me]
    seg = jnp.where(mine < n_branch, 0, mine - n_branch + 1)
    parent = meta[2 + n_shard + seg]

    def holder(piece):
        found = me
        for j in range(n_shard):
            found = jnp.where(meta[2 + j] == piece, j, found)
        return found

    out = []
    for run in range(n_branch):
        valid = jnp.where(seg > 0, 1, jnp.where(mine > run, 1, 0))
        out.append((holder(run), valid, run * pos_dev))
    has = jnp.where(parent > 0, 1, 0)
    out.append((holder(jnp.where(parent > 0, n_branch + parent - 1, -1)), has, n_branch * pos_dev))
    start = jnp.where(
        mine < n_branch,
        mine * pos_dev,
        jnp.where(mine < 2 * n_branch, n_branch * pos_dev, (n_branch + 1) * pos_dev),
    )
    return out, start


def table_kernel(meta, freq_ref, out_ref, *, n_shard, n_branch, pos_dev):
    out, start = chosen_pieces(meta, n_shard, n_branch, pos_dev)
    starts = [start] + [item[2] for item in out]
    shape = (pos_dev, PAIR)
    sign = jnp.where((lanes(shape) & 63) < 32, -1.0, 1.0)
    for i, first in enumerate(starts):
        pos = (lax.broadcasted_iota(jnp.int32, shape, 0) + first).astype(F32)
        angle = pos * freq_ref[...]
        out_ref[i * pos_dev : (i + 1) * pos_dev, :PAIR] = jnp.cos(angle)
        out_ref[i * pos_dev : (i + 1) * pos_dev, PAIR:] = jnp.sin(angle) * sign


def qkv_kernel(meta, x_ref, *refs, n_shard, n_branch, pos_dev, n_far):
    far_refs, refs = refs[:n_far], refs[n_far:]
    w_refs, refs = refs[:4], refs[4:]
    gain, shift, bias, tab, n1t_ref, q_ref, k_ref, v_ref, xr_ref, w, far, w_sem, far_sem = refs
    i = pl.program_id(0)
    rel = meta[1]
    width = x_ref.shape[-1]
    quarter = width // 4
    chosen, _ = chosen_pieces(meta, n_shard, n_branch, pos_dev)

    def w_copy(k):
        rows = pl.ds(pl.multiple_of((k ^ rel) * quarter, quarter), quarter)
        return pltpu.make_async_copy(w_refs[k], w.at[rows], w_sem.at[k])

    def far_copy(t, ref):
        return pltpu.make_async_copy(ref, far.at[t], far_sem.at[t])

    @pl.when(i == 0)
    def _():
        for k in range(4):
            w_copy(k).start()
        for t, (holder, _, _) in enumerate(chosen):
            if n_far == 1:
                far_copy(t, far_refs[0].at[holder]).start()
            else:
                for k in range(n_far):

                    @pl.when(holder ^ rel == k)
                    def _(t=t, k=k):
                        far_copy(t, far_refs[k]).start()
        for k in range(4):
            w_copy(k).wait()

    for t in range(len(chosen)):

        @pl.when(i == 2 + t)
        def _(t=t):
            far_copy(t, far_refs[0] if n_far > 1 else far_refs[0].at[0]).wait()

    def tile(x, queries):
        n, _ = normed(x.astype(F32))
        n1 = (n * gain[...].astype(F32) + shift[...].astype(F32)).astype(BF16)
        turned = n1.T
        for j in range(4):
            rows = pl.ds(pl.multiple_of(place(j ^ rel) * quarter, quarter), quarter)
            n1t_ref[rows, :] = turned[j * quarter : (j + 1) * quarter, :]
        cosine, sine = tab[:, :PAIR], tab[:, PAIR:]

        def turn(first, ref, scale):
            y = dot(n1, w[:, first : first + width]) + bias[:, first : first + width].astype(F32)
            for h in range(width // PAIR):
                part = y[:, h * PAIR : (h + 1) * PAIR]
                out = part * cosine + swap_halves(part) * sine
                ref[:, h * PAIR : (h + 1) * PAIR] = (out * scale).astype(BF16)

        if queries:
            turn(0, q_ref, 1.0 / math.sqrt(width // HEADS))
        turn(width, k_ref, 1.0)
        v_ref[...] = (dot(n1, w[:, 2 * width :]) + bias[:, 2 * width :].astype(F32)).astype(BF16)

    @pl.when(i < 2)
    def _():
        tile(x_ref[0], True)

    @pl.when(i >= 2)
    def _():
        x = far[jnp.maximum(i - 2, 0)]
        xr_ref[...] = x
        tile(x, False)


def attend_kernel(meta, q_ref, k_ref, v_ref, e_ref, o_ref, linv_ref, k_aug, q_aug, *, n_shard, n_branch, pos_dev):
    rows, keys = q_ref.shape[0], k_ref.shape[0]
    blocks = pos_dev // BLOCK

    @pl.when(pl.program_id(0) == 0)
    def _():
        chosen, _ = chosen_pieces(meta, n_shard, n_branch, pos_dev)
        shape = (pos_dev, PAIR)
        lane = lanes(shape) & 63
        block = lax.broadcasted_iota(jnp.int32, shape, 0) // BLOCK
        k_aug[:pos_dev] = jnp.where(lane - 32 == block, 1.0, 0.0).astype(BF16)
        k_aug[pos_dev : 2 * pos_dev] = jnp.where(lane == block, 1.0, 0.0).astype(BF16)
        for t, (_, valid, _) in enumerate(chosen):
            first = (2 + t) * pos_dev
            shut = jnp.where(valid > 0, 0.0, NEG)
            k_aug[first : first + pos_dev] = jnp.where(lane == 16, shut, 0.0).astype(BF16)
        for copy in range(2):
            clean = jnp.where((lane < blocks) & (lane >= block + copy), NEG, 0.0)
            noisy = (lane >= 32) & (lane < 32 + blocks)
            if copy == 0:
                noisy = noisy & (lane - 32 != block)
            out = jnp.where(noisy, NEG, clean)
            out = jnp.where(lane == 16, 1.0, out)
            q_aug[copy * pos_dev : (copy + 1) * pos_dev] = out.astype(BF16)

    low_q = lanes((rows, PAIR)) < 64
    low_k = lanes((keys, PAIR)) < 64
    q, k, v = q_ref[...], k_ref[...], v_ref[...]
    outs = []
    for h in range(2):
        here_q = low_q if h == 0 else ~low_q
        here_k = low_k if h == 0 else ~low_k
        q_h = jnp.where(here_q, q, q_aug[...])
        k_h = jnp.where(here_k, k, k_aug[...])
        v_h = jnp.where(here_k, v, jnp.ones_like(v))
        scores = dot_t(k_h, q_h)
        e = jnp.exp(scores - jnp.max(scores, axis=0, keepdims=True)).astype(BF16)
        e_ref[h] = e
        outs.append(t_dot(e, v_h))
    total = jnp.where(low_q, pltpu.roll(outs[0], 64, 1), pltpu.roll(outs[1], 64, 1))
    inv = 1.0 / total
    linv_ref[...] = inv
    o_ref[...] = (jnp.where(low_q, outs[0], outs[1]) * inv).astype(BF16)


def ff_kernel(meta, *refs, last, tile):
    wo_refs, refs = refs[:4], refs[4:]
    wu_refs, refs = refs[:4], refs[4:]
    wd_refs, refs = refs[:4], refs[4:]
    if not last:
        x_ref, att_ref, g_ref, bo, gain, shift, bup, *refs = refs
        mid_ref, n2_ref, n2t, acc, dn2, bug_ref, send_ref, two_ref, zero_ref, *refs = refs
        wo, wu, wd, gt, hid_ref, dup_ref, stage, sem, out_sem = refs
    else:
        mid_ref, n2_ref, n2t, acc_in, dn2_in, att_ref, g_ref, gain, bup, bdown, *refs = refs
        out_ref, branch_ref, datt_ref, small_ref, bug_ref, send_ref, two_ref, zero_ref, *refs = refs
        wo, wu, wd, gt, hid_ref, dup_ref, stage, sem, out_sem, acc, dn2, attt = refs
    rel = meta[1]
    rows, width = g_ref.shape
    quarter = width // 4
    half_ff = wu.shape[1]
    cols = half_ff // 4
    step_cols = 2 * cols

    def wo_copy(k):
        at = pl.ds(pl.multiple_of((k ^ rel) * quarter, quarter), quarter)
        return pltpu.make_async_copy(wo_refs[k], wo.at[at], sem.at[0, k])

    def wu_copy(k, p):
        at = pl.ds(pl.multiple_of((k ^ rel) * quarter, quarter), quarter)
        source = pl.ds(pl.multiple_of((ORDER[p] ^ rel) * cols, cols), cols)
        return pltpu.make_async_copy(
            wu_refs[k].at[:, source], wu.at[at, p * cols : (p + 1) * cols], sem.at[1 + p, k]
        )

    def wd_copy(p):
        return pltpu.make_async_copy(
            wd_refs[ORDER[p]], wd.at[p * cols : (p + 1) * cols], sem.at[5, p]
        )

    for k in range(4):
        wo_copy(k).start()
    for p in range(4):
        for k in range(4):
            wu_copy(k, p).start()
        wd_copy(p).start()
    if not last:
        for k in range(4):
            wo_copy(k).wait()
        for first in range(0, rows, tile):
            at = slice(first, first + tile)
            mid = x_ref[at].astype(F32) + dot(att_ref[at], wo[...]) + bo[...].astype(F32)
            mid_ref[at] = mid
            n, _ = normed(mid)
            n2_ref[at] = (n * gain[...].astype(F32) + shift[...].astype(F32)).astype(BF16)
        turned = n2_ref[...].T
        for j in range(4):
            at = pl.ds(pl.multiple_of(place(j ^ rel) * quarter, quarter), quarter)
            n2t[at, :] = turned[j * quarter : (j + 1) * quarter, :]
    gt[...] = g_ref[...].T
    if last:
        turned = att_ref[...].T
        for j in range(4):
            at = pl.ds(pl.multiple_of(place(j ^ rel) * quarter, quarter), quarter)
            attt[at, :] = turned[j * quarter : (j + 1) * quarter, :]

    for step in range(2):
        for p in (2 * step, 2 * step + 1):
            for k in range(4):
                wu_copy(k, p).wait()
            wd_copy(p).wait()
        here = slice(step * step_cols, (step + 1) * step_cols)
        w_up, w_down = wu[:, here], wd[here, :]
        bias = jnp.concatenate(
            [bup[pl.ds((ORDER[2 * step + c] ^ rel) * 2 + int(last), 1), :] for c in range(2)], axis=1
        )
        for first in range(0, rows, tile):
            at = slice(first, first + tile)
            up = dot(n2_ref[at], w_up) + bias
            d_hidden = dot_t(g_ref[at], w_down)
            cube = 0.044715 * up * up
            th = jnp.tanh(0.7978845608028654 * (up + cube * up))
            half = 0.5 * (1.0 + th)
            hidden = (up * half).astype(BF16)
            slope = half + (0.5 * 0.7978845608028654) * up * (1.0 - th * th) * (1.0 + 3.0 * cube)
            d_up = (d_hidden * slope).astype(BF16)
            hid_ref[at] = hidden
            dup_ref[at] = d_up
            more, d_more = dot(hidden, w_down), dot_t(d_up, w_up)
            if step == 0 and not last:
                acc[at] = more
                dn2[at] = d_more
            elif step == 0:
                acc[at] = acc_in[at] + more
                dn2[at] = dn2_in[at] + d_more
            else:
                acc[at] = acc[at] + more
                dn2[at] = dn2[at] + d_more
        sums = jnp.sum(dup_ref[...].astype(F32), axis=0, keepdims=True)
        grad_up = dot(n2t[...], dup_ref[...])
        grad_down = dot(gt[...], hid_ref[...])
        for c in range(2):
            p = 2 * step + c
            j = ORDER[p] ^ rel
            bug_ref[pl.ds(j, 1), :] = sums[:, c * cols : (c + 1) * cols]
            there = pl.ds(pl.multiple_of((j & 1) * cols, cols), cols)
            for r in range(4):
                block = slice(r * quarter, (r + 1) * quarter)
                stage[r, j >> 1, :, there] = grad_up[block, c * cols : (c + 1) * cols].astype(BF16)
                stage[p, 2 + r // 2, :, (r % 2) * cols : (r % 2 + 1) * cols] = grad_down[
                    block, c * cols : (c + 1) * cols
                ].astype(BF16)

    if last:
        for k in range(4):
            wo_copy(k).wait()
        sums = [jnp.zeros((1, width), F32) for _ in range(4)]
        for first in range(0, rows, tile):
            at = slice(first, first + tile)
            mid = mid_ref[at]
            out_ref[at] = (mid + acc[at] + bdown[...].astype(F32)).astype(BF16)
            n, inv = normed(mid)
            d = dn2[at]
            g = g_ref[at].astype(F32)
            branch = (g + norm_back(d, n, inv, gain[...].astype(F32))).astype(BF16)
            branch_ref[at] = branch
            datt_ref[at] = dot_t(branch, wo[...]).astype(BF16)
            for a, item in enumerate((branch.astype(F32), d * n, d, g)):
                sums[a] = sums[a] + jnp.sum(item, axis=0, keepdims=True)
        for a in range(4):
            small_ref[a : a + 1, :] = sums[a]
        grad_out = dot(attt[...], branch_ref[...])
        for r in range(4):
            stage[r, 4] = grad_out[r * quarter : (r + 1) * quarter].astype(BF16)
    else:
        for k in range(4):
            pass
    copies = [
        pltpu.make_async_copy(stage.at[0:2], send_ref, out_sem.at[0]),
        pltpu.make_async_copy(stage.at[2], two_ref, out_sem.at[1]),
        pltpu.make_async_copy(stage.at[3], zero_ref, out_sem.at[2]),
    ]
    for copy in copies:
        copy.start()
    for copy in copies:
        copy.wait()


def attend_back_kernel(
    q_ref, k_ref, v_ref, do_ref, o_ref, linv_ref, e_ref, n1t, tab,
    dq_ref, dk_ref, dv_ref, send_ref, two_ref, zero_ref, bias_ref, *, pos_dev,
):
    rows, keys = q_ref.shape[0], k_ref.shape[0]
    quarter = n1t.shape[0] // 4
    n_pair = q_ref.shape[1] // PAIR
    scale = 1.0 / 8.0
    lane_q, lane_k = lanes((rows, PAIR)), lanes((keys, PAIR))

    def unturn(t, first):
        parts = []
        for i in range(t.shape[0] // pos_dev):
            at = first[i] * pos_dev
            cosine, sine = tab[at : at + pos_dev, :PAIR], tab[at : at + pos_dev, PAIR:]
            part = t[i * pos_dev : (i + 1) * pos_dev]
            parts.append(part * cosine - swap_halves(part) * sine)
        return jnp.concatenate(parts, axis=0)

    for pair in range(n_pair):
        at = slice(pair * PAIR, (pair + 1) * PAIR)
        q, k, v = q_ref[:, at], k_ref[:, at], v_ref[:, at]
        do = do_ref[:, at].astype(F32) * linv_ref[:, at]
        product = do * o_ref[:, at].astype(F32)
        do_b = do.astype(BF16)
        d_q, d_k, d_v = [], [], []
        for h in range(2):
            here_q = (lane_q < 64) if h == 0 else (lane_q >= 64)
            here_k = (lane_k < 64) if h == 0 else (lane_k >= 64)
            free = 64 * (1 - h)
            delta = -jnp.sum(jnp.where(here_q, product, 0.0), axis=1, keepdims=True)
            high = delta.astype(BF16).astype(F32)
            low = delta - high
            extra = jnp.where(lane_q == free, high, jnp.where(lane_q == free + 1, low, 0.0))
            do_h = jnp.where(here_q, do, extra).astype(BF16)
            ones = jnp.where((lane_k == free) | (lane_k == free + 1), 1.0, 0.0).astype(BF16)
            v_h = jnp.where(here_k, v, ones)
            e = e_ref[2 * pair + h]
            d_scores = (dot_t(v_h, do_h) * e.astype(F32)).astype(BF16)
            d_v.append(dot(e, do_b))
            d_k.append(dot(d_scores, q))
            d_q.append(t_dot(d_scores, k))
        dv = jnp.where(lane_k < 64, d_v[0], d_v[1])
        dk = unturn(jnp.where(lane_k < 64, d_k[0], d_k[1]), [0, 0] + list(range(1, keys // pos_dev - 1)))
        dq = unturn(jnp.where(lane_q < 64, d_q[0], d_q[1]) * scale, [0, 0])
        dv_ref[:, at] = dv.astype(BF16)
        dk_ref[:, at] = dk.astype(BF16)
        dq_ref[:, at] = dq.astype(BF16)
    for a, (ref, count) in enumerate(((dq_ref, rows), (dk_ref, keys), (dv_ref, keys))):
        d = ref[...]
        bias_ref[a : a + 1, :] = jnp.sum(d.astype(F32), axis=0, keepdims=True)
        grad = dot(n1t[:, :count], d).astype(BF16)
        send_ref[0, a] = grad[:quarter]
        send_ref[1, a] = grad[quarter : 2 * quarter]
        two_ref[a] = grad[2 * quarter : 3 * quarter]
        zero_ref[a] = grad[3 * quarter :]


def input_back_kernel(meta, x_ref, xr_ref, dq, dk, dv, *refs, n_shard, n_branch, pos_dev, relative):
    w_refs, refs = refs[:4], refs[4:]
    if relative:
        gain, dn1_ref, small_ref, send_ref, two_ref, w, far, w_sem = refs
    else:
        gain, dn1_ref, small_ref, far_ref, w, far, w_sem = refs
    i = pl.program_id(0)
    rel = meta[1]
    width = x_ref.shape[-1]
    quarter = width // 4
    chosen, _ = chosen_pieces(meta, n_shard, n_branch, pos_dev)
    n_far = len(chosen)

    def w_copy(k):
        rows = pl.ds(pl.multiple_of((k ^ rel) * quarter, quarter), quarter)
        return pltpu.make_async_copy(w_refs[k], w.at[rows], w_sem.at[k])

    @pl.when(i == 0)
    def _():
        for k in range(4):
            w_copy(k).start()
        far[...] = jnp.zeros_like(far)
        small_ref[...] = jnp.zeros_like(small_ref)
        for k in range(4):
            w_copy(k).wait()

    def sums(d, x):
        n, _ = normed(x.astype(F32))
        small_ref[0:1, :] = small_ref[0:1, :] + jnp.sum(d * n, axis=0, keepdims=True)
        small_ref[1:2, :] = small_ref[1:2, :] + jnp.sum(d, axis=0, keepdims=True)

    keys = dot_t(dk[...], w[:, width : 2 * width]) + dot_t(dv[...], w[:, 2 * width :])

    @pl.when(i < 2)
    def _():
        d = keys + dot_t(dq[...], w[:, :width])
        dn1_ref[...] = d
        sums(d, x_ref[0])

    for t, (holder, _, _) in enumerate(chosen):

        @pl.when(i == 2 + t)
        def _(holder=holder):
            spot = place(holder ^ rel) if relative else holder
            far[spot] = far[spot] + keys
            sums(keys, xr_ref[...])

    @pl.when(i == 1 + n_far)
    def _():
        if relative:
            send_ref[...] = far[0:2].astype(BF16)
            two_ref[...] = far[2].astype(BF16)
        else:
            far_ref[...] = far[...].astype(BF16)


def final_kernel(x_ref, branch_ref, dn1_ref, got_ref, gain, out_ref):
    i = pl.program_id(0)
    d = dn1_ref[...] + jnp.where(i == 1, 1.0, 0.0) * got_ref[...].astype(F32)
    n, inv = normed(x_ref[0].astype(F32))
    back = norm_back(d, n, inv, gain[...].astype(F32))
    out_ref[0] = (branch_ref[...].astype(F32) + back).astype(BF16)


def swap(x, axis, bit):
    n = lax.axis_size(axis)
    return lax.ppermute(x, axis, [(i, i ^ bit) for i in range(n)])


def pieces_of(x):
    two = swap(x, "shard", 2)
    one = swap(x, "shard", 1)
    return [x, one, two, swap(two, "shard", 1)]


def select_bit(bit, a, b):
    return jnp.where(bit == 1, b, a)


def gather_small(x):
    n_shard = lax.axis_size("shard")
    if n_shard != 4:
        return lax.all_gather(x, "shard", axis=0)
    s = lax.axis_index("shard")
    a, b, c, d = pieces_of(x)
    odd, high = s & 1, s >> 1
    a, b = select_bit(odd, a, b), select_bit(odd, b, a)
    c, d = select_bit(odd, c, d), select_bit(odd, d, c)
    return jnp.stack(
        [select_bit(high, a, c), select_bit(high, b, d), select_bit(high, c, a), select_bit(high, d, b)]
    )


def halves(x, bit):
    size = x.shape[1] // 2
    keep = lax.dynamic_slice_in_dim(x, bit * size, size, 1)
    give = lax.dynamic_slice_in_dim(x, (1 - bit) * size, size, 1)
    return keep, give


def join(mine, other, bit):
    return jnp.concatenate([select_bit(bit, mine, other), select_bit(bit, other, mine)], axis=1)


def sum_over_rep(x):
    if lax.axis_size("rep") != 8:
        return lax.psum(x, "rep")
    r = lax.axis_index("rep")
    y, z = r & 1, (r >> 1) & 1
    keep, give = halves(x, y)
    part = keep + swap(give, "rep", 1)
    keep, give = halves(part, z)
    part = keep + swap(give, "rep", 2)
    part = part + swap(part, "rep", 4)
    part = join(part, swap(part, "rep", 2), z)
    return join(part, swap(part, "rep", 1), y)


def reduce_gradient(send, two, zero):
    got = swap(send, "shard", 1)
    across = swap(two + got[0], "shard", 2)
    return sum_over_rep(zero + got[1] + across)


def sum_small(x):
    if lax.axis_size("rep") != 8 or lax.axis_size("shard") != 4:
        return lax.psum(x, ("rep", "shard"))
    for axis, bit in (("shard", 1), ("shard", 2), ("rep", 1), ("rep", 2), ("rep", 4)):
        x = x + swap(x, axis, bit)
    return x


def shards(
    states,
    cotangent,
    norm1_gain,
    norm1_bias,
    qkv_weight,
    qkv_bias,
    out_weight,
    out_bias,
    norm2_gain,
    norm2_bias,
    up_weight,
    up_bias,
    down_weight,
    down_bias,
    slot_of_device,
    parent_segment,
):
    n_shard = lax.axis_size("shard")
    n_branch = n_shard // 4
    pos_dev, width = states.shape[1], states.shape[2]
    ff = up_weight.shape[1]
    rows = 2 * pos_dev
    n_far = n_branch + 1
    keys = rows + n_far * pos_dev
    relative = n_shard == 4
    quarter = width // 4
    cols = ff // 8
    me = lax.axis_index("shard")
    rel = me if relative else jnp.zeros((), jnp.int32)
    meta = jnp.concatenate([jnp.stack([me, rel]), slot_of_device[0], parent_segment[0]])
    sizes = dict(n_shard=n_shard, n_branch=n_branch, pos_dev=pos_dev)
    bound = lambda kernel, **more: functools.partial(kernel, **more)
    shape = jax.ShapeDtypeStruct

    vectors = jnp.concatenate(
        [norm1_gain, norm1_bias, qkv_bias, out_bias, norm2_gain, norm2_bias, up_bias, down_bias]
    )
    if relative:
        w_qkv = pieces_of(qkv_weight)
        x_far = pieces_of(states[1])
        w_out = pieces_of(out_weight)
        up_halves = up_weight.reshape(quarter, 4, 2, cols)
        w_up = [pieces_of(up_halves[:, :, h].reshape(quarter, 4 * cols)) for h in range(2)]
        w_down = [pieces_of(down_weight[h * cols : (h + 1) * cols]) for h in range(2)]
    else:
        gather = lambda item: lax.all_gather(item, "shard", axis=0, tiled=True)
        rows_of = lambda item: [item[j * quarter : (j + 1) * quarter] for j in range(4)]
        w_qkv = rows_of(gather(qkv_weight))
        x_far = [gather(states[1][None])]
        w_out = rows_of(gather(out_weight))
        up_halves = gather(up_weight).reshape(width, 4, 2, cols)
        w_up = [rows_of(up_halves[:, :, h].reshape(width, 4 * cols)) for h in range(2)]
        down_halves = gather(down_weight).reshape(4, 2, cols, width)
        w_down = [[down_halves[j, h] for j in range(4)] for h in range(2)]
    small = gather_small(vectors)
    marks, at = [], 0
    for item in (norm1_gain, norm1_bias, qkv_bias, out_bias, norm2_gain, norm2_bias, up_bias, down_bias):
        marks.append((at, item.shape[0]))
        at += item.shape[0]
    gain1, shift1, b_qkv, b_out, gain2, shift2, b_up, b_down = (
        small[:, first : first + size].reshape(1, n_shard * size) for first, size in marks
    )
    b_up = b_up.reshape(8, cols).astype(F32)

    freq = jnp.exp(-jnp.log(10000.0) * jnp.arange(32, dtype=F32) / 32)
    freq = jnp.tile(freq, 4).reshape(1, PAIR)
    table = pl.pallas_call(
        bound(table_kernel, **sizes),
        out_shape=shape(((1 + n_far) * pos_dev, 2 * PAIR), F32),
        grid_spec=pltpu.PrefetchScalarGridSpec(
            num_scalar_prefetch=1,
            grid=(1,),
            in_specs=[whole((1, PAIR))],
            out_specs=whole(((1 + n_far) * pos_dev, 2 * PAIR)),
        ),
        compiler_params=params(),
        name="rotary_table",
    )(meta, freq)

    own = lambda i, *_: (jnp.minimum(i, 1), 0)
    own3 = lambda i, *_: (jnp.minimum(i, 1), 0, 0)
    each = lambda i, *_: (i, 0)
    beyond = lambda i, *_: (jnp.maximum(i - 2, 0), 0)
    n1t, q, k, v, x_seen = pl.pallas_call(
        bound(qkv_kernel, n_far=len(x_far), **sizes),
        out_shape=[
            shape((width, keys), BF16),
            shape((rows, width), BF16),
            shape((keys, width), BF16),
            shape((keys, width), BF16),
            shape((n_far * pos_dev, width), BF16),
        ],
        grid_spec=pltpu.PrefetchScalarGridSpec(
            num_scalar_prefetch=1,
            grid=(2 + n_far,),
            in_specs=[pl.BlockSpec((1, pos_dev, width), own3)]
            + [ANY] * (len(x_far) + 4)
            + [whole((1, width)), whole((1, width)), whole((1, 3 * width))]
            + [pl.BlockSpec((pos_dev, 2 * PAIR), lambda i, *_: (jnp.maximum(i - 1, 0), 0))],
            out_specs=[
                pl.BlockSpec((width, pos_dev), lambda i, *_: (0, i)),
                pl.BlockSpec((pos_dev, width), own),
                pl.BlockSpec((pos_dev, width), each),
                pl.BlockSpec((pos_dev, width), each),
                pl.BlockSpec((pos_dev, width), beyond),
            ],
            scratch_shapes=[
                pltpu.VMEM((width, 3 * width), BF16),
                pltpu.VMEM((n_far, pos_dev, width), BF16),
                pltpu.SemaphoreType.DMA((4,)),
                pltpu.SemaphoreType.DMA((n_far,)),
            ],
        ),
        compiler_params=params(),
        name="norm_qkv",
    )(meta, states, *x_far, *w_qkv, gain1, shift1, b_qkv, table)

    pair = lambda i, *_: (0, i)
    n_pair = width // PAIR
    e, attended, linv = pl.pallas_call(
        bound(attend_kernel, **sizes),
        out_shape=[
            shape((HEADS, keys, rows), BF16),
            shape((rows, width), BF16),
            shape((rows, width), F32),
        ],
        grid_spec=pltpu.PrefetchScalarGridSpec(
            num_scalar_prefetch=1,
            grid=(n_pair,),
            in_specs=[
                pl.BlockSpec((rows, PAIR), pair),
                pl.BlockSpec((keys, PAIR), pair),
                pl.BlockSpec((keys, PAIR), pair),
            ],
            out_specs=[
                pl.BlockSpec((2, keys, rows), lambda i, *_: (i, 0, 0)),
                pl.BlockSpec((rows, PAIR), pair),
                pl.BlockSpec((rows, PAIR), pair),
            ],
            scratch_shapes=[pltpu.VMEM((keys, PAIR), BF16), pltpu.VMEM((rows, PAIR), BF16)],
        ),
        compiler_params=params(),
        name="attend",
    )(meta, q, k, v)

    x_rows = states.reshape(rows, width)
    g_rows = cotangent.reshape(rows, width)

    def ff_outs(units):
        return [
            shape((4, cols), F32),
            shape((2, units, quarter, width), BF16),
            shape((units, quarter, width), BF16),
            shape((units, quarter, width), BF16),
        ]

    def ff_scratch(units):
        return [
            pltpu.VMEM((width, width), BF16),
            pltpu.VMEM((width, 4 * cols), BF16),
            pltpu.VMEM((4 * cols, width), BF16),
            pltpu.VMEM((width, rows), BF16),
            pltpu.VMEM((rows, 2 * cols), BF16),
            pltpu.VMEM((rows, 2 * cols), BF16),
            pltpu.VMEM((4, units, quarter, width), BF16),
            pltpu.SemaphoreType.DMA((6, 4)),
            pltpu.SemaphoreType.DMA((3,)),
        ]

    smem = pl.BlockSpec(memory_space=pltpu.SMEM)
    full = whole((rows, width))
    vec = whole((1, width))
    blocks = [whole((4, cols)), ANY, ANY, ANY]
    mid, n2, n2t, acc, dn2, bug0, *chunk0 = pl.pallas_call(
        bound(ff_kernel, last=False, tile=pos_dev),
        out_shape=[
            shape((rows, width), F32),
            shape((rows, width), BF16),
            shape((width, rows), BF16),
            shape((rows, width), F32),
            shape((rows, width), F32),
            *ff_outs(4),
        ],
        grid=(1,),
        in_specs=[smem] + [ANY] * 12 + [full, full, full, vec, vec, vec, whole((8, cols))],
        out_specs=[full, full, whole((width, rows)), full, full, *blocks],
        scratch_shapes=ff_scratch(4),
        compiler_params=params(),
        name="feed_first",
    )(meta, *w_out, *w_up[0], *w_down[0], x_rows, attended, g_rows, b_out, gain2, shift2, b_up)

    output, branch, d_att, small2, bug1, *chunk1 = pl.pallas_call(
        bound(ff_kernel, last=True, tile=pos_dev),
        out_shape=[
            shape((rows, width), BF16),
            shape((rows, width), BF16),
            shape((rows, width), BF16),
            shape((8, width), F32),
            *ff_outs(5),
        ],
        grid=(1,),
        in_specs=[smem]
        + [ANY] * 12
        + [full, full, whole((width, rows)), full, full, full, full, vec, whole((8, cols)), vec],
        out_specs=[full, full, full, whole((8, width)), *blocks],
        scratch_shapes=ff_scratch(5)
        + [pltpu.VMEM((rows, width), F32), pltpu.VMEM((rows, width), F32), pltpu.VMEM((width, rows), BF16)],
        compiler_params=params(),
        name="feed_second",
    )(meta, *w_out, *w_up[1], *w_down[1], mid, n2, n2t, acc, dn2, attended, g_rows, gain2, b_up, b_down)

    quad = 2 * PAIR
    dq, dk, dv, send2, two2, zero2, small_qkv = pl.pallas_call(
        bound(attend_back_kernel, pos_dev=pos_dev),
        out_shape=[
            shape((rows, width), BF16),
            shape((keys, width), BF16),
            shape((keys, width), BF16),
            shape((2, 3, quarter, width), BF16),
            shape((3, quarter, width), BF16),
            shape((3, quarter, width), BF16),
            shape((8, width), F32),
        ],
        grid=(width // quad,),
        in_specs=[
            pl.BlockSpec((rows, quad), pair),
            pl.BlockSpec((keys, quad), pair),
            pl.BlockSpec((keys, quad), pair),
            pl.BlockSpec((rows, quad), pair),
            pl.BlockSpec((rows, quad), pair),
            pl.BlockSpec((rows, quad), pair),
            pl.BlockSpec((4, keys, rows), lambda i: (i, 0, 0)),
            whole((width, keys)),
            whole(((1 + n_far) * pos_dev, 2 * PAIR)),
        ],
        out_specs=[
            pl.BlockSpec((rows, quad), pair),
            pl.BlockSpec((keys, quad), pair),
            pl.BlockSpec((keys, quad), pair),
            pl.BlockSpec((2, 3, quarter, quad), lambda i: (0, 0, 0, i)),
            pl.BlockSpec((3, quarter, quad), lambda i: (0, 0, i)),
            pl.BlockSpec((3, quarter, quad), lambda i: (0, 0, i)),
            pl.BlockSpec((8, quad), pair),
        ],
        compiler_params=params(),
        name="attend_back",
    )(q, k, v, d_att, attended, linv, e, n1t, table)

    far_shapes = (
        [shape((2, pos_dev, width), BF16), shape((pos_dev, width), BF16)]
        if relative
        else [shape((n_shard, pos_dev, width), BF16)]
    )
    dn1, small1, *far = pl.pallas_call(
        bound(input_back_kernel, relative=relative, **sizes),
        out_shape=[shape((rows, width), F32), shape((8, width), F32), *far_shapes],
        grid_spec=pltpu.PrefetchScalarGridSpec(
            num_scalar_prefetch=1,
            grid=(2 + n_far,),
            in_specs=[
                pl.BlockSpec((1, pos_dev, width), own3),
                pl.BlockSpec((pos_dev, width), beyond),
                pl.BlockSpec((pos_dev, width), own),
                pl.BlockSpec((pos_dev, width), each),
                pl.BlockSpec((pos_dev, width), each),
            ]
            + [ANY] * 4
            + [vec],
            out_specs=[pl.BlockSpec((pos_dev, width), own), whole((8, width))]
            + [whole(item.shape) for item in far_shapes],
            scratch_shapes=[
                pltpu.VMEM((width, 3 * width), BF16),
                pltpu.VMEM((n_shard, pos_dev, width), F32),
                pltpu.SemaphoreType.DMA((4,)),
            ],
        ),
        compiler_params=params(),
        name="input_back",
    )(meta, states, x_seen, dq, dk, dv, *w_qkv, gain1)

    if relative:
        near = swap(far[0], "shard", 1)
        got = near[1] + swap(far[1] + near[0], "shard", 2)
    else:
        got = lax.psum_scatter(far[0], "shard", scatter_dimension=0)
    states_grad = pl.pallas_call(
        final_kernel,
        out_shape=shape((2, pos_dev, width), BF16),
        grid=(2,),
        in_specs=[
            pl.BlockSpec((1, pos_dev, width), lambda i: (i, 0, 0)),
            pl.BlockSpec((pos_dev, width), each),
            pl.BlockSpec((pos_dev, width), each),
            whole((pos_dev, width)),
            vec,
        ],
        out_specs=pl.BlockSpec((1, pos_dev, width), lambda i: (i, 0, 0)),
        compiler_params=params(),
        name="states_back",
    )(states, branch, dn1, got, gain1)

    def up_of(parts):
        both = jnp.stack([p[:2].reshape(2, -1, 2, cols) for p in parts])
        return both.transpose(2, 1, 3, 0, 4).reshape(-1, ff)

    def down_of(parts):
        both = jnp.stack([p[2:4].reshape(2, quarter, 2, -1) for p in parts])
        return both.transpose(0, 4, 1, 3, 2).reshape(2, -1, width)

    if relative:
        total0 = reduce_gradient(*chunk0)
        total1 = reduce_gradient(*chunk1)
        total2 = reduce_gradient(send2, two2, zero2)
        grad_up = up_of((total0, total1)).astype(F32)
        grad_down = down_of((total0, total1)).reshape(-1, width).astype(F32)
        grad_out = total1[4].astype(F32)
        grad_qkv = total2.transpose(1, 0, 2).reshape(quarter, 3 * width).astype(F32)
    else:
        natural = lambda send, two, zero: [zero, send[1], two, send[0]]
        first, second = natural(*chunk0), natural(*chunk1)
        third = natural(send2, two2, zero2)
        ups = jnp.concatenate([up_of(item) for item in zip(first, second)], axis=0)
        downs = jnp.concatenate([down_of(item).reshape(-1, width) for item in zip(first, second)], axis=0)
        outs = jnp.concatenate([item[4] for item in second], axis=0)
        qkvs = jnp.concatenate(
            [item.transpose(1, 0, 2).reshape(quarter, 3 * width) for item in third], axis=0
        )

        def reduced(item):
            part = lax.psum_scatter(item, "shard", scatter_dimension=0, tiled=True)
            return lax.psum(part, "rep").astype(F32)

        grad_up, grad_down, grad_out, grad_qkv = (reduced(item) for item in (ups, downs, outs, qkvs))

    grad_b_up = jnp.stack([bug0, bug1], axis=1).reshape(ff)
    flat = jnp.concatenate(
        [
            item.reshape(n_shard, -1)
            for item in (
                small1[0], small1[1], small_qkv[:3].reshape(-1), small2[0], small2[1], small2[2], grad_b_up, small2[3],
            )
        ],
        axis=1,
    )
    mine = lax.dynamic_index_in_dim(sum_small(flat), me, 0, keepdims=False)
    g_gain1, g_shift1, g_b_qkv, g_b_out, g_gain2, g_shift2, g_b_up, g_b_down = (
        mine[first : first + size] for first, size in marks
    )
    return (
        output.reshape(2, pos_dev, width),
        states_grad,
        g_gain1,
        g_shift1,
        grad_qkv,
        g_b_qkv,
        grad_out,
        g_b_out,
        g_gain2,
        g_shift2,
        grad_up,
        g_b_up,
        grad_down,
        g_b_down,
    )


def solution(mesh):
    in_specs = (
        P(None, ("rep", "shard"), None),
        P(None, ("rep", "shard"), None),
        P("shard"),
        P("shard"),
        P("shard", None),
        P("shard"),
        P("shard", None),
        P("shard"),
        P("shard"),
        P("shard"),
        P("shard", None),
        P("shard"),
        P("shard", None),
        P("shard"),
        P("rep", None),
        P("rep", None),
    )
    out_specs = (
        P(None, ("rep", "shard"), None),
        P(None, ("rep", "shard"), None),
        P("shard"),
        P("shard"),
        P("shard", None),
        P("shard"),
        P("shard", None),
        P("shard"),
        P("shard"),
        P("shard"),
        P("shard", None),
        P("shard"),
        P("shard", None),
        P("shard"),
    )
    return jax.shard_map(shards, mesh=mesh, in_specs=in_specs, out_specs=out_specs, check_vma=False)
```

```python
import functools
import math

import jax
import jax.numpy as jnp
from jax import lax
from jax.experimental import pallas as pl
from jax.experimental.pallas import tpu as pltpu
from jax.sharding import PartitionSpec as P

HEADS = 12
BLOCK = 16
NEG = -1e30
PAIR = 128
F32 = jnp.float32
BF16 = jnp.bfloat16
ANY = pl.BlockSpec(memory_space=pltpu.HBM)


SMEM = pl.BlockSpec(memory_space=pltpu.SMEM)


def params(mib=58):
    return pltpu.CompilerParams(vmem_limit_bytes=mib * 2**20)


def cost(us):
    return pl.CostEstimate(flops=int(us * 1.15e9), bytes_accessed=0, transcendentals=0)


def whole(shape):
    return pl.BlockSpec(shape, lambda *_: (0,) * len(shape))


def place(rel):
    return jnp.where(rel == 3, 0, jnp.where(rel == 0, 3, rel))


ORDER = (3, 1, 2, 0)


def dot(a, b):
    return lax.dot_general(a, b, (((1,), (0,)), ((), ())), preferred_element_type=F32)


def dot_t(a, b):
    return lax.dot_general(a, b, (((1,), (1,)), ((), ())), preferred_element_type=F32)


def t_dot(a, b):
    return lax.dot_general(a, b, (((0,), (0,)), ((), ())), preferred_element_type=F32)


def normed(x):
    spread = x - jnp.mean(x, axis=-1, keepdims=True)
    inv = lax.rsqrt(jnp.mean(spread * spread, axis=-1, keepdims=True) + 1e-05)
    return spread * inv, inv


def norm_back(d, n, inv, gain):
    e = d * gain
    return inv * (
        e - jnp.mean(e, axis=-1, keepdims=True) - n * jnp.mean(e * n, axis=-1, keepdims=True)
    )


def lanes(shape):
    return lax.broadcasted_iota(jnp.int32, shape, len(shape) - 1)


def swap_halves(t):
    return jnp.where((lanes(t.shape) & 63) < 32, pltpu.roll(t, 96, 1), pltpu.roll(t, 32, 1))

def chosen_pieces(slots, parents, n_shard, n_branch, pos_dev):
    me = lax.axis_index("shard")
    mine = slots[0, me]
    seg = jnp.where(mine < n_branch, 0, mine - n_branch + 1)
    parent = parents[0, seg]

    def holder(piece):
        found = me
        for j in range(n_shard):
            found = jnp.where(slots[0, j] == piece, j, found)
        return found

    out = []
    for run in range(n_branch):
        valid = jnp.where(seg > 0, 1, jnp.where(mine > run, 1, 0))
        out.append((holder(run), valid, run * pos_dev))
    has = jnp.where(parent > 0, 1, 0)
    out.append((holder(jnp.where(parent > 0, n_branch + parent - 1, -1)), has, n_branch * pos_dev))
    start = jnp.where(
        mine < n_branch,
        mine * pos_dev,
        jnp.where(mine < 2 * n_branch, n_branch * pos_dev, (n_branch + 1) * pos_dev),
    )
    return out, start


def relative_to(relative):
    return lax.axis_index("shard") if relative else jnp.zeros((), jnp.int32)


def half_of(how):
    y = lax.axis_index("rep") & 1
    return y if how == "direct" else 1 - y


def row_block(k, rel, quarter, how, chunk=None):
    first = (k ^ rel) * quarter
    if how == "whole":
        return pl.ds(pl.multiple_of(first, 16), quarter)
    first = first + half_of(how) * (quarter // 2)
    if chunk is None:
        return pl.ds(pl.multiple_of(first, 16), quarter // 2)
    return pl.ds(pl.multiple_of(first + chunk * (quarter // 4), 16), quarter // 4)


def pack_kernel(*refs, quarter, width, cols):
    vectors, refs = refs[:8], refs[8:]
    states, w_out, w_up, w_down, s_out, *refs = refs
    b_outs, (small, sem) = refs[:3], refs[3:]
    half = quarter // 2
    y = lax.axis_index("rep") & 1
    at = pl.ds(pl.multiple_of(y * half, half), half)
    pos_dev = states.shape[1]
    copies = [(states.at[1], s_out.at[0:pos_dev])]
    for p in range(3):
        for j in range(4):
            source = w_up.at[at, j * width + p * cols : j * width + (p + 1) * cols]
            copies.append((source, b_outs[p].at[j * half : (j + 1) * half]))
        rows = pl.ds(pl.multiple_of(p * cols + y * (cols // 2), cols // 2), cols // 2)
        for b in range(3):
            first = 4 * half + b * (cols // 2)
            copies.append((w_down.at[rows, b * cols : (b + 1) * cols], b_outs[p].at[first : first + cols // 2]))
    for b in range(3):
        first = 4 * half + 3 * (cols // 2) + b * half
        copies.append((w_out.at[at, b * cols : (b + 1) * cols], b_outs[0].at[first : first + half]))
    copies = [pltpu.make_async_copy(a, b, sem.at[i]) for i, (a, b) in enumerate(copies)]
    for copy in copies:
        copy.start()
    small[...] = jnp.zeros_like(small)
    for r, ref in enumerate(vectors):
        small[r : r + 1, : ref.shape[0]] = ref[...].astype(F32).reshape(1, -1)
    s_out[pos_dev:, :] = small[...].astype(BF16)
    for copy in copies:
        copy.wait()


def unpack_kernel(a, b, c, d, vec_ref, up_ref, held, sem, *, sizes, pos_dev, cols):
    rel = lax.axis_index("shard")
    copies = [
        pltpu.make_async_copy(ref.at[pos_dev : pos_dev + 16], held.at[k ^ rel], sem.at[k])
        for k, ref in enumerate((a, b, c, d))
    ]
    for copy in copies:
        copy.start()
    for copy in copies:
        copy.wait()
    for j in range(4):
        part = held[j].astype(F32)
        for r, size in enumerate(sizes):
            vec_ref[r : r + 1, j * size : (j + 1) * size] = part[r : r + 1, :size]
        for p in range(3):
            up_ref[j * 3 + p : j * 3 + p + 1, :] = part[6:7, p * cols : (p + 1) * cols]


def table_kernel(slots, parents, freq_ref, out_ref, *, n_shard, n_branch, pos_dev):
    out, start = chosen_pieces(slots, parents, n_shard, n_branch, pos_dev)
    starts = [start] + [item[2] for item in out]
    shape = (pos_dev, PAIR)
    sign = jnp.where((lanes(shape) & 63) < 32, -1.0, 1.0)
    for i, first in enumerate(starts):
        pos = (lax.broadcasted_iota(jnp.int32, shape, 0) + first).astype(F32)
        angle = pos * freq_ref[...]
        out_ref[i * pos_dev : (i + 1) * pos_dev, :PAIR] = jnp.cos(angle)
        out_ref[i * pos_dev : (i + 1) * pos_dev, PAIR:] = jnp.sin(angle) * sign


def qkv_kernel(slots, parents, x_ref, *refs, n_shard, n_branch, pos_dev, n_far, hows, relative):
    far_refs, refs = refs[:n_far], refs[n_far:]
    w_refs, refs = refs[: len(hows)], refs[len(hows) :]
    vec, tab, n1t_ref, q_ref, k_ref, v_ref, xr_ref, w, far, w_sem, far_sem = refs
    i = pl.program_id(0)
    rel = relative_to(relative)
    width = x_ref.shape[-1]
    quarter = width // 4
    chosen, _ = chosen_pieces(slots, parents, n_shard, n_branch, pos_dev)

    def w_copy(a):
        at = row_block(hows[a][0], rel, quarter, *hows[a][1:])
        return pltpu.make_async_copy(w_refs[a], w.at[at], w_sem.at[a])

    def far_copy(t, ref):
        return pltpu.make_async_copy(ref, far.at[t], far_sem.at[t])

    @pl.when(i == 0)
    def _():
        for a in range(len(hows)):
            w_copy(a).start()
        for t, (holder, _, _) in enumerate(chosen):
            if n_far == 1:
                far_copy(t, far_refs[0].at[holder]).start()
            else:
                for k in range(n_far):

                    @pl.when(holder ^ rel == k)
                    def _(t=t, k=k):
                        far_copy(t, far_refs[k].at[0:pos_dev]).start()
        for a in range(len(hows)):
            w_copy(a).wait()

    for t in range(len(chosen)):

        @pl.when(i == 2 + t)
        def _(t=t):
            far_copy(t, far_refs[0].at[0:pos_dev] if n_far > 1 else far_refs[0].at[0]).wait()

    def tile(x, queries):
        n, _ = normed(x.astype(F32))
        n1 = (n * vec[0:1, :width] + vec[1:2, :width]).astype(BF16)
        turned = n1.T
        for j in range(4):
            rows = pl.ds(pl.multiple_of(place(j ^ rel) * quarter, quarter), quarter)
            n1t_ref[rows, :] = turned[j * quarter : (j + 1) * quarter, :]
        cosine, sine = tab[:, :PAIR], tab[:, PAIR:]

        def turn(first, ref, scale):
            y = dot(n1, w[:, first : first + width]) + vec[2:3, first : first + width]
            for h in range(width // PAIR):
                part = y[:, h * PAIR : (h + 1) * PAIR]
                out = part * cosine + swap_halves(part) * sine
                ref[:, h * PAIR : (h + 1) * PAIR] = (out * scale).astype(BF16)

        if queries:
            turn(0, q_ref, 1.0 / math.sqrt(width // HEADS))
        turn(width, k_ref, 1.0)
        v_ref[...] = (dot(n1, w[:, 2 * width :]) + vec[2:3, 2 * width : 3 * width]).astype(BF16)

    @pl.when(i < 2)
    def _():
        tile(x_ref[0], True)

    @pl.when(i >= 2)
    def _():
        x = far[jnp.maximum(i - 2, 0)]
        xr_ref[...] = x
        tile(x, False)


def attend_kernel(slots, parents, q_ref, k_ref, v_ref, e_ref, o_ref, linv_ref, k_aug, q_aug, *, n_shard, n_branch, pos_dev):
    rows, keys = q_ref.shape[0], k_ref.shape[0]
    blocks = pos_dev // BLOCK

    @pl.when(pl.program_id(0) == 0)
    def _():
        chosen, _ = chosen_pieces(slots, parents, n_shard, n_branch, pos_dev)
        shape = (pos_dev, PAIR)
        lane = lanes(shape) & 63
        block = lax.broadcasted_iota(jnp.int32, shape, 0) // BLOCK
        k_aug[:pos_dev] = jnp.where(lane - 32 == block, 1.0, 0.0).astype(BF16)
        k_aug[pos_dev : 2 * pos_dev] = jnp.where(lane == block, 1.0, 0.0).astype(BF16)
        for t, (_, valid, _) in enumerate(chosen):
            first = (2 + t) * pos_dev
            shut = jnp.where(valid > 0, 0.0, NEG)
            k_aug[first : first + pos_dev] = jnp.where(lane == 16, shut, 0.0).astype(BF16)
        for copy in range(2):
            clean = jnp.where((lane < blocks) & (lane >= block + copy), NEG, 0.0)
            noisy = (lane >= 32) & (lane < 32 + blocks)
            if copy == 0:
                noisy = noisy & (lane - 32 != block)
            out = jnp.where(noisy, NEG, clean)
            out = jnp.where(lane == 16, 1.0, out)
            q_aug[copy * pos_dev : (copy + 1) * pos_dev] = out.astype(BF16)

    low_q = lanes((rows, PAIR)) < 64
    low_k = lanes((keys, PAIR)) < 64
    q, k, v = q_ref[...], k_ref[...], v_ref[...]
    outs = []
    for h in range(2):
        here_q = low_q if h == 0 else ~low_q
        here_k = low_k if h == 0 else ~low_k
        q_h = jnp.where(here_q, q, q_aug[...])
        k_h = jnp.where(here_k, k, k_aug[...])
        v_h = jnp.where(here_k, v, jnp.ones_like(v))
        scores = dot_t(k_h, q_h)
        e = jnp.exp(scores - jnp.max(scores, axis=0, keepdims=True)).astype(BF16)
        e_ref[h] = e
        outs.append(t_dot(e, v_h))
    total = jnp.where(low_q, pltpu.roll(outs[0], 64, 1), pltpu.roll(outs[1], 64, 1))
    inv = 1.0 / total
    linv_ref[...] = inv
    o_ref[...] = (jnp.where(low_q, outs[0], outs[1]) * inv).astype(BF16)


def ff_kernel(*refs, part, tile, hows_o, hows, relative):
    first_part, last = part == 0, part == 2
    wo_refs, refs = (refs[: len(hows_o)], refs[len(hows_o) :]) if part != 1 else ((), refs)
    count = sum(2 if how == "whole" else 1 for _, how in hows)
    w_refs, refs = refs[:count], refs[count:]
    vec, bup, g_ref, *refs = refs
    if first_part:
        x_ref, att_ref, *refs = refs
        mid_ref, n2_ref, n2t, acc, dn2, bug_ref, *refs = refs
        g_refs, refs = refs[:6], refs[6:]
        wu, wd, gt, hid_ref, dup_ref, stage, sem, out_sem, wo = refs
    elif not last:
        n2_ref, n2t, acc_in, dn2_in, *refs = refs
        acc, dn2, bug_ref, *refs = refs
        g_refs, refs = refs[:6], refs[6:]
        wu, wd, gt, hid_ref, dup_ref, stage, sem, out_sem = refs
    else:
        n2_ref, n2t, acc_in, dn2_in, mid_ref, att_ref, *refs = refs
        out_ref, branch_ref, datt_ref, small_ref, attt, bug_ref, *refs = refs
        g_refs, refs = refs[:6], refs[6:]
        wu, wd, gt, hid_ref, dup_ref, stage, sem, out_sem, wo, acc, dn2 = refs
    rel = relative_to(relative)
    rows, width = g_ref.shape
    quarter = width // 4
    cols = wu.shape[1] // 4
    half = quarter // 2
    step_cols = 2 * cols

    o_copies = []
    for a, ref in enumerate(wo_refs):
        k, how = hows_o[a]
        at = row_block(k, rel, quarter, how)
        if how == "whole":
            o_copies.append(pltpu.make_async_copy(ref, wo.at[at], sem.at[0]))
        else:
            for b in range(3):
                first = 4 * half + 3 * (cols // 2) + b * half
                o_copies.append(
                    pltpu.make_async_copy(
                        ref.at[first : first + half], wo.at[at, b * cols : (b + 1) * cols], sem.at[0]
                    )
                )
    up_copies, down_copies = [], []
    at_ref = 0
    for k, how in hows:
        at = row_block(k, rel, quarter, how)
        if how == "whole":
            up_source, down_source = w_refs[at_ref], w_refs[at_ref + 1]
            at_ref += 2
        else:
            up_source = down_source = w_refs[at_ref]
            at_ref += 1
        for p in range(4):
            there = slice(p * cols, (p + 1) * cols)
            j = ORDER[p] ^ rel
            if how == "whole":
                source = up_source.at[:, pl.ds(pl.multiple_of(j * width + part * cols, cols), cols)]
            else:
                source = up_source.at[pl.ds(pl.multiple_of(j * half, half), half)]
            up_copies.append(pltpu.make_async_copy(source, wu.at[at, there], sem.at[1]))
        spot = ORDER.index(k) * cols
        if how == "whole":
            source = down_source.at[part * cols : (part + 1) * cols]
            down_copies.append(pltpu.make_async_copy(source, wd.at[spot : spot + cols], sem.at[2]))
        else:
            there = pl.ds(pl.multiple_of(spot + half_of(how) * (cols // 2), cols // 2), cols // 2)
            for b in range(3):
                first = 4 * half + b * (cols // 2)
                down_copies.append(
                    pltpu.make_async_copy(
                        down_source.at[first : first + cols // 2], wd.at[there, b * cols : (b + 1) * cols], sem.at[2]
                    )
                )

    for copy in (*o_copies, *up_copies, *down_copies):
        copy.start()
    gt[...] = g_ref[...].T
    if first_part:
        for copy in o_copies:
            copy.wait()
        for first in range(0, rows, tile):
            at = slice(first, first + tile)
            mid = x_ref[at].astype(F32) + dot(att_ref[at], wo[...]) + vec[3:4, :width]
            mid_ref[at] = mid
            n, _ = normed(mid)
            n2_ref[at] = (n * vec[4:5, :width] + vec[5:6, :width]).astype(BF16)
        turned = n2_ref[...].T
        for j in range(4):
            at = pl.ds(pl.multiple_of(place(j ^ rel) * quarter, quarter), quarter)
            n2t[at, :] = turned[j * quarter : (j + 1) * quarter, :]
    if last:
        turned = att_ref[...].T
        for j in range(4):
            at = pl.ds(pl.multiple_of(place(j ^ rel) * quarter, quarter), quarter)
            attt[at, :] = turned[j * quarter : (j + 1) * quarter, :]
    for copy in (*up_copies, *down_copies):
        copy.wait()

    for step in range(2):
        here = slice(step * step_cols, (step + 1) * step_cols)
        w_up, w_down = wu[:, here], wd[here, :]
        bias = jnp.concatenate(
            [bup[pl.ds((ORDER[2 * step + c] ^ rel) * 3 + part, 1), :] for c in range(2)], axis=1
        )
        for first in range(0, rows, tile):
            at = slice(first, first + tile)
            up = dot(n2_ref[at], w_up) + bias
            d_hidden = dot_t(g_ref[at], w_down)
            cube = 0.044715 * up * up
            th = jnp.tanh(0.7978845608028654 * (up + cube * up))
            left = 0.5 * (1.0 + th)
            hidden = (up * left).astype(BF16)
            slope = left + (0.5 * 0.7978845608028654) * up * (1.0 - th * th) * (1.0 + 3.0 * cube)
            d_up = (d_hidden * slope).astype(BF16)
            hid_ref[at] = hidden
            dup_ref[at] = d_up
            more, d_more = dot(hidden, w_down), dot_t(d_up, w_up)
            if step == 0 and first_part:
                acc[at] = more
                dn2[at] = d_more
            elif step == 0:
                acc[at] = acc_in[at] + more
                dn2[at] = dn2_in[at] + d_more
            else:
                acc[at] = acc[at] + more
                dn2[at] = dn2[at] + d_more
        sums = jnp.sum(dup_ref[...].astype(F32), axis=0, keepdims=True)
        grad_up = dot(n2t[...], dup_ref[...])
        grad_down = dot(gt[...], hid_ref[...])
        for c in range(2):
            p = 2 * step + c
            j = ORDER[p] ^ rel
            bug_ref[pl.ds(j, 1), :] = sums[:, c * cols : (c + 1) * cols]
            for r in range(4):
                block = slice(r * quarter, (r + 1) * quarter)
                stage[r, j] = grad_up[block, c * cols : (c + 1) * cols].astype(BF16)
                stage[p, 4 + r] = grad_down[block, c * cols : (c + 1) * cols].astype(BF16)

    n = stage.shape[1] // 2
    sources = (stage.at[0, :n], stage.at[0, n:], stage.at[1, :n], stage.at[1, n:], stage.at[2], stage.at[3])
    g_copies = [pltpu.make_async_copy(a, b, out_sem.at[i]) for i, (a, b) in enumerate(zip(sources, g_refs))]
    for copy in g_copies:
        copy.start()
    if last:
        for copy in o_copies:
            copy.wait()
        sums = [jnp.zeros((1, width), F32) for _ in range(4)]
        for first in range(0, rows, tile):
            at = slice(first, first + tile)
            mid = mid_ref[at]
            out_ref[at] = (mid + acc[at] + vec[7:8, :width]).astype(BF16)
            n, inv = normed(mid)
            d = dn2[at]
            g = g_ref[at].astype(F32)
            branch = (g + norm_back(d, n, inv, vec[4:5, :width])).astype(BF16)
            branch_ref[at] = branch
            datt_ref[at] = dot_t(branch, wo[...]).astype(BF16)
            for a, item in enumerate((branch.astype(F32), d * n, d, g)):
                sums[a] = sums[a] + jnp.sum(item, axis=0, keepdims=True)
        for a in range(4):
            small_ref[a : a + 1, :] = sums[a]
    for copy in g_copies:
        copy.wait()


def attend_back_kernel(q_ref, k_ref, v_ref, do_ref, o_ref, linv_ref, e_ref, n1t, tab, *refs, pos_dev, group):
    if group == 0:
        attt, branch, *refs = refs
    if group == 2:
        earlier, refs = refs[:3], refs[3:]
    dq_ref, dk_ref, dv_ref, bias_ref, *g_refs = refs
    rows, keys = q_ref.shape[0], k_ref.shape[0]
    quarter = n1t.shape[0] // 4
    quad = q_ref.shape[1] * 2
    scale = 1.0 / 8.0
    lane_q, lane_k = lanes((rows, PAIR)), lanes((keys, PAIR))

    def unturn(t, first):
        parts = []
        for i in range(t.shape[0] // pos_dev):
            at = first[i] * pos_dev
            cosine, sine = tab[at : at + pos_dev, :PAIR], tab[at : at + pos_dev, PAIR:]
            part = t[i * pos_dev : (i + 1) * pos_dev]
            parts.append(part * cosine - swap_halves(part) * sine)
        return jnp.concatenate(parts, axis=0)

    def pair(at):
        q, k, v = q_ref[...], k_ref[...], v_ref[...]
        do = do_ref[...].astype(F32) * linv_ref[...]
        product = do * o_ref[...].astype(F32)
        do_b = do.astype(BF16)
        d_q, d_k, d_v = [], [], []
        for h in range(2):
            here_q = (lane_q < 64) if h == 0 else (lane_q >= 64)
            here_k = (lane_k < 64) if h == 0 else (lane_k >= 64)
            free = 64 * (1 - h)
            delta = -jnp.sum(jnp.where(here_q, product, 0.0), axis=1, keepdims=True)
            high = delta.astype(BF16).astype(F32)
            low = delta - high
            extra = jnp.where(lane_q == free, high, jnp.where(lane_q == free + 1, low, 0.0))
            do_h = jnp.where(here_q, do, extra).astype(BF16)
            ones = jnp.where((lane_k == free) | (lane_k == free + 1), 1.0, 0.0).astype(BF16)
            v_h = jnp.where(here_k, v, ones)
            e = e_ref[h]
            d_scores = (dot_t(v_h, do_h) * e.astype(F32)).astype(BF16)
            d_v.append(dot(e, do_b))
            d_k.append(dot(d_scores, q))
            d_q.append(t_dot(d_scores, k))
        dv = jnp.where(lane_k < 64, d_v[0], d_v[1])
        dk = unturn(jnp.where(lane_k < 64, d_k[0], d_k[1]), [0, 0] + list(range(1, keys // pos_dev - 1)))
        dq = unturn(jnp.where(lane_q < 64, d_q[0], d_q[1]) * scale, [0, 0])
        dv_ref[:, at] = dv.astype(BF16)
        dk_ref[:, at] = dk.astype(BF16)
        dq_ref[:, at] = dq.astype(BF16)

    i = pl.program_id(0)
    for a in range(2):

        @pl.when(i == a)
        def _(a=a):
            pair(slice(a * PAIR, (a + 1) * PAIR))

    def put(unit, grad):
        half = g_refs[4].shape[0] // 2
        for r in range(4):
            block = grad[r * quarter : (r + 1) * quarter].astype(BF16)
            if r < 2:
                g_refs[2 * r + unit // half][unit % half] = block
            else:
                g_refs[2 + r][unit] = block

    if group == 0:

        @pl.when(i == 0)
        def _():
            for b in range(3):
                at = slice(b * quad, (b + 1) * quad)
                put(3 + b, dot(attt[...], branch[:, at]))

    @pl.when(i == 1)
    def _():
        mine = (dq_ref, dk_ref, dv_ref)
        for a, ref in enumerate(mine):
            d = ref[...]
            bias_ref[a : a + 1, :] = jnp.sum(d.astype(F32), axis=0, keepdims=True)
            if group != 1:
                put(a + (3 if group == 2 else 0), dot(n1t[:, : d.shape[0]], d))
        if group == 2:
            for a, ref in enumerate(earlier):
                put(a, dot(n1t[:, : ref.shape[0]], ref[...]))


def input_back_kernel(slots, parents, x_ref, xr_ref, *refs, n_shard, n_branch, pos_dev, relative, hows):
    grads, refs = refs[:9], refs[9:]
    w_refs, refs = refs[: len(hows)], refs[len(hows) :]
    if relative:
        vec, dn1_ref, small_ref, send_ref, two_ref, w, far, w_sem = refs
    else:
        vec, dn1_ref, small_ref, far_ref, w, far, w_sem = refs
    i = pl.program_id(0)
    rel = relative_to(relative)
    width = x_ref.shape[-1]
    quarter = width // 4
    quad = 2 * PAIR
    chosen, _ = chosen_pieces(slots, parents, n_shard, n_branch, pos_dev)
    n_far = len(chosen)

    def w_copy(a):
        at = row_block(hows[a][0], rel, quarter, *hows[a][1:])
        return pltpu.make_async_copy(w_refs[a], w.at[at], w_sem.at[a])

    @pl.when(i == 0)
    def _():
        for a in range(len(hows)):
            w_copy(a).start()
        far[...] = jnp.zeros_like(far)
        small_ref[...] = jnp.zeros_like(small_ref)
        for a in range(len(hows)):
            w_copy(a).wait()

    def sums(d, x):
        n, _ = normed(x.astype(F32))
        small_ref[0:1, :] = small_ref[0:1, :] + jnp.sum(d * n, axis=0, keepdims=True)
        small_ref[1:2, :] = small_ref[1:2, :] + jnp.sum(d, axis=0, keepdims=True)

    def back(a):
        d = jnp.concatenate([grads[3 * a + g][...] for g in range(3)], axis=1)
        return dot_t(d, w[:, a * width : (a + 1) * width])

    keys = back(1) + back(2)

    @pl.when(i < 2)
    def _():
        d = keys + back(0)
        dn1_ref[...] = d
        sums(d, x_ref[0])

    for t, (holder, _, _) in enumerate(chosen):

        @pl.when(i == 2 + t)
        def _(holder=holder):
            spot = place(holder ^ rel) if relative else holder
            far[spot] = far[spot] + keys
            sums(keys, xr_ref[...])

    @pl.when(i == 1 + n_far)
    def _():
        if relative:
            send_ref[...] = far[0:2].astype(BF16)
            two_ref[...] = far[2].astype(BF16)
        else:
            far_ref[...] = far[...].astype(BF16)


def final_kernel(x_ref, branch_ref, dn1_ref, got_ref, vec, out_ref):
    i = pl.program_id(0)
    d = dn1_ref[...] + jnp.where(i == 1, 1.0, 0.0) * got_ref[...].astype(F32)
    n, inv = normed(x_ref[0].astype(F32))
    back = norm_back(d, n, inv, vec[0:1, : d.shape[1]])
    out_ref[0] = (branch_ref[...].astype(F32) + back).astype(BF16)


def swap(x, axis, bit):
    n = lax.axis_size(axis)
    return lax.ppermute(x, axis, [(i, i ^ bit) for i in range(n)])


def core(x):
    return swap(x, "shard", 1)


def across(x):
    return swap(x, "shard", 2)


def tie(x, *others):
    return lax.optimization_barrier((x, *others))[0]


def select_bit(bit, a, b):
    return jnp.where(bit == 1, b, a)


class Reduction:
    def __init__(self, chunk):
        *send, self.two, self.zero = chunk
        self.got = [core(item) for item in send]
        self.step = 0

    def go(self, *after):
        got = tie(self.got, *after)
        r = lax.axis_index("rep")
        if self.step == 0:
            self.part = self.two + jnp.concatenate(got[:2], axis=0)
            self.kept = self.zero + jnp.concatenate(got[2:], axis=0)
            self.got = across(self.part)
        elif self.step in (1, 2):
            bit = self.step
            total = self.kept + got
            size = total.shape[1] // 2
            here = (r // bit) & 1
            self.kept = lax.dynamic_slice_in_dim(total, here * size, size, 1)
            self.part = lax.dynamic_slice_in_dim(total, (1 - here) * size, size, 1)
            self.got = swap(self.part, "rep", bit)
        elif self.step == 3:
            self.part = self.kept + got
            self.got = swap(self.part, "rep", 4)
        elif self.step == 4:
            self.part = self.part + got
            self.got = swap(self.part, "rep", 2)
        else:
            here = (r // 2) & 1
            self.part = jnp.concatenate(
                [select_bit(here, self.part, got), select_bit(here, got, self.part)], axis=1
            )
            self.got = swap(self.part, "rep", 1)
        self.step += 1
        return self.part


class SmallSum:
    LINKS = (("shard", 1), ("shard", 2), ("rep", 1), ("rep", 2), ("rep", 4))

    def __init__(self, x):
        self.part, self.step = x, 0
        self.got = swap(x, *self.LINKS[0])

    def go(self, *after):
        self.part = self.part + tie(self.got, *after)
        self.step += 1
        if self.step < 5:
            self.got = swap(self.part, *self.LINKS[self.step])
        return self.part


class FarGrad:
    def __init__(self, send, two):
        self.two, self.got, self.step = two, core(send), 0

    def go(self, *after):
        got = tie(self.got, *after)
        if self.step == 0:
            self.own = got[1]
            self.part = self.two + got[0]
            self.got = across(self.part)
        else:
            self.part = self.own + got
        self.step += 1
        return self.part


def collect_kernel(*refs, quarter):
    parts, (up_ref, down_ref, whole_ref) = refs[:6], refs[6:]
    half = quarter // 2
    y = lax.axis_index("rep") & 1
    mine = pl.ds(pl.multiple_of(y * half, half), half)
    other = pl.ds(pl.multiple_of((1 - y) * half, half), half)
    for p in range(3):
        cols = parts[2 * p].shape[2]
        for which, at in ((0, mine), (1, other)):
            ref = parts[2 * p + which]
            for j in range(4):
                first = j * 3 * cols + p * cols
                up_ref[at, first : first + cols] = ref[j].astype(F32)
                whole_ref[j, at, :] = ref[4 + j].astype(F32)
        down_ref[p * cols : (p + 1) * cols, :] = whole_ref[...].reshape(4 * quarter, cols).T


def collect_qkv_kernel(*refs, quarter):
    parts, (out_ref, qkv_ref) = refs[:4], refs[4:]
    half = quarter // 2
    y = lax.axis_index("rep") & 1
    cols = parts[0].shape[2]
    for which in range(2):
        at = pl.ds(pl.multiple_of((y if which == 0 else 1 - y) * half, half), half)
        first, second = parts[which], parts[2 + which]
        for b in range(3):
            out_ref[at, b * cols : (b + 1) * cols] = first[3 + b].astype(F32)
        for a in range(3):
            for g, block in enumerate((first[a], second[a], second[3 + a])):
                qkv_ref[at, (3 * a + g) * cols : (3 * a + g + 1) * cols] = block.astype(F32)


def shards(
    states,
    cotangent,
    norm1_gain,
    norm1_bias,
    qkv_weight,
    qkv_bias,
    out_weight,
    out_bias,
    norm2_gain,
    norm2_bias,
    up_weight,
    up_bias,
    down_weight,
    down_bias,
    slots,
    parents,
):
    n_shard = lax.axis_size("shard")
    n_branch = n_shard // 4
    pos_dev, width = states.shape[1], states.shape[2]
    ff = up_weight.shape[1]
    rows = 2 * pos_dev
    n_far = n_branch + 1
    keys = rows + n_far * pos_dev
    relative = n_shard == 4 and lax.axis_size("rep") == 8
    quarter = width // 4
    cols = ff // 12
    quad = 2 * PAIR
    me = lax.axis_index("shard")
    sizes = dict(n_shard=n_shard, n_branch=n_branch, pos_dev=pos_dev)
    bound = functools.partial
    shape = jax.ShapeDtypeStruct
    vectors = (norm1_gain, norm1_bias, qkv_bias, out_bias, norm2_gain, norm2_bias, up_bias, down_bias)

    natural = [(k, "whole") for k in range(4)]
    if relative:
        half = quarter // 2
        rest = 4 * half + 3 * (cols // 2)
        pack_shapes = [
            shape((pos_dev + 16, width), BF16),
            shape((rest + 3 * half, cols), BF16),
            shape((rest, cols), BF16),
            shape((rest, cols), BF16),
        ]
        packed = pl.pallas_call(
            bound(pack_kernel, quarter=quarter, width=width, cols=cols),
            out_shape=pack_shapes,
            grid=(1,),
            in_specs=[whole(item.shape) for item in vectors] + [ANY] * 4,
            out_specs=[whole(item.shape) for item in pack_shapes],
            scratch_shapes=[pltpu.VMEM((16, width), F32), pltpu.SemaphoreType.DMA((32,))],
            compiler_params=params(),
            cost_estimate=cost(2),
            name="pack",
        )
        q_two = across(qkv_weight)
        q_one = core(qkv_weight)
        x_own, *b_half = packed(*vectors, states, out_weight, up_weight, down_weight)
        x_one = core(x_own)
        x_two = across(x_own)
        x_far = [x_own, x_one, x_two, core(x_two)]
        w_qkv = [qkv_weight, q_one, q_two, core(q_two)]
        how_qkv = natural
        how_out = [(0, "whole"), (1, "whole"), (2, "direct"), (2, "via"), (3, "direct"), (3, "via")]
        o_one, u_one, d_one = core(out_weight), core(up_weight), core(down_weight)
        b_two = [across(tie(b_half[0], x_two, q_two))]
        b_two += [across(tie(b_half[p], b_two[0])) for p in (1, 2)]
        b_via = [swap(item, "rep", 1) for item in b_two]
        b_three = [core(item) for item in b_two]
        b_last = [core(item) for item in b_via]
        w_out = [out_weight, o_one, b_two[0], b_via[0], b_three[0], b_last[0]]
        w_ff = [
            [up_weight, down_weight, u_one, d_one, b_two[p], b_via[p], b_three[p], b_last[p]] for p in range(3)
        ]
        how_ff = how_out
        vec, b_up = pl.pallas_call(
            bound(unpack_kernel, sizes=[item.shape[0] for item in vectors], pos_dev=pos_dev, cols=cols),
            out_shape=[shape((8, ff), F32), shape((12, cols), F32)],
            grid=(1,),
            in_specs=[ANY] * 4,
            out_specs=[whole((8, ff)), whole((12, cols))],
            scratch_shapes=[pltpu.VMEM((4, 16, width), BF16), pltpu.SemaphoreType.DMA((4,))],
            compiler_params=params(),
            cost_estimate=cost(2),
            name="unpack",
        )(*x_far)
    else:
        gather = lambda item: lax.all_gather(item, "shard", axis=0, tiled=True)
        rows_of = lambda item: [item[j * quarter : (j + 1) * quarter] for j in range(4)]
        w_qkv, how_qkv = rows_of(gather(qkv_weight)), natural
        x_far = [gather(states[1][None])]
        w_out, how_out = rows_of(gather(out_weight)), natural
        ups, downs = rows_of(gather(up_weight)), gather(down_weight)
        pieces = []
        for k in range(4):
            pieces += [ups[k], downs[k * width : (k + 1) * width]]
        w_ff, how_ff = [pieces] * 3, natural
        small = lax.all_gather(jnp.concatenate(vectors), "shard", axis=0)
        lines, at = [], 0
        for item in vectors:
            n = item.shape[0]
            line = small[:, at : at + n].reshape(1, n_shard * n).astype(F32)
            lines.append(jnp.pad(line, ((0, 0), (0, ff - n_shard * n))))
            at += n
        vec = jnp.concatenate(lines, axis=0)
        b_up = vec[6].reshape(12, cols)

    freq = jnp.exp(-jnp.log(10000.0) * jnp.arange(32, dtype=F32) / 32)
    freq = jnp.tile(freq, 4).reshape(1, PAIR)
    table = pl.pallas_call(
        bound(table_kernel, **sizes),
        out_shape=shape(((1 + n_far) * pos_dev, 2 * PAIR), F32),
        grid=(1,),
        in_specs=[SMEM, SMEM, whole((1, PAIR))],
        out_specs=whole(((1 + n_far) * pos_dev, 2 * PAIR)),
        compiler_params=params(),
        cost_estimate=cost(3.5),
        name="rotary_table",
    )(slots, parents, freq)

    own = lambda i: (jnp.minimum(i, 1), 0)
    own3 = lambda i: (jnp.minimum(i, 1), 0, 0)
    each = lambda i: (i, 0)
    beyond = lambda i: (jnp.maximum(i - 2, 0), 0)
    n1t, q, k, v, x_seen = pl.pallas_call(
        bound(qkv_kernel, n_far=len(x_far), hows=how_qkv, relative=relative, **sizes),
        out_shape=[
            shape((width, keys), BF16),
            shape((rows, width), BF16),
            shape((keys, width), BF16),
            shape((keys, width), BF16),
            shape((n_far * pos_dev, width), BF16),
        ],
        grid=(2 + n_far,),
        in_specs=[SMEM, SMEM, pl.BlockSpec((1, pos_dev, width), own3)]
        + [ANY] * (len(x_far) + len(how_qkv))
        + [whole((8, ff)), pl.BlockSpec((pos_dev, 2 * PAIR), lambda i: (jnp.maximum(i - 1, 0), 0))],
        out_specs=[
            pl.BlockSpec((width, pos_dev), lambda i: (0, i)),
            pl.BlockSpec((pos_dev, width), own),
            pl.BlockSpec((pos_dev, width), each),
            pl.BlockSpec((pos_dev, width), each),
            pl.BlockSpec((pos_dev, width), beyond),
        ],
        scratch_shapes=[
            pltpu.VMEM((width, 3 * width), BF16),
            pltpu.VMEM((n_far, pos_dev, width), BF16),
            pltpu.SemaphoreType.DMA((10,)),
            pltpu.SemaphoreType.DMA((n_far,)),
        ],
        compiler_params=params(),
        cost_estimate=cost(11),
        name="norm_qkv",
    )(slots, parents, states, *x_far, *w_qkv, vec, table)

    pair = lambda i: (0, i)
    n_pair = width // PAIR
    e, attended, linv = pl.pallas_call(
        bound(attend_kernel, **sizes),
        out_shape=[
            shape((HEADS, keys, rows), BF16),
            shape((rows, width), BF16),
            shape((rows, width), F32),
        ],
        grid=(n_pair,),
        in_specs=[
            SMEM,
            SMEM,
            pl.BlockSpec((rows, PAIR), pair),
            pl.BlockSpec((keys, PAIR), pair),
            pl.BlockSpec((keys, PAIR), pair),
        ],
        out_specs=[
            pl.BlockSpec((2, keys, rows), lambda i: (i, 0, 0)),
            pl.BlockSpec((rows, PAIR), pair),
            pl.BlockSpec((rows, PAIR), pair),
        ],
        scratch_shapes=[pltpu.VMEM((keys, PAIR), BF16), pltpu.VMEM((rows, PAIR), BF16)],
        compiler_params=params(),
        cost_estimate=cost(17),
        name="attend",
    )(slots, parents, tie(q, b_two[0]) if relative else q, k, v)

    if relative:
        attended = tie(attended, *b_via)

    x_rows = states.reshape(rows, width)
    g_rows = cotangent.reshape(rows, width)
    full = whole((rows, width))
    turned = whole((width, rows))
    vecs = [whole((8, ff)), whole((12, cols))]
    wide, low = shape((rows, width), F32), shape((rows, width), BF16)

    def feed(part, ins, in_specs, outs, out_specs, scratch):
        units = 8
        weights = ([] if part == 1 else w_out) + w_ff[part]
        result = pl.pallas_call(
            bound(ff_kernel, part=part, tile=pos_dev, hows_o=how_out, hows=how_ff, relative=relative),
            out_shape=outs
            + [
                shape((4, cols), F32),
                *[shape((units // 2, quarter, cols), BF16)] * 4,
                shape((units, quarter, cols), BF16),
                shape((units, quarter, cols), BF16),
            ],
            grid=(1,),
            in_specs=[ANY] * len(weights) + vecs + [full] + in_specs,
            out_specs=out_specs + [whole((4, cols))] + [ANY] * 6,
            scratch_shapes=[
                pltpu.VMEM((width, 4 * cols), BF16),
                pltpu.VMEM((4 * cols, width), BF16),
                pltpu.VMEM((width, rows), BF16),
                pltpu.VMEM((rows, 2 * cols), BF16),
                pltpu.VMEM((rows, 2 * cols), BF16),
                pltpu.VMEM((4, units, quarter, cols), BF16),
                pltpu.SemaphoreType.DMA((3,)),
                pltpu.SemaphoreType.DMA((6,)),
            ]
            + scratch,
            compiler_params=params(),
            cost_estimate=cost(13),
            name=("feed_first", "feed_second", "feed_third")[part],
        )(*weights, vec, b_up, g_rows, *ins)
        return result[:-6], result[-6:]

    square = pltpu.VMEM((width, width), BF16)
    (mid, n2, n2t, acc, dn2, bug0), chunk0 = feed(
        0, (x_rows, attended), [full, full], [wide, low, shape((width, rows), BF16), wide, wide],
        [full, full, turned, full, full], [square],
    )
    if relative:
        sum0 = Reduction(chunk0)
        n2 = tie(n2, sum0.go(bug0))
    (acc, dn2, bug1), chunk1 = feed(
        1, (n2, n2t, acc, dn2), [full, turned, full, full], [wide, wide], [full, full], []
    )
    if relative:
        sum1 = Reduction(chunk1)
        n2 = tie(n2, sum1.go(sum0.go(bug1)))
    (output, branch, d_att, small2, attt, bug2), chunk2 = feed(
        2, (n2, n2t, acc, dn2, mid, attended), [full, turned, full, full, full, full],
        [low, low, low, shape((8, width), F32), shape((width, rows), BF16)], [full, full, full, whole((8, width)), turned],
        [square, pltpu.VMEM((rows, width), F32), pltpu.VMEM((rows, width), F32)],
    )
    if relative:
        sum2 = Reduction(chunk2)

    def back(g, d_att, *more):
        here = lambda i: (0, 2 * g + i)
        grads = [] if g == 1 else [shape((3, quarter, quad), BF16)] * 4 + [shape((6, quarter, quad), BF16)] * 2
        outs = [shape((n, quad), t) for n, t in ((rows, BF16), (keys, BF16), (keys, BF16), (8, F32))] + grads
        return pl.pallas_call(
            bound(attend_back_kernel, pos_dev=pos_dev, group=g),
            out_shape=outs,
            grid=(2,),
            in_specs=[
                pl.BlockSpec((rows, PAIR), here),
                pl.BlockSpec((keys, PAIR), here),
                pl.BlockSpec((keys, PAIR), here),
                pl.BlockSpec((rows, PAIR), here),
                pl.BlockSpec((rows, PAIR), here),
                pl.BlockSpec((rows, PAIR), here),
                pl.BlockSpec((2, keys, rows), lambda i: (2 * g + i, 0, 0)),
                whole((width, keys)),
                whole(((1 + n_far) * pos_dev, 2 * PAIR)),
            ]
            + [whole(item.shape) for item in more],
            out_specs=[whole(item.shape) for item in outs],
            compiler_params=params(),
            cost_estimate=cost(11),
            name=f"attend_back_{g}",
        )(q, k, v, d_att, attended, linv, e, n1t, table, *more)

    def turns(last, *items):
        for item in items:
            last = item.go(last)
        return last

    backs = []
    for g in range(3):
        if relative:
            if g == 0:
                last = turns(small2, sum0, sum1, sum2)
            elif g == 1:
                last = turns(backs[0][3], sum0, sum1, sum2, sum3)
            else:
                last = turns(backs[1][3], sum0, sum1, sum2, sum3)
            d_att = tie(d_att, last)
        backs.append(back(g, d_att, *((attt, branch), (), tuple(backs[1][:3]) if g == 2 else ())[g]))
        if relative and g == 0:
            sum3 = Reduction(backs[0][4:])
        if relative and g == 2:
            sum4 = Reduction(backs[2][4:])
    d_all = [backs[g][a] for a in range(3) for g in range(3)]
    small_qkv = jnp.concatenate([item[3][:3] for item in backs], axis=1)
    if relative:
        last = turns(backs[2][3], sum0, sum1, sum2, sum3, sum4)
        d_all[0] = tie(d_all[0], last)

    far_shapes = (
        [shape((2, pos_dev, width), BF16), shape((pos_dev, width), BF16)]
        if relative
        else [shape((n_shard, pos_dev, width), BF16)]
    )
    dn1, small1, *far = pl.pallas_call(
        bound(input_back_kernel, relative=relative, hows=how_qkv, **sizes),
        out_shape=[shape((rows, width), F32), shape((8, width), F32), *far_shapes],
        grid=(2 + n_far,),
        in_specs=[
            SMEM,
            SMEM,
            pl.BlockSpec((1, pos_dev, width), own3),
            pl.BlockSpec((pos_dev, width), beyond),
        ]
        + [pl.BlockSpec((pos_dev, quad), own)] * 3
        + [pl.BlockSpec((pos_dev, quad), each)] * 6
        + [ANY] * len(how_qkv)
        + [whole((8, ff))],
        out_specs=[pl.BlockSpec((pos_dev, width), own), whole((8, width))]
        + [whole(item.shape) for item in far_shapes],
        scratch_shapes=[
            pltpu.VMEM((width, 3 * width), BF16),
            pltpu.VMEM((n_shard, pos_dev, width), F32),
            pltpu.SemaphoreType.DMA((10,)),
        ],
        compiler_params=params(),
        cost_estimate=cost(10),
        name="input_back",
    )(slots, parents, states, x_seen, *d_all, *w_qkv, vec)

    collect = pl.pallas_call(
        bound(collect_kernel, quarter=quarter),
        out_shape=[shape((quarter, ff), F32), shape((ff // 4, width), F32)],
        scratch_shapes=[pltpu.VMEM((4, quarter, cols), F32)],
        compiler_params=params(),
        cost_estimate=cost(4),
        name="collect",
    )
    vectors_grad = jnp.concatenate([small1[:2], small_qkv, small2[:4], jnp.concatenate([bug0, bug1, bug2], axis=1)], axis=0)
    if relative:
        far_sum = FarGrad(*far)
        small_sum = SmallSum(vectors_grad)
        order = [
            sum1, sum2, sum3, sum4, far_sum, small_sum, sum2, sum3, sum4, small_sum, sum3, far_sum, sum4,
            small_sum, None, sum4, small_sum, sum4, small_sum,
        ]
        last = small1
        for item in order:
            if item is None:
                halves = [half for part in (sum0, sum1, sum2) for half in (part.part, part.got)]
                grad_up, grad_down = collect(tie(halves[0], last), *halves[1:])
                last = grad_down
            else:
                last = item.go(last)
        counts = [item.step for item in (sum0, sum1, sum2, sum3, sum4)]
        assert counts == [6] * 5, counts
        got, total = far_sum.part, small_sum.part
    else:
        got = lax.psum_scatter(far[0], "shard", scatter_dimension=0)
        total = lax.psum(vectors_grad, ("rep", "shard"))
    states_grad = pl.pallas_call(
        final_kernel,
        out_shape=shape((2, pos_dev, width), BF16),
        grid=(2,),
        in_specs=[
            pl.BlockSpec((1, pos_dev, width), lambda i: (i, 0, 0)),
            pl.BlockSpec((pos_dev, width), each),
            pl.BlockSpec((pos_dev, width), each),
            whole((pos_dev, width)),
            whole((8, ff)),
        ],
        out_specs=pl.BlockSpec((1, pos_dev, width), lambda i: (i, 0, 0)),
        compiler_params=params(),
        cost_estimate=cost(4),
        name="states_back",
    )(states, branch, dn1, got, vec)

    def up_of(parts):
        return jnp.stack([item[:4] for item in parts]).transpose(2, 1, 0, 3).reshape(-1, ff)

    def down_of(parts):
        return jnp.stack([item[4:8] for item in parts]).transpose(0, 3, 1, 2).reshape(3, -1, width)

    def out_of(part):
        return part[3:].transpose(1, 0, 2).reshape(-1, width)

    def qkv_of(parts):
        return jnp.stack(parts).transpose(2, 1, 0, 3).reshape(-1, 3 * width)

    if relative:
        grad_out, grad_qkv = pl.pallas_call(
            bound(collect_qkv_kernel, quarter=quarter),
            out_shape=[shape((quarter, width), F32), shape((quarter, 3 * width), F32)],
            compiler_params=params(),
            cost_estimate=cost(2),
            name="collect_qkv",
        )(sum3.part, sum3.got, sum4.part, sum4.got)
    else:

        def natural_order(chunk):
            *send, two, zero = chunk
            return [zero, jnp.concatenate(send[2:]), two, jnp.concatenate(send[:2])]

        parts = list(zip(*(natural_order(chunk) for chunk in (chunk0, chunk1, chunk2))))
        quads = list(zip(natural_order(backs[0][4:]), natural_order(backs[2][4:])))
        ups = jnp.concatenate([up_of(item) for item in parts], axis=0)
        downs = jnp.concatenate([down_of(item).reshape(-1, width) for item in parts], axis=0)
        outs = jnp.concatenate([out_of(item[0]) for item in quads], axis=0)
        qkvs = jnp.concatenate([qkv_of((a[:3], b[:3], b[3:])) for a, b in quads], axis=0)

        def reduced(item):
            part = lax.psum_scatter(item, "shard", scatter_dimension=0, tiled=True)
            return lax.psum(part, "rep").astype(F32)

        grad_up, grad_down, grad_out, grad_qkv = (reduced(item) for item in (ups, downs, outs, qkvs))

    def own_rows(first, count):
        line = total[first : first + count].reshape(-1)
        n = line.shape[0] // n_shard
        return lax.dynamic_slice_in_dim(line, me * n, n)

    return (
        output.reshape(2, pos_dev, width),
        states_grad,
        own_rows(0, 1),
        own_rows(1, 1),
        grad_qkv,
        own_rows(2, 3),
        grad_out,
        own_rows(5, 1),
        own_rows(6, 1),
        own_rows(7, 1),
        grad_up,
        own_rows(9, 4),
        grad_down,
        own_rows(8, 1),
    )


def solution(mesh):
    in_specs = (
        P(None, ("rep", "shard"), None),
        P(None, ("rep", "shard"), None),
        P("shard"),
        P("shard"),
        P("shard", None),
        P("shard"),
        P("shard", None),
        P("shard"),
        P("shard"),
        P("shard"),
        P("shard", None),
        P("shard"),
        P("shard", None),
        P("shard"),
        P("rep", None),
        P("rep", None),
    )
    out_specs = (
        P(None, ("rep", "shard"), None),
        P(None, ("rep", "shard"), None),
        P("shard"),
        P("shard"),
        P("shard", None),
        P("shard"),
        P("shard", None),
        P("shard"),
        P("shard"),
        P("shard"),
        P("shard", None),
        P("shard"),
        P("shard", None),
        P("shard"),
    )
    return jax.shard_map(shards, mesh=mesh, in_specs=in_specs, out_specs=out_specs, check_vma=False)
```

```python
import functools
import math

import jax
import jax.numpy as jnp
from jax import lax
from jax.experimental import pallas as pl
from jax.experimental.pallas import tpu as pltpu
from jax.sharding import PartitionSpec as P

HEADS = 12
BLOCK = 16
NEG = -1e30
PAIR = 128
F32 = jnp.float32
BF16 = jnp.bfloat16
ANY = pl.BlockSpec(memory_space=pltpu.HBM)


SMEM = pl.BlockSpec(memory_space=pltpu.SMEM)


def params(mib=58):
    return pltpu.CompilerParams(vmem_limit_bytes=mib * 2**20)


def cost(us):
    return pl.CostEstimate(flops=int(us * 1.15e9), bytes_accessed=0, transcendentals=0)


def whole(shape):
    return pl.BlockSpec(shape, lambda *_: (0,) * len(shape))


def place(rel):
    return jnp.where(rel == 3, 0, jnp.where(rel == 0, 3, rel))


ORDER = (3, 1, 2, 0)


def dot(a, b):
    return lax.dot_general(a, b, (((1,), (0,)), ((), ())), preferred_element_type=F32)


def dot_t(a, b):
    return lax.dot_general(a, b, (((1,), (1,)), ((), ())), preferred_element_type=F32)


def t_dot(a, b):
    return lax.dot_general(a, b, (((0,), (0,)), ((), ())), preferred_element_type=F32)


def normed(x):
    spread = x - jnp.mean(x, axis=-1, keepdims=True)
    inv = lax.rsqrt(jnp.mean(spread * spread, axis=-1, keepdims=True) + 1e-05)
    return spread * inv, inv


def norm_back(d, n, inv, gain):
    e = d * gain
    return inv * (
        e - jnp.mean(e, axis=-1, keepdims=True) - n * jnp.mean(e * n, axis=-1, keepdims=True)
    )


def lanes(shape):
    return lax.broadcasted_iota(jnp.int32, shape, len(shape) - 1)


def swap_halves(t):
    return jnp.where((lanes(t.shape) & 63) < 32, pltpu.roll(t, 96, 1), pltpu.roll(t, 32, 1))

def chosen_pieces(slots, parents, n_shard, n_branch, pos_dev):
    me = lax.axis_index("shard")
    mine = slots[0, me]
    seg = jnp.where(mine < n_branch, 0, mine - n_branch + 1)
    parent = parents[0, seg]

    def holder(piece):
        found = me
        for j in range(n_shard):
            found = jnp.where(slots[0, j] == piece, j, found)
        return found

    out = []
    for run in range(n_branch):
        valid = jnp.where(seg > 0, 1, jnp.where(mine > run, 1, 0))
        out.append((holder(run), valid, run * pos_dev))
    has = jnp.where(parent > 0, 1, 0)
    out.append((holder(jnp.where(parent > 0, n_branch + parent - 1, -1)), has, n_branch * pos_dev))
    start = jnp.where(
        mine < n_branch,
        mine * pos_dev,
        jnp.where(mine < 2 * n_branch, n_branch * pos_dev, (n_branch + 1) * pos_dev),
    )
    return out, start


def relative_to(relative):
    return lax.axis_index("shard") if relative else jnp.zeros((), jnp.int32)


def half_of(how):
    y = lax.axis_index("rep") & 1
    return y if how == "direct" else 1 - y


def row_block(k, rel, quarter, how, chunk=None):
    first = (k ^ rel) * quarter
    if how == "whole":
        return pl.ds(pl.multiple_of(first, 16), quarter)
    first = first + half_of(how) * (quarter // 2)
    if chunk is None:
        return pl.ds(pl.multiple_of(first, 16), quarter // 2)
    return pl.ds(pl.multiple_of(first + chunk * (quarter // 4), 16), quarter // 4)


def pack_kernel(*refs, quarter, width, cols):
    vectors, refs = refs[:8], refs[8:]
    states, w_out, w_up, w_down, s_out, *refs = refs
    b_outs, (small, sem) = refs[:3], refs[3:]
    half = quarter // 2
    y = lax.axis_index("rep") & 1
    at = pl.ds(pl.multiple_of(y * half, half), half)
    pos_dev = states.shape[1]
    copies = [(states.at[1], s_out.at[0:pos_dev])]
    for p in range(3):
        for j in range(4):
            source = w_up.at[at, j * width + p * cols : j * width + (p + 1) * cols]
            copies.append((source, b_outs[p].at[j * half : (j + 1) * half]))
        rows = pl.ds(pl.multiple_of(p * cols + y * (cols // 2), cols // 2), cols // 2)
        for b in range(3):
            first = 4 * half + b * (cols // 2)
            copies.append((w_down.at[rows, b * cols : (b + 1) * cols], b_outs[p].at[first : first + cols // 2]))
    for b in range(3):
        first = 4 * half + 3 * (cols // 2) + b * half
        copies.append((w_out.at[at, b * cols : (b + 1) * cols], b_outs[0].at[first : first + half]))
    copies = [pltpu.make_async_copy(a, b, sem.at[i]) for i, (a, b) in enumerate(copies)]
    for copy in copies:
        copy.start()
    small[...] = jnp.zeros_like(small)
    for r, ref in enumerate(vectors):
        small[r : r + 1, : ref.shape[0]] = ref[...].astype(F32).reshape(1, -1)
    s_out[pos_dev:, :] = small[...].astype(BF16)
    for copy in copies:
        copy.wait()


def unpack_kernel(a, b, c, d, vec_ref, up_ref, held, sem, *, sizes, pos_dev, cols):
    rel = lax.axis_index("shard")
    copies = [
        pltpu.make_async_copy(ref.at[pos_dev : pos_dev + 16], held.at[k ^ rel], sem.at[k])
        for k, ref in enumerate((a, b, c, d))
    ]
    for copy in copies:
        copy.start()
    for copy in copies:
        copy.wait()
    for j in range(4):
        part = held[j].astype(F32)
        for r, size in enumerate(sizes):
            vec_ref[r : r + 1, j * size : (j + 1) * size] = part[r : r + 1, :size]
        for p in range(3):
            up_ref[j * 3 + p : j * 3 + p + 1, :] = part[6:7, p * cols : (p + 1) * cols]


def table_kernel(slots, parents, freq_ref, out_ref, *, n_shard, n_branch, pos_dev):
    out, start = chosen_pieces(slots, parents, n_shard, n_branch, pos_dev)
    starts = [start] + [item[2] for item in out]
    shape = (pos_dev, PAIR)
    sign = jnp.where((lanes(shape) & 63) < 32, -1.0, 1.0)
    for i, first in enumerate(starts):
        pos = (lax.broadcasted_iota(jnp.int32, shape, 0) + first).astype(F32)
        angle = pos * freq_ref[...]
        out_ref[i * pos_dev : (i + 1) * pos_dev, :PAIR] = jnp.cos(angle)
        out_ref[i * pos_dev : (i + 1) * pos_dev, PAIR:] = jnp.sin(angle) * sign


def qkv_kernel(slots, parents, x_ref, *refs, n_shard, n_branch, pos_dev, n_far, hows, relative):
    far_refs, refs = refs[:n_far], refs[n_far:]
    w_refs, refs = refs[: len(hows)], refs[len(hows) :]
    vec, tab, n1t_ref, q_ref, k_ref, v_ref, xr_ref, w, n1, w_sem, far_sem = refs
    i = pl.program_id(0)
    rel = relative_to(relative)
    width = x_ref.shape[-1]
    quarter = width // 4
    quad = 2 * PAIR
    rows = 2 * pos_dev
    chosen, _ = chosen_pieces(slots, parents, n_shard, n_branch, pos_dev)

    def w_copies(g):
        out = []
        for ref, (k, how) in zip(w_refs, hows):
            for a in range(3):
                source = ref.at[:, a * width + g * quad : a * width + (g + 1) * quad]
                target = w.at[g, row_block(k, rel, quarter, how), a * quad : (a + 1) * quad]
                out.append(pltpu.make_async_copy(source, target, w_sem.at[g]))
        return out

    def far_copy(t, ref):
        return pltpu.make_async_copy(ref, xr_ref.at[t * pos_dev : (t + 1) * pos_dev], far_sem.at[t])

    @pl.when(i == 0)
    def _():
        for t, (holder, _, _) in enumerate(chosen):
            if n_far == 1:
                far_copy(t, far_refs[0].at[holder]).start()
            else:
                for k in range(n_far):

                    @pl.when(holder ^ rel == k)
                    def _(t=t, k=k):
                        far_copy(t, far_refs[k].at[0:pos_dev]).start()
        for g in range(3):
            for copy in w_copies(g):
                copy.start()
        for t in range(2 + len(chosen)):
            if t >= 2:
                far_copy(t - 2, far_refs[0].at[0:pos_dev] if n_far > 1 else far_refs[0].at[0]).wait()
            x = x_ref[t] if t < 2 else xr_ref[(t - 2) * pos_dev : (t - 1) * pos_dev]
            n, _ = normed(x.astype(F32))
            part = (n * vec[0:1, :width] + vec[1:2, :width]).astype(BF16)
            n1[t * pos_dev : (t + 1) * pos_dev] = part
            turned = part.T
            for j in range(4):
                at = pl.ds(pl.multiple_of(place(j ^ rel) * quarter, quarter), quarter)
                n1t_ref[at, t * pos_dev : (t + 1) * pos_dev] = turned[j * quarter : (j + 1) * quarter, :]

    for g in range(3):

        @pl.when(i == g)
        def _(g=g):
            for copy in w_copies(g):
                copy.wait()

            def product(a, n):
                bias = vec[2:3, a * width + g * quad : a * width + (g + 1) * quad]
                return dot(n1[:n], w[g, :, a * quad : (a + 1) * quad]) + bias

            def turn(y, ref, scale):
                for t in range(y.shape[0] // pos_dev):
                    first = max(t - 1, 0) * pos_dev
                    cosine, sine = tab[first : first + pos_dev, :PAIR], tab[first : first + pos_dev, PAIR:]
                    for h in range(2):
                        part = y[t * pos_dev : (t + 1) * pos_dev, h * PAIR : (h + 1) * PAIR]
                        out = part * cosine + swap_halves(part) * sine
                        ref[t * pos_dev : (t + 1) * pos_dev, h * PAIR : (h + 1) * PAIR] = (out * scale).astype(BF16)

            turn(product(0, rows), q_ref, 1.0 / math.sqrt(width // HEADS))
            turn(product(1, n1.shape[0]), k_ref, 1.0)
            v_ref[...] = product(2, n1.shape[0]).astype(BF16)


def attend_kernel(slots, parents, q_ref, k_ref, v_ref, e_ref, o_ref, linv_ref, k_aug, q_aug, *, n_shard, n_branch, pos_dev):
    rows, keys = q_ref.shape[0], k_ref.shape[0]
    blocks = pos_dev // BLOCK

    @pl.when(pl.program_id(0) == 0)
    def _():
        chosen, _ = chosen_pieces(slots, parents, n_shard, n_branch, pos_dev)
        shape = (pos_dev, PAIR)
        lane = lanes(shape) & 63
        block = lax.broadcasted_iota(jnp.int32, shape, 0) // BLOCK
        k_aug[:pos_dev] = jnp.where(lane - 32 == block, 1.0, 0.0).astype(BF16)
        k_aug[pos_dev : 2 * pos_dev] = jnp.where(lane == block, 1.0, 0.0).astype(BF16)
        for t, (_, valid, _) in enumerate(chosen):
            first = (2 + t) * pos_dev
            shut = jnp.where(valid > 0, 0.0, NEG)
            k_aug[first : first + pos_dev] = jnp.where(lane == 16, shut, 0.0).astype(BF16)
        for copy in range(2):
            clean = jnp.where((lane < blocks) & (lane >= block + copy), NEG, 0.0)
            noisy = (lane >= 32) & (lane < 32 + blocks)
            if copy == 0:
                noisy = noisy & (lane - 32 != block)
            out = jnp.where(noisy, NEG, clean)
            out = jnp.where(lane == 16, 1.0, out)
            q_aug[copy * pos_dev : (copy + 1) * pos_dev] = out.astype(BF16)

    low_q = lanes((rows, PAIR)) < 64
    low_k = lanes((keys, PAIR)) < 64
    q, k, v = q_ref[...], k_ref[...], v_ref[...]
    ones = jnp.ones_like(v)
    q_h = [jnp.where(low_q, q, q_aug[...]), jnp.where(low_q, q_aug[...], q)]
    k_h = [jnp.where(low_k, k, k_aug[...]), jnp.where(low_k, k_aug[...], k)]
    v_t = [jnp.where(low_k, v, ones).T, jnp.where(low_k, ones, v).T]
    chunks = [slice(c * pos_dev, (c + 1) * pos_dev) for c in range(keys // pos_dev)]

    def peak(scores):
        return functools.reduce(jnp.maximum, [jnp.max(item, axis=0, keepdims=True) for item in scores])

    def weigh(h, at, scores, top):
        e = jnp.exp(scores - top).astype(BF16)
        e_ref[h, at] = e
        return e

    scores = [[dot_t(k_h[0][at], q_h[0]) for at in chunks], []]
    weights = [[], []]
    outs = [jnp.zeros((PAIR, rows), F32) for _ in range(2)]
    top = peak(scores[0])
    for c, at in enumerate(chunks):
        scores[1].append(dot_t(k_h[1][at], q_h[1]))
        weights[0].append(weigh(0, at, scores[0][c], top))
    top = peak(scores[1])
    for c, at in enumerate(chunks):
        outs[0] = outs[0] + dot(v_t[0][:, at], weights[0][c])
        weights[1].append(weigh(1, at, scores[1][c], top))
    for c, at in enumerate(chunks):
        outs[1] = outs[1] + dot(v_t[1][:, at], weights[1][c])
    outs = [item.T for item in outs]
    total = jnp.where(low_q, pltpu.roll(outs[0], 64, 1), pltpu.roll(outs[1], 64, 1))
    inv = 1.0 / total
    linv_ref[...] = inv
    o_ref[...] = (jnp.where(low_q, outs[0], outs[1]) * inv).astype(BF16)


def ff_kernel(*refs, part, hows_o, hows, relative):
    first, last = part == 0, part == 2
    wo_refs, refs = (refs[: len(hows_o)], refs[len(hows_o) :]) if part != 1 else ((), refs)
    count = sum(2 if how == "whole" else 1 for _, how in hows)
    w_refs, refs = refs[:count], refs[count:]
    vec, bup, g_in, *refs = refs
    if first:
        x_in, att_in, mid_out, n2_out, n2t_out, attt_out, acc_out, dn2_out, *refs = refs
    elif not last:
        n2_in, n2t_in, acc_out, dn2_out, *refs = refs
    else:
        n2_in, n2t_in, *refs = refs
        parts_in, mid_in, out_out, branch_out, datt_out, small_ref, *refs = refs[:4], *refs[4:]
    bug_ref, *refs = refs
    g_refs, refs = refs[:6], refs[6:]
    wu, wd, g, gt, n2, n2t, hid, dup, acc, dn2, low, stage, w_sem, in_sem, out_sem, *refs = refs
    if first:
        wo, mid, x, att, attt = refs
    elif last:
        wo, mid, parts = refs
    rel = relative_to(relative)
    rows, width = g.shape
    quarter = width // 4
    cols = wu.shape[1] // 4
    half = quarter // 2
    out_copies = []

    def put(source, target):
        copy = pltpu.make_async_copy(source, target, out_sem.at[len(out_copies)])
        copy.start()
        out_copies.append(copy)

    def spread(ref, value):
        for j in range(4):
            at = pl.ds(pl.multiple_of(place(j ^ rel) * quarter, quarter), quarter)
            ref[at, :] = value[j * quarter : (j + 1) * quarter, :]

    o_copies = []
    for a, ref in enumerate(wo_refs):
        k, how = hows_o[a]
        at = row_block(k, rel, quarter, how)
        if how == "whole":
            o_copies.append(pltpu.make_async_copy(ref, wo.at[at], w_sem.at[0]))
        else:
            for b in range(3):
                line = 4 * half + 3 * (cols // 2) + b * half
                source = ref.at[line : line + half]
                o_copies.append(pltpu.make_async_copy(source, wo.at[at, b * cols : (b + 1) * cols], w_sem.at[0]))
    up_copies, down_copies = [], []
    at_ref = 0
    for k, how in hows:
        at = row_block(k, rel, quarter, how)
        if how == "whole":
            up_source, down_source = w_refs[at_ref], w_refs[at_ref + 1]
            at_ref += 2
        else:
            up_source = down_source = w_refs[at_ref]
            at_ref += 1
        for p in range(4):
            there = slice(p * cols, (p + 1) * cols)
            j = ORDER[p] ^ rel
            if how == "whole":
                source = up_source.at[:, pl.ds(pl.multiple_of(j * width + part * cols, cols), cols)]
            else:
                source = up_source.at[pl.ds(pl.multiple_of(j * half, half), half)]
            up_copies.append(pltpu.make_async_copy(source, wu.at[at, there], w_sem.at[1]))
        p = ORDER.index(k)
        spot, sem = p * cols, w_sem.at[2]
        if how == "whole":
            source = down_source.at[part * cols : (part + 1) * cols]
            down_copies.append(pltpu.make_async_copy(source, wd.at[spot : spot + cols], sem))
        else:
            there = pl.ds(pl.multiple_of(spot + half_of(how) * (cols // 2), cols // 2), cols // 2)
            for b in range(3):
                line = 4 * half + b * (cols // 2)
                source = down_source.at[line : line + cols // 2]
                target = wd.at[there, b * cols : (b + 1) * cols]
                down_copies.append(pltpu.make_async_copy(source, target, sem))

    if first:
        pairs = [(x_in, x), (att_in, att), (g_in, g)]
    else:
        pairs = [(n2_in, n2), (g_in, g), (n2t_in, n2t)]
    if last:
        pairs += [(mid_in, mid)] + [(ref, parts.at[i]) for i, ref in enumerate(parts_in)]
    in_copies = [pltpu.make_async_copy(a, b, in_sem.at[i]) for i, (a, b) in enumerate(pairs)]
    if first:
        starts = in_copies[:2] + o_copies + up_copies + in_copies[2:] + down_copies
    else:
        starts = in_copies[:1] + up_copies + in_copies[1:2] + down_copies + in_copies[2:3]
    starts += o_copies + in_copies[3:] if last else []
    for copy in starts:
        copy.start()

    if first:
        for copy in (*in_copies[:2], *o_copies):
            copy.wait()
        mid[...] = x[...].astype(F32) + dot(att[...], wo[...]) + vec[3:4, :width]
        put(mid, mid_out)
        n, _ = normed(mid[...])
        n2[...] = (n * vec[4:5, :width] + vec[5:6, :width]).astype(BF16)
        put(n2, n2_out)
        spread(n2t, n2[...].T)
        put(n2t, n2t_out)
        spread(attt, att[...].T)
        put(attt, attt_out)
    else:
        in_copies[0].wait()

    bias = jnp.concatenate([bup[pl.ds((k ^ rel) * 3 + part, 1), :] for k in ORDER], axis=1)
    for copy in up_copies:
        copy.wait()
    up = dot(n2[...], wu[...]) + bias
    in_copies[2 if first else 1].wait()
    for copy in down_copies:
        copy.wait()
    d_hidden = dot_t(g[...], wd[...])
    cube = 0.044715 * up * up
    th = jnp.tanh(0.7978845608028654 * (up + cube * up))
    left = 0.5 * (1.0 + th)
    hid[...] = (up * left).astype(BF16)
    slope = left + (0.5 * 0.7978845608028654) * up * (1.0 - th * th) * (1.0 + 3.0 * cube)
    d_up = d_hidden * slope
    sums = jnp.sum(d_up, axis=0, keepdims=True)
    dup[...] = d_up.astype(BF16)
    gt[...] = g[...].T
    grad_down = dot(gt[...], hid[...])
    for p in range(4):
        bug_ref[pl.ds(ORDER[p] ^ rel, 1), :] = sums[:, p * cols : (p + 1) * cols]
        for r in range(4):
            block = slice(r * quarter, (r + 1) * quarter)
            stage[p, 4 + r] = grad_down[block, p * cols : (p + 1) * cols].astype(BF16)
    put(stage.at[0, 4:8], g_refs[1])
    put(stage.at[1, 4:8], g_refs[3])
    more, d_more = dot(hid[...], wd[...]), dot_t(dup[...], wu[...])
    if last:
        acc[...] = more
        dn2[...] = d_more
    else:
        low[0] = more.astype(BF16)
        low[1] = d_more.astype(BF16)
        put(low.at[0], acc_out)
        put(low.at[1], dn2_out)
    if not first:
        in_copies[2].wait()
    grad_up = dot(n2t[...], dup[...])
    for p in range(4):
        for r in range(4):
            block = slice(r * quarter, (r + 1) * quarter)
            stage[r, ORDER[p] ^ rel] = grad_up[block, p * cols : (p + 1) * cols].astype(BF16)
    put(stage.at[0, 0:4], g_refs[0])
    put(stage.at[1, 0:4], g_refs[2])
    put(stage.at[2], g_refs[4])
    put(stage.at[3], g_refs[5])

    if last:
        for copy in (*in_copies[3:], *o_copies):
            copy.wait()
        base = mid[...]
        n, inv = normed(base)
        d = dn2[...] + parts[1].astype(F32) + parts[3].astype(F32)
        ct = g[...].astype(F32)
        branch = (ct + norm_back(d, n, inv, vec[4:5, :width])).astype(BF16)
        low[0] = branch
        put(low.at[0], branch_out)
        hid2 = dot_t(branch, wo[...])
        for a, item in enumerate((branch.astype(F32), d * n, d, ct)):
            small_ref[a : a + 1, :] = jnp.sum(item, axis=0, keepdims=True)
        low[1] = hid2.astype(BF16)
        put(low.at[1], datt_out)
        total = base + acc[...] + parts[0].astype(F32) + parts[2].astype(F32) + vec[7:8, :width]
        low[2] = total.astype(BF16)
        put(low.at[2], out_out)
    for copy in out_copies:
        copy.wait()


def attend_back_kernel(q_ref, k_ref, v_ref, do_ref, o_ref, linv_ref, e_ref, tab, n1t_in, *refs, pos_dev, group):
    if group == 0:
        attt_in, branch_in, *refs = refs
    if group == 2:
        earlier_in, refs = refs[:3], refs[3:]
    dq_ref, dk_ref, dv_ref, bias_ref, *refs = refs
    if group != 1:
        g_refs, refs = refs[:6], refs[6:]
        n1t, stage, in_sem, out_sem, *refs = refs
    if group == 0:
        attt, branch = refs
    if group == 2:
        earlier = refs
    rows, keys = q_ref.shape[0], k_ref.shape[0]
    quad = 2 * PAIR
    quarter = n1t_in.shape[0] // 4
    scale = 1.0 / 8.0
    i = pl.program_id(0)
    low_q, low_k = lanes((rows, PAIR)) < 64, lanes((keys, PAIR)) < 64
    if group != 1:
        pairs = [(n1t_in, n1t)]
        pairs += [(attt_in, attt), (branch_in, branch)] if group == 0 else list(zip(earlier_in, earlier))
        in_copies = [pltpu.make_async_copy(a, b, in_sem.at[n]) for n, (a, b) in enumerate(pairs)]

        @pl.when(i == 0)
        def _():
            for copy in in_copies:
                copy.start()

    def unturn(t, first):
        parts = []
        for n in range(t.shape[0] // pos_dev):
            at = first[n] * pos_dev
            cosine, sine = tab[at : at + pos_dev, :PAIR], tab[at : at + pos_dev, PAIR:]
            part = t[n * pos_dev : (n + 1) * pos_dev]
            parts.append(part * cosine - swap_halves(part) * sine)
        return jnp.concatenate(parts, axis=0)

    def pair(at):
        q, k, v = q_ref[...], k_ref[...], v_ref[...]
        do = do_ref[...].astype(F32) * linv_ref[...]
        product = do * o_ref[...].astype(F32)
        do_b = do.astype(BF16)
        k_t = k.T
        do_h, v_h = [], []
        for h in range(2):
            here_q, here_k = (low_q, low_k) if h == 0 else (~low_q, ~low_k)
            free = 64 * (1 - h)
            delta = -jnp.sum(jnp.where(here_q, product, 0.0), axis=1, keepdims=True)
            high = delta.astype(BF16).astype(F32)
            lane_q, lane_k = lanes((rows, PAIR)), lanes((keys, PAIR))
            extra = jnp.where(lane_q == free, high, jnp.where(lane_q == free + 1, delta - high, 0.0))
            do_h.append(jnp.where(here_q, do, extra).astype(BF16))
            ones = jnp.where((lane_k == free) | (lane_k == free + 1), 1.0, 0.0).astype(BF16)
            v_h.append(jnp.where(here_k, v, ones))
        chunks = [slice(c * pos_dev, (c + 1) * pos_dev) for c in range(keys // pos_dev)]
        d_q = [jnp.zeros((PAIR, rows), F32) for _ in range(2)]
        d_k, d_v = [[], []], [[], []]
        steps = [(c, h) for c in chunks for h in range(2)]
        d_probs = dot_t(v_h[0][chunks[0]], do_h[0])
        for n, (c, h) in enumerate(steps):
            if n + 1 < len(steps):
                c_next, h_next = steps[n + 1]
                coming = dot_t(v_h[h_next][c_next], do_h[h_next])
            e = e_ref[h, c]
            d_scores = (d_probs * e.astype(F32)).astype(BF16)
            d_v[h].append(dot(e, do_b))
            d_k[h].append(dot(d_scores, q))
            d_q[h] = d_q[h] + dot(k_t[:, c], d_scores)
            d_probs = coming
        d_k, d_v = ([jnp.concatenate(item, axis=0) for item in both] for both in (d_k, d_v))
        d_q = [item.T for item in d_q]
        dv = jnp.where(low_k, d_v[0], d_v[1])
        dk = unturn(jnp.where(low_k, d_k[0], d_k[1]), [0, 0] + list(range(1, keys // pos_dev - 1)))
        dq = unturn(jnp.where(low_q, d_q[0], d_q[1]) * scale, [0, 0])
        dv_ref[:, at] = dv.astype(BF16)
        dk_ref[:, at] = dk.astype(BF16)
        dq_ref[:, at] = dq.astype(BF16)

    for a in range(2):

        @pl.when(i == a)
        def _(a=a):
            pair(slice(a * PAIR, (a + 1) * PAIR))

    def put(unit, grad):
        for r in range(4):
            stage[r, unit] = grad[r * quarter : (r + 1) * quarter].astype(BF16)

    if group == 0:

        @pl.when(i == 0)
        def _():
            in_copies[1].wait()
            in_copies[2].wait()
            for b in range(3):
                put(3 + b, dot(attt[...], branch[:, b * quad : (b + 1) * quad]))

    @pl.when(i == 1)
    def _():
        mine = (dq_ref, dk_ref, dv_ref)
        for a, ref in enumerate(mine):
            bias_ref[a : a + 1, :] = jnp.sum(ref[...].astype(F32), axis=0, keepdims=True)
        if group == 1:
            return
        in_copies[0].wait()
        if group == 2:
            for a, ref in enumerate(earlier):
                in_copies[1 + a].wait()
                put(a, dot(n1t[:, : ref.shape[0]], ref[...]))
        for a, ref in enumerate(mine):
            put(a + (3 if group == 2 else 0), dot(n1t[:, : ref.shape[0]], ref[...]))
        sources = [stage.at[r, u : u + 3] for r in range(2) for u in (0, 3)] + [stage.at[2], stage.at[3]]
        copies = [pltpu.make_async_copy(a, b, out_sem.at[n]) for n, (a, b) in enumerate(zip(sources, g_refs))]
        for copy in copies:
            copy.start()
        for copy in copies:
            copy.wait()


def input_back_kernel(slots, parents, x_ref, xr_ref, *refs, n_shard, n_branch, pos_dev, relative, hows):
    grads, refs = refs[:9], refs[9:]
    w_refs, refs = refs[: len(hows)], refs[len(hows) :]
    vec, dn1_ref, small_ref, *refs = refs
    outs, (w, d_in, acc, w_sem, d_sem) = refs[: 3 if relative else 1], refs[3 if relative else 1 :]
    rel = relative_to(relative)
    width = x_ref.shape[-1]
    quarter = width // 4
    quad = 2 * PAIR
    rows, keys = dn1_ref.shape[0], acc.shape[0]
    chosen, _ = chosen_pieces(slots, parents, n_shard, n_branch, pos_dev)

    def copies(a):
        out = []
        for ref, (k, how) in zip(w_refs, hows):
            source = ref.at[:, a * width : (a + 1) * width]
            out.append(pltpu.make_async_copy(source, w.at[a, row_block(k, rel, quarter, how)], w_sem.at[a]))
        n = rows if a == 0 else keys
        for g in range(3):
            target = d_in.at[a, 0:n, g * quad : (g + 1) * quad]
            out.append(pltpu.make_async_copy(grads[3 * a + g], target, d_sem.at[a]))
        return out

    for a in (1, 2, 0):
        for copy in copies(a):
            copy.start()
    for a in (1, 2, 0):
        for copy in copies(a):
            copy.wait()
        n = rows if a == 0 else keys
        more = dot_t(d_in[a, :n], w[a])
        if a == 1:
            acc[...] = more
        else:
            acc[:n] = acc[:n] + more
    total, plain = jnp.zeros((1, width), F32), jnp.zeros((1, width), F32)
    for t in range(keys // pos_dev):
        d = acc[t * pos_dev : (t + 1) * pos_dev]
        x = x_ref[t] if t < 2 else xr_ref[(t - 2) * pos_dev : (t - 1) * pos_dev]
        n, _ = normed(x.astype(F32))
        total = total + jnp.sum(d * n, axis=0, keepdims=True)
        plain = plain + jnp.sum(d, axis=0, keepdims=True)
        if t < 2:
            dn1_ref[t * pos_dev : (t + 1) * pos_dev] = d
    small_ref[0:1, :] = total
    small_ref[1:2, :] = plain
    if relative:
        parts = [acc[(2 + t) * pos_dev : (3 + t) * pos_dev] for t in range(len(chosen))]
        for k, ref in zip((3, 1, 2), outs):
            ref[...] = sum(
                jnp.where(holder ^ rel == k, 1.0, 0.0) * part for (holder, _, _), part in zip(chosen, parts)
            ).astype(BF16)
    else:
        outs[0][...] = jnp.zeros_like(outs[0])
        for t, (holder, _, _) in enumerate(chosen):
            part = acc[(2 + t) * pos_dev : (3 + t) * pos_dev]
            outs[0][holder] = (outs[0][holder].astype(F32) + part).astype(BF16)


def final_kernel(x_ref, branch_ref, dn1_ref, got_ref, vec, out_ref):
    i = pl.program_id(0)
    d = dn1_ref[...] + jnp.where(i == 1, 1.0, 0.0) * got_ref[...].astype(F32)
    n, inv = normed(x_ref[0].astype(F32))
    back = norm_back(d, n, inv, vec[0:1, : d.shape[1]])
    out_ref[0] = (branch_ref[...].astype(F32) + back).astype(BF16)


def swap(x, axis, bit):
    n = lax.axis_size(axis)
    return lax.ppermute(x, axis, [(i, i ^ bit) for i in range(n)])


def core(x):
    return swap(x, "shard", 1)


def across(x):
    return swap(x, "shard", 2)


def tie(x, *others):
    return lax.optimization_barrier((x, *others))[0]


def select_bit(bit, a, b):
    return jnp.where(bit == 1, b, a)


class Reduction:
    def __init__(self, chunk):
        *send, self.two, self.zero = chunk
        self.got = [core(item) for item in send]
        self.step = 0
        self.joined = None

    def join(self, other):
        assert self.step == other.step == 1
        self.joined = other

    def go(self, *after):
        got = tie(self.got, *after)
        r = lax.axis_index("rep")
        if self.step == 0:
            self.part = self.two + jnp.concatenate(got[:2], axis=0)
            self.kept = self.zero + jnp.concatenate(got[2:], axis=0)
            self.got = across(self.part)
        elif self.step in (1, 2):
            bit = self.step
            total = self.kept + got
            if self.step == 1 and self.joined:
                total = jnp.concatenate([total, self.joined.kept + tie(self.joined.got, got)], axis=0)
            size = total.shape[1] // 2
            here = (r // bit) & 1
            self.kept = lax.dynamic_slice_in_dim(total, here * size, size, 1)
            self.part = lax.dynamic_slice_in_dim(total, (1 - here) * size, size, 1)
            self.got = swap(self.part, "rep", bit)
        elif self.step == 3:
            self.part = self.kept + got
            self.got = swap(self.part, "rep", 4)
        elif self.step == 4:
            self.part = self.part + got
            self.got = swap(self.part, "rep", 2)
        else:
            here = (r // 2) & 1
            self.part = jnp.concatenate(
                [select_bit(here, self.part, got), select_bit(here, got, self.part)], axis=1
            )
            self.got = swap(self.part, "rep", 1)
        self.step += 1
        return self.part


class SmallSum:
    LINKS = (("shard", 1), ("shard", 2), ("rep", 1), ("rep", 2), ("rep", 4))

    def __init__(self, x):
        self.part, self.step = x, 0
        self.got = swap(x, *self.LINKS[0])

    def go(self, *after):
        self.part = self.part + tie(self.got, *after)
        self.step += 1
        if self.step < 5:
            self.got = swap(self.part, *self.LINKS[self.step])
        return self.part


class FarGrad:
    def __init__(self, three, one, two):
        self.two, self.got, self.step = two, [core(three), core(one)], 0

    def go(self, *after):
        got = tie(self.got, *after)
        if self.step == 0:
            self.own = got[1]
            self.part = self.two + got[0]
            self.got = across(self.part)
        else:
            self.part = self.own + got
        self.step += 1
        return self.part


def collect_kernel(*refs, quarter):
    parts, (up_ref, down_ref, whole_ref) = refs[:4], refs[4:]
    half = quarter // 2
    y = lax.axis_index("rep") & 1
    cols = parts[0].shape[2]
    for p in range(3):
        pair, unit = (0, 8 * p) if p < 2 else (2, 0)
        for which in range(2):
            at = pl.ds(pl.multiple_of((y if which == 0 else 1 - y) * half, half), half)
            ref = parts[pair + which]
            for j in range(4):
                first = j * 3 * cols + p * cols
                up_ref[at, first : first + cols] = ref[unit + j].astype(F32)
                whole_ref[j, at, :] = ref[unit + 4 + j].astype(F32)
        down_ref[p * cols : (p + 1) * cols, :] = whole_ref[...].reshape(4 * quarter, cols).T


def collect_qkv_kernel(*refs, quarter):
    parts, (out_ref, qkv_ref) = refs[:4], refs[4:]
    half = quarter // 2
    y = lax.axis_index("rep") & 1
    cols = parts[0].shape[2]
    for which in range(2):
        at = pl.ds(pl.multiple_of((y if which == 0 else 1 - y) * half, half), half)
        first, second = parts[which], parts[2 + which]
        for b in range(3):
            out_ref[at, b * cols : (b + 1) * cols] = first[3 + b].astype(F32)
        for a in range(3):
            for g, block in enumerate((first[a], second[a], second[3 + a])):
                qkv_ref[at, (3 * a + g) * cols : (3 * a + g + 1) * cols] = block.astype(F32)


def shards(
    states,
    cotangent,
    norm1_gain,
    norm1_bias,
    qkv_weight,
    qkv_bias,
    out_weight,
    out_bias,
    norm2_gain,
    norm2_bias,
    up_weight,
    up_bias,
    down_weight,
    down_bias,
    slots,
    parents,
):
    n_shard = lax.axis_size("shard")
    n_branch = n_shard // 4
    pos_dev, width = states.shape[1], states.shape[2]
    ff = up_weight.shape[1]
    rows = 2 * pos_dev
    n_far = n_branch + 1
    keys = rows + n_far * pos_dev
    relative = n_shard == 4 and lax.axis_size("rep") == 8
    quarter = width // 4
    cols = ff // 12
    quad = 2 * PAIR
    me = lax.axis_index("shard")
    sizes = dict(n_shard=n_shard, n_branch=n_branch, pos_dev=pos_dev)
    bound = functools.partial
    shape = jax.ShapeDtypeStruct
    vectors = (norm1_gain, norm1_bias, qkv_bias, out_bias, norm2_gain, norm2_bias, up_bias, down_bias)

    freq = jnp.exp(-jnp.log(10000.0) * jnp.arange(32, dtype=F32) / 32)
    freq = jnp.tile(freq, 4).reshape(1, PAIR)
    table = pl.pallas_call(
        bound(table_kernel, **sizes),
        out_shape=shape(((1 + n_far) * pos_dev, 2 * PAIR), F32),
        grid=(1,),
        in_specs=[SMEM, SMEM, whole((1, PAIR))],
        out_specs=whole(((1 + n_far) * pos_dev, 2 * PAIR)),
        compiler_params=params(),
        cost_estimate=cost(3.5),
        name="rotary_table",
    )(slots, parents, freq)

    natural = [(k, "whole") for k in range(4)]
    if relative:
        half = quarter // 2
        rest = 4 * half + 3 * (cols // 2)
        pack_shapes = [
            shape((pos_dev + 16, width), BF16),
            shape((rest + 3 * half, cols), BF16),
            shape((rest, cols), BF16),
            shape((rest, cols), BF16),
        ]
        packed = pl.pallas_call(
            bound(pack_kernel, quarter=quarter, width=width, cols=cols),
            out_shape=pack_shapes,
            grid=(1,),
            in_specs=[whole(item.shape) for item in vectors] + [ANY] * 4,
            out_specs=[whole(item.shape) for item in pack_shapes],
            scratch_shapes=[pltpu.VMEM((16, width), F32), pltpu.SemaphoreType.DMA((32,))],
            compiler_params=params(),
            cost_estimate=cost(2),
            name="pack",
        )
        q_two = across(qkv_weight)
        q_one = core(qkv_weight)
        x_own, *b_half = packed(*vectors, states, out_weight, up_weight, down_weight)
        x_one = core(x_own)
        x_two = across(x_own)
        x_two, _ = lax.optimization_barrier((x_two, table))
        x_far = [x_own, x_one, x_two, core(x_two)]
        w_qkv = [qkv_weight, q_one, q_two, core(q_two)]
        how_qkv = natural
        how_out = [(0, "whole"), (1, "whole"), (2, "direct"), (2, "via"), (3, "direct"), (3, "via")]
        o_one, u_one, d_one = core(out_weight), core(up_weight), core(down_weight)
        b_two = [across(tie(b_half[0], x_two, q_two))]
        vec, b_up = pl.pallas_call(
            bound(unpack_kernel, sizes=[item.shape[0] for item in vectors], pos_dev=pos_dev, cols=cols),
            out_shape=[shape((8, ff), F32), shape((12, cols), F32)],
            grid=(1,),
            in_specs=[ANY] * 4,
            out_specs=[whole((8, ff)), whole((12, cols))],
            scratch_shapes=[pltpu.VMEM((4, 16, width), BF16), pltpu.SemaphoreType.DMA((4,))],
            compiler_params=params(),
            cost_estimate=cost(2),
            name="unpack",
        )(*x_far)
    else:
        gather = lambda item: lax.all_gather(item, "shard", axis=0, tiled=True)
        rows_of = lambda item: [item[j * quarter : (j + 1) * quarter] for j in range(4)]
        w_qkv, how_qkv = rows_of(gather(qkv_weight)), natural
        x_far = [gather(states[1][None])]
        w_out, how_out = rows_of(gather(out_weight)), natural
        ups, downs = rows_of(gather(up_weight)), gather(down_weight)
        pieces = []
        for k in range(4):
            pieces += [ups[k], downs[k * width : (k + 1) * width]]
        w_ff, how_ff = [pieces] * 3, natural
        small = lax.all_gather(jnp.concatenate(vectors), "shard", axis=0)
        lines, at = [], 0
        for item in vectors:
            n = item.shape[0]
            line = small[:, at : at + n].reshape(1, n_shard * n).astype(F32)
            lines.append(jnp.pad(line, ((0, 0), (0, ff - n_shard * n))))
            at += n
        vec = jnp.concatenate(lines, axis=0)
        b_up = vec[6].reshape(12, cols)

    each = lambda i: (i, 0)
    n1t, q, k, v, x_seen = pl.pallas_call(
        bound(qkv_kernel, n_far=len(x_far), hows=how_qkv, relative=relative, **sizes),
        out_shape=[
            shape((width, keys), BF16),
            shape((rows, width), BF16),
            shape((keys, width), BF16),
            shape((keys, width), BF16),
            shape((n_far * pos_dev, width), BF16),
        ],
        grid=(3,),
        in_specs=[SMEM, SMEM, whole((2, pos_dev, width))]
        + [ANY] * (len(x_far) + len(how_qkv))
        + [whole((8, ff)), whole(((1 + n_far) * pos_dev, 2 * PAIR))],
        out_specs=[
            whole((width, keys)),
            pl.BlockSpec((rows, quad), lambda i: (0, i)),
            pl.BlockSpec((keys, quad), lambda i: (0, i)),
            pl.BlockSpec((keys, quad), lambda i: (0, i)),
            whole((n_far * pos_dev, width)),
        ],
        scratch_shapes=[
            pltpu.VMEM((3, width, 3 * quad), BF16),
            pltpu.VMEM((keys, width), BF16),
            pltpu.SemaphoreType.DMA((3,)),
            pltpu.SemaphoreType.DMA((n_far,)),
        ],
        compiler_params=params(),
        cost_estimate=cost(11),
        name="norm_qkv",
    )(slots, parents, states, *x_far, *w_qkv, vec, table)

    if relative:
        b_two[0] = tie(b_two[0], q)
        b_two += [across(tie(b_half[p], b_two[0])) for p in (1, 2)]
        b_via = [swap(b_two[0], "rep", 1)]
        b_three = [core(b_two[0])]

    pair = lambda i: (0, i)
    n_pair = width // PAIR
    e, attended, linv = pl.pallas_call(
        bound(attend_kernel, **sizes),
        out_shape=[
            shape((HEADS, keys, rows), BF16),
            shape((rows, width), BF16),
            shape((rows, width), F32),
        ],
        grid=(n_pair,),
        in_specs=[
            SMEM,
            SMEM,
            pl.BlockSpec((rows, PAIR), pair),
            pl.BlockSpec((keys, PAIR), pair),
            pl.BlockSpec((keys, PAIR), pair),
        ],
        out_specs=[
            pl.BlockSpec((2, keys, rows), lambda i: (i, 0, 0)),
            pl.BlockSpec((rows, PAIR), pair),
            pl.BlockSpec((rows, PAIR), pair),
        ],
        scratch_shapes=[pltpu.VMEM((keys, PAIR), BF16), pltpu.VMEM((rows, PAIR), BF16)],
        compiler_params=params(),
        cost_estimate=cost(17),
        name="attend",
    )(slots, parents, tie(q, b_two[0]) if relative else q, k, v)

    if relative:
        b_last = [core(tie(b_via[0], attended))]
        b_two[1:] = [tie(item, attended) for item in b_two[1:]]
        b_via += [swap(item, "rep", 1) for item in b_two[1:]]
        b_three += [core(item) for item in b_two[1:]]
        attended = tie(attended, b_last[0], *b_two[1:])
        w_out = [out_weight, o_one, b_two[0], b_via[0], b_three[0], b_last[0]]
        how_ff = how_out
        w_ff = [[up_weight, down_weight, u_one, d_one, b_two[0], b_via[0], b_three[0], b_last[0]]]

    x_rows = states.reshape(rows, width)
    g_rows = cotangent.reshape(rows, width)
    wide, low, turned = shape((rows, width), F32), shape((rows, width), BF16), shape((width, rows), BF16)

    def feed(part, ins, outs, scratch, vmem_out=()):
        weights = ([] if part == 1 else w_out) + w_ff[part]
        vm = lambda item: pltpu.VMEM(item.shape, item.dtype)
        outs = outs + list(vmem_out) + [shape((4, cols), F32)]
        grads = [shape((4, quarter, cols), BF16)] * 4 + [shape((8, quarter, cols), BF16)] * 2
        n_any = len(outs) - len(vmem_out) - 1
        result = pl.pallas_call(
            bound(ff_kernel, part=part, hows_o=how_out, hows=how_ff, relative=relative),
            out_shape=outs + grads,
            grid=(1,),
            in_specs=[ANY] * len(weights) + [whole((8, ff)), whole((12, cols))] + [ANY] * (1 + len(ins)),
            out_specs=[ANY] * n_any + [whole(item.shape) for item in outs[n_any:]] + [ANY] * 6,
            scratch_shapes=[
                pltpu.VMEM((width, 4 * cols), BF16),
                pltpu.VMEM((4 * cols, width), BF16),
                vm(low),
                vm(turned),
                vm(low),
                vm(turned),
                pltpu.VMEM((rows, 4 * cols), BF16),
                pltpu.VMEM((rows, 4 * cols), BF16),
                vm(wide),
                vm(wide),
                pltpu.VMEM((3, rows, width), BF16),
                pltpu.VMEM((4, 8, quarter, cols), BF16),
                pltpu.SemaphoreType.DMA((3,)),
                pltpu.SemaphoreType.DMA((8,)),
                pltpu.SemaphoreType.DMA((12,)),
            ]
            + scratch,
            compiler_params=params(),
            cost_estimate=cost(13),
            name=("feed_first", "feed_second", "feed_third")[part],
        )(*weights, vec, b_up, g_rows, *ins)
        return result[:-6], result[-6:]

    square = pltpu.VMEM((width, width), BF16)
    (mid, n2, n2t, attt, *parts, bug0), chunk0 = feed(
        0, (x_rows, attended), [wide, low, turned, turned, low, low],
        [square, pltpu.VMEM((rows, width), F32)] + [pltpu.VMEM((rows, width), BF16)] * 2 + [pltpu.VMEM((width, rows), BF16)],
    )
    if relative:
        sum0 = Reduction(chunk0)
        b_via[1:] = [tie(item, bug0) for item in b_via[1:]]
        b_last += [core(item) for item in b_via[1:]]
        w_ff += [
            [up_weight, down_weight, u_one, d_one, b_two[p], b_via[p], b_three[p], b_last[p]] for p in (1, 2)
        ]
        n2 = tie(n2, sum0.go(*b_via[1:]))
    (*more, bug1), chunk1 = feed(1, (n2, n2t), [low, low], [])
    if relative:
        sum1 = Reduction(chunk1)
        sum0.got = tie(sum0.got, bug1)
        n2 = tie(n2, sum1.go(bug1))
        n2, sum0.got = lax.optimization_barrier((n2, sum0.got))
        sum0.join(sum1)
    (output, branch, d_att, small2, bug2), chunk2 = feed(
        2, (n2, n2t, *parts, *more, mid), [low, low, low],
        [square, pltpu.VMEM((rows, width), F32), pltpu.VMEM((4, rows, width), BF16)], [shape((8, width), F32)],
    )
    if relative:
        sum2 = Reduction(chunk2)

    def back(g, d_att, *more):
        here = lambda i: (0, 2 * g + i)
        grads = [] if g == 1 else [shape((3, quarter, quad), BF16)] * 4 + [shape((6, quarter, quad), BF16)] * 2
        outs = [shape((n, quad), t) for n, t in ((rows, BF16), (keys, BF16), (keys, BF16), (8, F32))]
        scratch = []
        if g != 1:
            scratch = [
                pltpu.VMEM((width, keys), BF16),
                pltpu.VMEM((4, 6, quarter, quad), BF16),
                pltpu.SemaphoreType.DMA((4,)),
                pltpu.SemaphoreType.DMA((6,)),
            ] + [pltpu.VMEM(item.shape, item.dtype) for item in more]
        return pl.pallas_call(
            bound(attend_back_kernel, pos_dev=pos_dev, group=g),
            out_shape=outs + grads,
            grid=(2,),
            in_specs=[
                pl.BlockSpec((rows, PAIR), here),
                pl.BlockSpec((keys, PAIR), here),
                pl.BlockSpec((keys, PAIR), here),
                pl.BlockSpec((rows, PAIR), here),
                pl.BlockSpec((rows, PAIR), here),
                pl.BlockSpec((rows, PAIR), here),
                pl.BlockSpec((2, keys, rows), lambda i: (2 * g + i, 0, 0)),
                whole(((1 + n_far) * pos_dev, 2 * PAIR)),
                ANY,
            ]
            + [ANY] * len(more),
            out_specs=[whole(item.shape) for item in outs] + [ANY] * len(grads),
            scratch_shapes=scratch,
            compiler_params=params(),
            cost_estimate=cost(11),
            name=f"attend_back_{g}",
        )(q, k, v, d_att, attended, linv, e, table, n1t, *more)

    def turns(last, *items):
        for item in items:
            last = item.go(last)
        return last

    backs = []
    for g in range(3):
        if relative:
            if g == 0:
                last = turns(small2, sum0, sum2)
            elif g == 1:
                last = turns(backs[0][3], sum0, sum2, sum3)
            else:
                last = turns(backs[1][3], sum0, sum2, sum3)
            d_att = tie(d_att, last)
        backs.append(back(g, d_att, *((attt, branch), (), tuple(backs[1][:3]) if g == 2 else ())[g]))
        if relative and g == 0:
            sum3 = Reduction(backs[0][4:])
        if relative and g == 2:
            sum4 = Reduction(backs[2][4:])
    d_all = [backs[g][a] for a in range(3) for g in range(3)]
    small_qkv = jnp.concatenate([item[3][:3] for item in backs], axis=1)
    if relative:
        last = turns(backs[2][3], sum0, sum2, sum3, sum4)
        d_all[0] = tie(d_all[0], last)

    far_shapes = (
        [shape((pos_dev, width), BF16)] * 3
        if relative
        else [shape((n_shard, pos_dev, width), BF16)]
    )
    dn1, small1, *far = pl.pallas_call(
        bound(input_back_kernel, relative=relative, hows=how_qkv, **sizes),
        out_shape=[shape((rows, width), F32), shape((8, width), F32), *far_shapes],
        grid=(1,),
        in_specs=[SMEM, SMEM, whole((2, pos_dev, width)), whole((n_far * pos_dev, width))]
        + [ANY] * (9 + len(how_qkv))
        + [whole((8, ff))],
        out_specs=[whole((rows, width)), whole((8, width))] + [whole(item.shape) for item in far_shapes],
        scratch_shapes=[
            pltpu.VMEM((3, width, width), BF16),
            pltpu.VMEM((3, keys, width), BF16),
            pltpu.VMEM((keys, width), F32),
            pltpu.SemaphoreType.DMA((3,)),
            pltpu.SemaphoreType.DMA((3,)),
        ],
        compiler_params=params(),
        cost_estimate=cost(10),
        name="input_back",
    )(slots, parents, states, x_seen, *d_all, *w_qkv, vec)

    collect = pl.pallas_call(
        bound(collect_kernel, quarter=quarter),
        out_shape=[shape((quarter, ff), F32), shape((ff // 4, width), F32)],
        scratch_shapes=[pltpu.VMEM((4, quarter, cols), F32)],
        compiler_params=params(),
        cost_estimate=cost(4),
        name="collect",
    )
    vectors_grad = jnp.concatenate([small1[:2], small_qkv, small2[:4], jnp.concatenate([bug0, bug1, bug2], axis=1)], axis=0)
    if relative:
        far_sum = FarGrad(*far)
        small_sum = SmallSum(vectors_grad)
        order = [
            sum2, sum3, sum4, far_sum, small_sum, small_sum, sum0, sum4, small_sum, sum2, sum3, sum4, small_sum, sum3,
            sum4, far_sum, sum4, small_sum, None,
        ]
        last = small1
        for item in order:
            if item is None:
                halves = [half for part in (sum0, sum2) for half in (part.part, part.got)]
                grad_up, grad_down = collect(tie(halves[0], last), *halves[1:])
                last = grad_down
            else:
                last = item.go(last)
        counts = [item.step for item in (sum0, sum2, sum3, sum4)]
        assert counts == [6] * 4, counts
        got, total = far_sum.part, small_sum.part
    else:
        got = lax.psum_scatter(far[0], "shard", scatter_dimension=0)
        total = lax.psum(vectors_grad, ("rep", "shard"))
    states_grad = pl.pallas_call(
        final_kernel,
        out_shape=shape((2, pos_dev, width), BF16),
        grid=(2,),
        in_specs=[
            pl.BlockSpec((1, pos_dev, width), lambda i: (i, 0, 0)),
            pl.BlockSpec((pos_dev, width), each),
            pl.BlockSpec((pos_dev, width), each),
            whole((pos_dev, width)),
            whole((8, ff)),
        ],
        out_specs=pl.BlockSpec((1, pos_dev, width), lambda i: (i, 0, 0)),
        compiler_params=params(),
        cost_estimate=cost(4),
        name="states_back",
    )(states, branch, dn1, got, vec)

    def up_of(parts):
        return jnp.stack([item[:4] for item in parts]).transpose(2, 1, 0, 3).reshape(-1, ff)

    def down_of(parts):
        return jnp.stack([item[4:8] for item in parts]).transpose(0, 3, 1, 2).reshape(3, -1, width)

    def out_of(part):
        return part[3:].transpose(1, 0, 2).reshape(-1, width)

    def qkv_of(parts):
        return jnp.stack(parts).transpose(2, 1, 0, 3).reshape(-1, 3 * width)

    if relative:
        grad_out, grad_qkv = pl.pallas_call(
            bound(collect_qkv_kernel, quarter=quarter),
            out_shape=[shape((quarter, width), F32), shape((quarter, 3 * width), F32)],
            compiler_params=params(),
            cost_estimate=cost(2),
            name="collect_qkv",
        )(sum3.part, sum3.got, sum4.part, sum4.got)
    else:

        def natural_order(chunk):
            *send, two, zero = chunk
            return [zero, jnp.concatenate(send[2:]), two, jnp.concatenate(send[:2])]

        parts = list(zip(*(natural_order(chunk) for chunk in (chunk0, chunk1, chunk2))))
        quads = list(zip(natural_order(backs[0][4:]), natural_order(backs[2][4:])))
        ups = jnp.concatenate([up_of(item) for item in parts], axis=0)
        downs = jnp.concatenate([down_of(item).reshape(-1, width) for item in parts], axis=0)
        outs = jnp.concatenate([out_of(item[0]) for item in quads], axis=0)
        qkvs = jnp.concatenate([qkv_of((a[:3], b[:3], b[3:])) for a, b in quads], axis=0)

        def reduced(item):
            part = lax.psum_scatter(item, "shard", scatter_dimension=0, tiled=True)
            return lax.psum(part, "rep").astype(F32)

        grad_up, grad_down, grad_out, grad_qkv = (reduced(item) for item in (ups, downs, outs, qkvs))

    def own_rows(first, count):
        line = total[first : first + count].reshape(-1)
        n = line.shape[0] // n_shard
        return lax.dynamic_slice_in_dim(line, me * n, n)

    return (
        output.reshape(2, pos_dev, width),
        states_grad,
        own_rows(0, 1),
        own_rows(1, 1),
        grad_qkv,
        own_rows(2, 3),
        grad_out,
        own_rows(5, 1),
        own_rows(6, 1),
        own_rows(7, 1),
        grad_up,
        own_rows(9, 4),
        grad_down,
        own_rows(8, 1),
    )


def solution(mesh):
    in_specs = (
        P(None, ("rep", "shard"), None),
        P(None, ("rep", "shard"), None),
        P("shard"),
        P("shard"),
        P("shard", None),
        P("shard"),
        P("shard", None),
        P("shard"),
        P("shard"),
        P("shard"),
        P("shard", None),
        P("shard"),
        P("shard", None),
        P("shard"),
        P("rep", None),
        P("rep", None),
    )
    out_specs = (
        P(None, ("rep", "shard"), None),
        P(None, ("rep", "shard"), None),
        P("shard"),
        P("shard"),
        P("shard", None),
        P("shard"),
        P("shard", None),
        P("shard"),
        P("shard"),
        P("shard"),
        P("shard", None),
        P("shard"),
        P("shard", None),
        P("shard"),
    )
    return jax.shard_map(shards, mesh=mesh, in_specs=in_specs, out_specs=out_specs, check_vma=False)
```

```python
import functools
import math

import jax
import jax.numpy as jnp
from jax import lax
from jax.experimental import pallas as pl
from jax.experimental.pallas import tpu as pltpu
from jax.sharding import PartitionSpec as P

HEADS = 12
BLOCK = 16
NEG = -1e30
PAIR = 128
F32 = jnp.float32
BF16 = jnp.bfloat16
ANY = pl.BlockSpec(memory_space=pltpu.HBM)


SMEM = pl.BlockSpec(memory_space=pltpu.SMEM)


def params(mib=58):
    return pltpu.CompilerParams(vmem_limit_bytes=mib * 2**20)


def cost(us):
    return pl.CostEstimate(flops=int(us * 1.15e9), bytes_accessed=0, transcendentals=0)


def whole(shape):
    return pl.BlockSpec(shape, lambda *_: (0,) * len(shape))


def place(rel):
    return jnp.where(rel == 3, 0, jnp.where(rel == 0, 3, rel))


ORDER = (3, 1, 2, 0)


def dot(a, b):
    return lax.dot_general(a, b, (((1,), (0,)), ((), ())), preferred_element_type=F32)


def dot_t(a, b):
    return lax.dot_general(a, b, (((1,), (1,)), ((), ())), preferred_element_type=F32)


def t_dot(a, b):
    return lax.dot_general(a, b, (((0,), (0,)), ((), ())), preferred_element_type=F32)


def normed(x):
    spread = x - jnp.mean(x, axis=-1, keepdims=True)
    inv = lax.rsqrt(jnp.mean(spread * spread, axis=-1, keepdims=True) + 1e-05)
    return spread * inv, inv


def norm_back(d, n, inv, gain):
    e = d * gain
    return inv * (
        e - jnp.mean(e, axis=-1, keepdims=True) - n * jnp.mean(e * n, axis=-1, keepdims=True)
    )


def lanes(shape):
    return lax.broadcasted_iota(jnp.int32, shape, len(shape) - 1)


def swap_halves(t):
    return jnp.where((lanes(t.shape) & 63) < 32, pltpu.roll(t, 96, 1), pltpu.roll(t, 32, 1))

def chosen_pieces(slots, parents, n_shard, n_branch, pos_dev):
    me = lax.axis_index("shard")
    mine = slots[0, me]
    seg = jnp.where(mine < n_branch, 0, mine - n_branch + 1)
    parent = parents[0, seg]

    def holder(piece):
        found = me
        for j in range(n_shard):
            found = jnp.where(slots[0, j] == piece, j, found)
        return found

    out = []
    for run in range(n_branch):
        valid = jnp.where(seg > 0, 1, jnp.where(mine > run, 1, 0))
        out.append((holder(run), valid, run * pos_dev))
    has = jnp.where(parent > 0, 1, 0)
    out.append((holder(jnp.where(parent > 0, n_branch + parent - 1, -1)), has, n_branch * pos_dev))
    start = jnp.where(
        mine < n_branch,
        mine * pos_dev,
        jnp.where(mine < 2 * n_branch, n_branch * pos_dev, (n_branch + 1) * pos_dev),
    )
    return out, start


def relative_to(relative):
    return lax.axis_index("shard") if relative else jnp.zeros((), jnp.int32)


def half_of(how):
    y = lax.axis_index("rep") & 1
    return y if how == "direct" else 1 - y


def row_block(k, rel, quarter, how, chunk=None):
    first = (k ^ rel) * quarter
    if how == "whole":
        return pl.ds(pl.multiple_of(first, 16), quarter)
    first = first + half_of(how) * (quarter // 2)
    if chunk is None:
        return pl.ds(pl.multiple_of(first, 16), quarter // 2)
    return pl.ds(pl.multiple_of(first + chunk * (quarter // 4), 16), quarter // 4)


def pack_kernel(*refs, quarter, width, cols):
    vectors, refs = refs[:8], refs[8:]
    states, w_out, w_up, w_down, s_out, *refs = refs
    b_outs, (small, sem) = refs[:3], refs[3:]
    half = quarter // 2
    y = lax.axis_index("rep") & 1
    at = pl.ds(pl.multiple_of(y * half, half), half)
    pos_dev = states.shape[1]
    copies = [(states.at[1], s_out.at[0:pos_dev])]
    for p in range(3):
        for j in range(4):
            source = w_up.at[at, j * width + p * cols : j * width + (p + 1) * cols]
            copies.append((source, b_outs[p].at[j * half : (j + 1) * half]))
        rows = pl.ds(pl.multiple_of(p * cols + y * (cols // 2), cols // 2), cols // 2)
        for b in range(3):
            first = 4 * half + b * (cols // 2)
            copies.append((w_down.at[rows, b * cols : (b + 1) * cols], b_outs[p].at[first : first + cols // 2]))
    for b in range(3):
        first = 4 * half + 3 * (cols // 2) + b * half
        copies.append((w_out.at[at, b * cols : (b + 1) * cols], b_outs[0].at[first : first + half]))
    copies = [pltpu.make_async_copy(a, b, sem.at[i]) for i, (a, b) in enumerate(copies)]
    for copy in copies:
        copy.start()
    small[...] = jnp.zeros_like(small)
    for r, ref in enumerate(vectors):
        small[r : r + 1, : ref.shape[0]] = ref[...].astype(F32).reshape(1, -1)
    s_out[pos_dev:, :] = small[...].astype(BF16)
    for copy in copies:
        copy.wait()


def unpack_kernel(a, b, c, d, vec_ref, up_ref, held, sem, *, sizes, pos_dev, cols):
    rel = lax.axis_index("shard")
    copies = [
        pltpu.make_async_copy(ref.at[pos_dev : pos_dev + 16], held.at[k ^ rel], sem.at[k])
        for k, ref in enumerate((a, b, c, d))
    ]
    for copy in copies:
        copy.start()
    for copy in copies:
        copy.wait()
    for j in range(4):
        part = held[j].astype(F32)
        for r, size in enumerate(sizes):
            vec_ref[r : r + 1, j * size : (j + 1) * size] = part[r : r + 1, :size]
        for p in range(3):
            up_ref[j * 3 + p : j * 3 + p + 1, :] = part[6:7, p * cols : (p + 1) * cols]


def table_kernel(slots, parents, freq_ref, out_ref, *, n_shard, n_branch, pos_dev):
    out, start = chosen_pieces(slots, parents, n_shard, n_branch, pos_dev)
    starts = [start] + [item[2] for item in out]
    shape = (pos_dev, PAIR)
    sign = jnp.where((lanes(shape) & 63) < 32, -1.0, 1.0)
    for i, first in enumerate(starts):
        pos = (lax.broadcasted_iota(jnp.int32, shape, 0) + first).astype(F32)
        angle = pos * freq_ref[...]
        out_ref[i * pos_dev : (i + 1) * pos_dev, :PAIR] = jnp.cos(angle)
        out_ref[i * pos_dev : (i + 1) * pos_dev, PAIR:] = jnp.sin(angle) * sign


def qkv_kernel(slots, parents, x_ref, *refs, n_shard, n_branch, pos_dev, n_far, hows, relative):
    far_refs, refs = refs[:n_far], refs[n_far:]
    w_refs, refs = refs[: len(hows)], refs[len(hows) :]
    vec, tab, n1t_ref, q_ref, k_ref, v_ref, xr_ref, w, n1, w_sem, far_sem = refs
    i = pl.program_id(0)
    rel = relative_to(relative)
    width = x_ref.shape[-1]
    quarter = width // 4
    quad = 2 * PAIR
    rows = 2 * pos_dev
    chosen, _ = chosen_pieces(slots, parents, n_shard, n_branch, pos_dev)

    def w_copies(g):
        out = []
        for ref, (k, how) in zip(w_refs, hows):
            for a in range(3):
                source = ref.at[:, a * width + g * quad : a * width + (g + 1) * quad]
                target = w.at[g, row_block(k, rel, quarter, how), a * quad : (a + 1) * quad]
                out.append(pltpu.make_async_copy(source, target, w_sem.at[g]))
        return out

    def far_copy(t, ref):
        return pltpu.make_async_copy(ref, xr_ref.at[t * pos_dev : (t + 1) * pos_dev], far_sem.at[t])

    @pl.when(i == 0)
    def _():
        for t, (holder, _, _) in enumerate(chosen):
            if n_far == 1:
                far_copy(t, far_refs[0].at[holder]).start()
            else:
                for k in range(n_far):

                    @pl.when(holder ^ rel == k)
                    def _(t=t, k=k):
                        far_copy(t, far_refs[k].at[0:pos_dev]).start()
        for g in range(3):
            for copy in w_copies(g):
                copy.start()
        for t in range(2 + len(chosen)):
            if t >= 2:
                far_copy(t - 2, far_refs[0].at[0:pos_dev] if n_far > 1 else far_refs[0].at[0]).wait()
            x = x_ref[t] if t < 2 else xr_ref[(t - 2) * pos_dev : (t - 1) * pos_dev]
            n, _ = normed(x.astype(F32))
            part = (n * vec[0:1, :width] + vec[1:2, :width]).astype(BF16)
            n1[t * pos_dev : (t + 1) * pos_dev] = part
            turned = part.T
            for j in range(4):
                at = pl.ds(pl.multiple_of(place(j ^ rel) * quarter, quarter), quarter)
                n1t_ref[at, t * pos_dev : (t + 1) * pos_dev] = turned[j * quarter : (j + 1) * quarter, :]

    for g in range(3):

        @pl.when(i == g)
        def _(g=g):
            for copy in w_copies(g):
                copy.wait()

            def product(a, n):
                bias = vec[2:3, a * width + g * quad : a * width + (g + 1) * quad]
                return dot(n1[:n], w[g, :, a * quad : (a + 1) * quad]) + bias

            def turn(y, ref, scale):
                for t in range(y.shape[0] // pos_dev):
                    first = max(t - 1, 0) * pos_dev
                    cosine, sine = tab[first : first + pos_dev, :PAIR], tab[first : first + pos_dev, PAIR:]
                    for h in range(2):
                        part = y[t * pos_dev : (t + 1) * pos_dev, h * PAIR : (h + 1) * PAIR]
                        out = part * cosine + swap_halves(part) * sine
                        ref[t * pos_dev : (t + 1) * pos_dev, h * PAIR : (h + 1) * PAIR] = (out * scale).astype(BF16)

            turn(product(0, rows), q_ref, 1.0 / math.sqrt(width // HEADS))
            turn(product(1, n1.shape[0]), k_ref, 1.0)
            v_ref[...] = product(2, n1.shape[0]).astype(BF16)


def attend_kernel(slots, parents, q_ref, k_ref, v_ref, e_ref, o_ref, linv_ref, k_aug, q_aug, *, n_shard, n_branch, pos_dev):
    rows, keys = q_ref.shape[0], k_ref.shape[0]
    blocks = pos_dev // BLOCK

    @pl.when(pl.program_id(0) == 0)
    def _():
        chosen, _ = chosen_pieces(slots, parents, n_shard, n_branch, pos_dev)
        shape = (pos_dev, PAIR)
        lane = lanes(shape) & 63
        block = lax.broadcasted_iota(jnp.int32, shape, 0) // BLOCK
        k_aug[:pos_dev] = jnp.where(lane - 32 == block, 1.0, 0.0).astype(BF16)
        k_aug[pos_dev : 2 * pos_dev] = jnp.where(lane == block, 1.0, 0.0).astype(BF16)
        for t, (_, valid, _) in enumerate(chosen):
            first = (2 + t) * pos_dev
            shut = jnp.where(valid > 0, 0.0, NEG)
            k_aug[first : first + pos_dev] = jnp.where(lane == 16, shut, 0.0).astype(BF16)
        for copy in range(2):
            clean = jnp.where((lane < blocks) & (lane >= block + copy), NEG, 0.0)
            noisy = (lane >= 32) & (lane < 32 + blocks)
            if copy == 0:
                noisy = noisy & (lane - 32 != block)
            out = jnp.where(noisy, NEG, clean)
            out = jnp.where(lane == 16, 1.0, out)
            q_aug[copy * pos_dev : (copy + 1) * pos_dev] = out.astype(BF16)

    low_q = lanes((rows, PAIR)) < 64
    low_k = lanes((keys, PAIR)) < 64
    q, k, v = q_ref[...], k_ref[...], v_ref[...]
    ones = jnp.ones_like(v)
    q_h = [jnp.where(low_q, q, q_aug[...]), jnp.where(low_q, q_aug[...], q)]
    k_h = [jnp.where(low_k, k, k_aug[...]), jnp.where(low_k, k_aug[...], k)]
    v_t = [jnp.where(low_k, v, ones).T, jnp.where(low_k, ones, v).T]
    chunks = [slice(c * pos_dev, (c + 1) * pos_dev) for c in range(keys // pos_dev)]

    def peak(scores):
        return functools.reduce(jnp.maximum, [jnp.max(item, axis=0, keepdims=True) for item in scores])

    def weigh(h, at, scores, top):
        e = jnp.exp(scores - top).astype(BF16)
        e_ref[h, at] = e
        return e

    scores = [[dot_t(k_h[0][at], q_h[0]) for at in chunks], []]
    weights = [[], []]
    outs = [jnp.zeros((PAIR, rows), F32) for _ in range(2)]
    top = peak(scores[0])
    for c, at in enumerate(chunks):
        scores[1].append(dot_t(k_h[1][at], q_h[1]))
        weights[0].append(weigh(0, at, scores[0][c], top))
    top = peak(scores[1])
    for c, at in enumerate(chunks):
        outs[0] = outs[0] + dot(v_t[0][:, at], weights[0][c])
        weights[1].append(weigh(1, at, scores[1][c], top))
    for c, at in enumerate(chunks):
        outs[1] = outs[1] + dot(v_t[1][:, at], weights[1][c])
    outs = [item.T for item in outs]
    total = jnp.where(low_q, pltpu.roll(outs[0], 64, 1), pltpu.roll(outs[1], 64, 1))
    inv = 1.0 / total
    linv_ref[...] = inv
    o_ref[...] = (jnp.where(low_q, outs[0], outs[1]) * inv).astype(BF16)


def ff_kernel(*refs, part, hows_o, hows, relative):
    first, last = part == 0, part == 2
    wo_refs, refs = (refs[: len(hows_o)], refs[len(hows_o) :]) if part != 1 else ((), refs)
    count = sum(2 if how == "whole" else 1 for _, how in hows)
    w_refs, refs = refs[:count], refs[count:]
    vec, bup, g_in, *refs = refs
    if first:
        x_in, att_in, mid_out, n2_out, n2t_out, attt_out, acc_out, dn2_out, *refs = refs
    elif not last:
        n2_in, n2t_in, acc_out, dn2_out, *refs = refs
    else:
        n2_in, n2t_in, *refs = refs
        parts_in, mid_in, out_out, branch_out, datt_out, small_ref, *refs = refs[:4], *refs[4:]
    bug_ref, *refs = refs
    g_refs, refs = refs[:6], refs[6:]
    wu, wd, g, gt, n2, n2t, hid, dup, acc, dn2, low, stage, w_sem, in_sem, out_sem, *refs = refs
    if first:
        wo, mid, x, att, attt = refs
    elif last:
        wo, mid, parts = refs
    rel = relative_to(relative)
    rows, width = g.shape
    quarter = width // 4
    cols = wu.shape[1] // 4
    half = quarter // 2
    out_copies = []

    def put(source, target):
        copy = pltpu.make_async_copy(source, target, out_sem.at[len(out_copies)])
        copy.start()
        out_copies.append(copy)

    def spread(ref, value):
        for j in range(4):
            at = pl.ds(pl.multiple_of(place(j ^ rel) * quarter, quarter), quarter)
            ref[at, :] = value[j * quarter : (j + 1) * quarter, :]

    o_copies = []
    for a, ref in enumerate(wo_refs):
        k, how = hows_o[a]
        at = row_block(k, rel, quarter, how)
        if how == "whole":
            o_copies.append(pltpu.make_async_copy(ref, wo.at[at], w_sem.at[0]))
        else:
            for b in range(3):
                line = 4 * half + 3 * (cols // 2) + b * half
                source = ref.at[line : line + half]
                o_copies.append(pltpu.make_async_copy(source, wo.at[at, b * cols : (b + 1) * cols], w_sem.at[0]))
    up_copies, down_copies = [], []
    at_ref = 0
    for k, how in hows:
        at = row_block(k, rel, quarter, how)
        if how == "whole":
            up_source, down_source = w_refs[at_ref], w_refs[at_ref + 1]
            at_ref += 2
        else:
            up_source = down_source = w_refs[at_ref]
            at_ref += 1
        for p in range(4):
            there = slice(p * cols, (p + 1) * cols)
            j = ORDER[p] ^ rel
            if how == "whole":
                source = up_source.at[:, pl.ds(pl.multiple_of(j * width + part * cols, cols), cols)]
            else:
                source = up_source.at[pl.ds(pl.multiple_of(j * half, half), half)]
            up_copies.append(pltpu.make_async_copy(source, wu.at[at, there], w_sem.at[1]))
        p = ORDER.index(k)
        spot, sem = p * cols, w_sem.at[2]
        if how == "whole":
            source = down_source.at[part * cols : (part + 1) * cols]
            down_copies.append(pltpu.make_async_copy(source, wd.at[spot : spot + cols], sem))
        else:
            there = pl.ds(pl.multiple_of(spot + half_of(how) * (cols // 2), cols // 2), cols // 2)
            for b in range(3):
                line = 4 * half + b * (cols // 2)
                source = down_source.at[line : line + cols // 2]
                target = wd.at[there, b * cols : (b + 1) * cols]
                down_copies.append(pltpu.make_async_copy(source, target, sem))

    if first:
        pairs = [(x_in, x), (att_in, att), (g_in, g)]
    else:
        pairs = [(n2_in, n2), (g_in, g), (n2t_in, n2t)]
    if last:
        pairs += [(mid_in, mid)] + [(ref, parts.at[i]) for i, ref in enumerate(parts_in)]
    in_copies = [pltpu.make_async_copy(a, b, in_sem.at[i]) for i, (a, b) in enumerate(pairs)]
    if first:
        starts = in_copies[:2] + o_copies + up_copies + in_copies[2:] + down_copies
    else:
        starts = in_copies[:1] + up_copies + in_copies[1:2] + down_copies + in_copies[2:3]
    starts += o_copies + in_copies[3:] if last else []
    for copy in starts:
        copy.start()

    if first:
        for copy in (*in_copies[:2], *o_copies):
            copy.wait()
        mid[...] = x[...].astype(F32) + dot(att[...], wo[...]) + vec[3:4, :width]
        put(mid, mid_out)
        n, _ = normed(mid[...])
        n2[...] = (n * vec[4:5, :width] + vec[5:6, :width]).astype(BF16)
        put(n2, n2_out)
        spread(n2t, n2[...].T)
        put(n2t, n2t_out)
        spread(attt, att[...].T)
        put(attt, attt_out)
    else:
        in_copies[0].wait()

    bias = jnp.concatenate([bup[pl.ds((k ^ rel) * 3 + part, 1), :] for k in ORDER], axis=1)
    for copy in up_copies:
        copy.wait()
    up = dot(n2[...], wu[...]) + bias
    in_copies[2 if first else 1].wait()
    for copy in down_copies:
        copy.wait()
    d_hidden = dot_t(g[...], wd[...])
    cube = 0.044715 * up * up
    th = jnp.tanh(0.7978845608028654 * (up + cube * up))
    left = 0.5 * (1.0 + th)
    hid[...] = (up * left).astype(BF16)
    slope = left + (0.5 * 0.7978845608028654) * up * (1.0 - th * th) * (1.0 + 3.0 * cube)
    d_up = d_hidden * slope
    sums = jnp.sum(d_up, axis=0, keepdims=True)
    dup[...] = d_up.astype(BF16)
    gt[...] = g[...].T
    grad_down = dot(gt[...], hid[...])
    for p in range(4):
        bug_ref[pl.ds(ORDER[p] ^ rel, 1), :] = sums[:, p * cols : (p + 1) * cols]
        for r in range(4):
            block = slice(r * quarter, (r + 1) * quarter)
            stage[p, 4 + r] = grad_down[block, p * cols : (p + 1) * cols].astype(BF16)
    put(stage.at[0, 4:8], g_refs[1])
    put(stage.at[1, 4:8], g_refs[3])
    more, d_more = dot(hid[...], wd[...]), dot_t(dup[...], wu[...])
    if last:
        acc[...] = more
        dn2[...] = d_more
    else:
        low[0] = more.astype(BF16)
        low[1] = d_more.astype(BF16)
        put(low.at[0], acc_out)
        put(low.at[1], dn2_out)
    if not first:
        in_copies[2].wait()
    grad_up = dot(n2t[...], dup[...])
    for p in range(4):
        for r in range(4):
            block = slice(r * quarter, (r + 1) * quarter)
            stage[r, ORDER[p] ^ rel] = grad_up[block, p * cols : (p + 1) * cols].astype(BF16)
    put(stage.at[0, 0:4], g_refs[0])
    put(stage.at[1, 0:4], g_refs[2])
    put(stage.at[2], g_refs[4])
    put(stage.at[3], g_refs[5])

    if last:
        for copy in (*in_copies[3:], *o_copies):
            copy.wait()
        base = mid[...]
        n, inv = normed(base)
        d = dn2[...] + parts[1].astype(F32) + parts[3].astype(F32)
        ct = g[...].astype(F32)
        branch = (ct + norm_back(d, n, inv, vec[4:5, :width])).astype(BF16)
        low[0] = branch
        put(low.at[0], branch_out)
        hid2 = dot_t(branch, wo[...])
        for a, item in enumerate((branch.astype(F32), d * n, d, ct)):
            small_ref[a : a + 1, :] = jnp.sum(item, axis=0, keepdims=True)
        low[1] = hid2.astype(BF16)
        put(low.at[1], datt_out)
        total = base + acc[...] + parts[0].astype(F32) + parts[2].astype(F32) + vec[7:8, :width]
        low[2] = total.astype(BF16)
        put(low.at[2], out_out)
    for copy in out_copies:
        copy.wait()


def attend_back_kernel(q_ref, k_ref, v_ref, do_ref, o_ref, linv_ref, e_ref, tab, n1t_in, *refs, pos_dev, group):
    if group == 0:
        attt_in, branch_in, *refs = refs
    dq_ref, dk_ref, dv_ref, bias_ref, *refs = refs
    g_refs, refs = refs[: 6 if group == 0 else 4], refs[6 if group == 0 else 4 :]
    n1t, stage, in_sem, out_sem, *refs = refs
    if group == 0:
        attt, branch = refs
    rows, keys = q_ref.shape[0], k_ref.shape[0]
    quad = 2 * PAIR
    quarter = n1t_in.shape[0] // 4
    scale = 1.0 / 8.0
    i = pl.program_id(0)
    low_q, low_k = lanes((rows, PAIR)) < 64, lanes((keys, PAIR)) < 64
    pairs = [(n1t_in, n1t)] + ([(attt_in, attt), (branch_in, branch)] if group == 0 else [])
    in_copies = [pltpu.make_async_copy(a, b, in_sem.at[n]) for n, (a, b) in enumerate(pairs)]

    @pl.when(i == 0)
    def _():
        for copy in in_copies:
            copy.start()

    def unturn(t, first):
        parts = []
        for n in range(t.shape[0] // pos_dev):
            at = first[n] * pos_dev
            cosine, sine = tab[at : at + pos_dev, :PAIR], tab[at : at + pos_dev, PAIR:]
            part = t[n * pos_dev : (n + 1) * pos_dev]
            parts.append(part * cosine - swap_halves(part) * sine)
        return jnp.concatenate(parts, axis=0)

    def pair(at):
        q, k, v = q_ref[...], k_ref[...], v_ref[...]
        do = do_ref[...].astype(F32) * linv_ref[...]
        product = do * o_ref[...].astype(F32)
        do_b = do.astype(BF16)
        k_t = k.T
        do_h, v_h = [], []
        for h in range(2):
            here_q, here_k = (low_q, low_k) if h == 0 else (~low_q, ~low_k)
            free = 64 * (1 - h)
            delta = -jnp.sum(jnp.where(here_q, product, 0.0), axis=1, keepdims=True)
            high = delta.astype(BF16).astype(F32)
            lane_q, lane_k = lanes((rows, PAIR)), lanes((keys, PAIR))
            extra = jnp.where(lane_q == free, high, jnp.where(lane_q == free + 1, delta - high, 0.0))
            do_h.append(jnp.where(here_q, do, extra).astype(BF16))
            ones = jnp.where((lane_k == free) | (lane_k == free + 1), 1.0, 0.0).astype(BF16)
            v_h.append(jnp.where(here_k, v, ones))
        chunks = [slice(c * pos_dev, (c + 1) * pos_dev) for c in range(keys // pos_dev)]
        d_q = [jnp.zeros((PAIR, rows), F32) for _ in range(2)]
        d_k, d_v = [[], []], [[], []]
        steps = [(c, h) for c in chunks for h in range(2)]
        d_probs = dot_t(v_h[0][chunks[0]], do_h[0])
        for n, (c, h) in enumerate(steps):
            if n + 1 < len(steps):
                c_next, h_next = steps[n + 1]
                coming = dot_t(v_h[h_next][c_next], do_h[h_next])
            e = e_ref[h, c]
            d_scores = (d_probs * e.astype(F32)).astype(BF16)
            d_v[h].append(dot(e, do_b))
            d_k[h].append(dot(d_scores, q))
            d_q[h] = d_q[h] + dot(k_t[:, c], d_scores)
            d_probs = coming
        d_k, d_v = ([jnp.concatenate(item, axis=0) for item in both] for both in (d_k, d_v))
        d_q = [item.T for item in d_q]
        dv = jnp.where(low_k, d_v[0], d_v[1])
        dk = unturn(jnp.where(low_k, d_k[0], d_k[1]), [0, 0] + list(range(1, keys // pos_dev - 1)))
        dq = unturn(jnp.where(low_q, d_q[0], d_q[1]) * scale, [0, 0])
        dv_ref[:, at] = dv.astype(BF16)
        dk_ref[:, at] = dk.astype(BF16)
        dq_ref[:, at] = dq.astype(BF16)

    for a in range(2):

        @pl.when(i == a)
        def _(a=a):
            pair(slice(a * PAIR, (a + 1) * PAIR))

    def put(unit, grad):
        for r in range(4):
            stage[r, unit] = grad[r * quarter : (r + 1) * quarter].astype(BF16)

    if group == 0:

        @pl.when(i == 0)
        def _():
            in_copies[1].wait()
            in_copies[2].wait()
            for b in range(3):
                put(3 + b, dot(attt[...], branch[:, b * quad : (b + 1) * quad]))

    @pl.when(i == 1)
    def _():
        mine = (dq_ref, dk_ref, dv_ref)
        for a, ref in enumerate(mine):
            bias_ref[a : a + 1, :] = jnp.sum(ref[...].astype(F32), axis=0, keepdims=True)
        in_copies[0].wait()
        for a, ref in enumerate(mine):
            put(a, dot(n1t[:, : ref.shape[0]], ref[...]))
        if group == 0:
            sources = [stage.at[r, u : u + 3] for r in range(2) for u in (0, 3)] + [stage.at[2], stage.at[3]]
        else:
            sources = [stage.at[r] for r in range(4)]
        copies = [pltpu.make_async_copy(a, b, out_sem.at[n]) for n, (a, b) in enumerate(zip(sources, g_refs))]
        for copy in copies:
            copy.start()
        for copy in copies:
            copy.wait()


def input_back_kernel(slots, parents, x_ref, xr_ref, *refs, n_shard, n_branch, pos_dev, relative, hows):
    grads, refs = refs[:9], refs[9:]
    w_refs, refs = refs[: len(hows)], refs[len(hows) :]
    vec, dn1_ref, small_ref, *refs = refs
    outs, (w, d_in, acc, w_sem, d_sem) = refs[: 3 if relative else 1], refs[3 if relative else 1 :]
    rel = relative_to(relative)
    width = x_ref.shape[-1]
    quarter = width // 4
    quad = 2 * PAIR
    rows, keys = dn1_ref.shape[0], acc.shape[0]
    chosen, _ = chosen_pieces(slots, parents, n_shard, n_branch, pos_dev)

    def copies(a):
        out = []
        for ref, (k, how) in zip(w_refs, hows):
            source = ref.at[:, a * width : (a + 1) * width]
            out.append(pltpu.make_async_copy(source, w.at[a, row_block(k, rel, quarter, how)], w_sem.at[a]))
        n = rows if a == 0 else keys
        for g in range(3):
            target = d_in.at[a, 0:n, g * quad : (g + 1) * quad]
            out.append(pltpu.make_async_copy(grads[3 * a + g], target, d_sem.at[a]))
        return out

    for a in (1, 2, 0):
        for copy in copies(a):
            copy.start()
    for a in (1, 2, 0):
        for copy in copies(a):
            copy.wait()
        n = rows if a == 0 else keys
        more = dot_t(d_in[a, :n], w[a])
        if a == 1:
            acc[...] = more
        else:
            acc[:n] = acc[:n] + more
    total, plain = jnp.zeros((1, width), F32), jnp.zeros((1, width), F32)
    for t in range(keys // pos_dev):
        d = acc[t * pos_dev : (t + 1) * pos_dev]
        x = x_ref[t] if t < 2 else xr_ref[(t - 2) * pos_dev : (t - 1) * pos_dev]
        n, _ = normed(x.astype(F32))
        total = total + jnp.sum(d * n, axis=0, keepdims=True)
        plain = plain + jnp.sum(d, axis=0, keepdims=True)
        if t < 2:
            dn1_ref[t * pos_dev : (t + 1) * pos_dev] = d
    small_ref[0:1, :] = total
    small_ref[1:2, :] = plain
    if relative:
        parts = [acc[(2 + t) * pos_dev : (3 + t) * pos_dev] for t in range(len(chosen))]
        for k, ref in zip((3, 1, 2), outs):
            ref[...] = sum(
                jnp.where(holder ^ rel == k, 1.0, 0.0) * part for (holder, _, _), part in zip(chosen, parts)
            ).astype(BF16)
    else:
        outs[0][...] = jnp.zeros_like(outs[0])
        for t, (holder, _, _) in enumerate(chosen):
            part = acc[(2 + t) * pos_dev : (3 + t) * pos_dev]
            outs[0][holder] = (outs[0][holder].astype(F32) + part).astype(BF16)


def final_kernel(x_ref, branch_ref, dn1_ref, got_ref, vec, out_ref):
    i = pl.program_id(0)
    d = dn1_ref[...] + jnp.where(i == 1, 1.0, 0.0) * got_ref[...].astype(F32)
    n, inv = normed(x_ref[0].astype(F32))
    back = norm_back(d, n, inv, vec[0:1, : d.shape[1]])
    out_ref[0] = (branch_ref[...].astype(F32) + back).astype(BF16)


def swap(x, axis, bit):
    n = lax.axis_size(axis)
    return lax.ppermute(x, axis, [(i, i ^ bit) for i in range(n)])


def core(x):
    return swap(x, "shard", 1)


def across(x):
    return swap(x, "shard", 2)


def tie(x, *others):
    return lax.optimization_barrier((x, *others))[0]


def select_bit(bit, a, b):
    return jnp.where(bit == 1, b, a)


class Reduction:
    def __init__(self, chunk):
        *send, two, zero = chunk
        self.near = [(two, zero, len(send) // 2)]
        self.got = [core(item) for item in send]
        self.step = 0

    def more(self, chunk):
        *send, two, zero = chunk
        self.near.append((two, zero, len(send) // 2))
        self.got += [core(item) for item in send]

    def go(self, *after):
        got = tie(self.got, *after)
        r = lax.axis_index("rep")
        if self.step == 0:
            parts, kept = [], []
            for two, zero, n in self.near:
                parts.append(two + jnp.concatenate(got[:n], axis=0))
                kept.append(zero + jnp.concatenate(got[n : 2 * n], axis=0))
                got = got[2 * n :]
            self.part, self.kept = jnp.concatenate(parts, axis=0), jnp.concatenate(kept, axis=0)
            self.got = across(self.part)
        elif self.step in (1, 2):
            bit = self.step
            total = self.kept + got
            size = total.shape[1] // 2
            here = (r // bit) & 1
            self.kept = lax.dynamic_slice_in_dim(total, here * size, size, 1)
            self.part = lax.dynamic_slice_in_dim(total, (1 - here) * size, size, 1)
            self.got = swap(self.part, "rep", bit)
        elif self.step == 3:
            self.part = self.kept + got
            self.got = swap(self.part, "rep", 4)
        elif self.step == 4:
            self.part = self.part + got
            self.got = swap(self.part, "rep", 2)
        else:
            here = (r // 2) & 1
            self.part = jnp.concatenate(
                [select_bit(here, self.part, got), select_bit(here, got, self.part)], axis=1
            )
            self.got = swap(self.part, "rep", 1)
        self.step += 1
        return self.part


class SmallSum:
    LINKS = (("shard", 1), ("shard", 2), ("rep", 1), ("rep", 2), ("rep", 4))

    def __init__(self, x):
        self.part, self.step = x, 0
        self.got = swap(x, *self.LINKS[0])

    def go(self, *after):
        self.part = self.part + tie(self.got, *after)
        self.step += 1
        if self.step < 5:
            self.got = swap(self.part, *self.LINKS[self.step])
        return self.part


class FarGrad:
    def __init__(self, three, one, two):
        self.two, self.got, self.step = two, [core(three), core(one)], 0

    def go(self, *after):
        got = tie(self.got, *after)
        if self.step == 0:
            self.own = got[1]
            self.part = self.two + got[0]
            self.got = across(self.part)
        else:
            self.part = self.own + got
        self.step += 1
        return self.part


def collect_kernel(*refs, quarter):
    parts, (up_ref, down_ref, whole_ref) = refs[:6], refs[6:]
    half = quarter // 2
    y = lax.axis_index("rep") & 1
    cols = parts[0].shape[2]
    for p in range(3):
        for which in range(2):
            at = pl.ds(pl.multiple_of((y if which == 0 else 1 - y) * half, half), half)
            ref = parts[2 * p + which]
            for j in range(4):
                first = j * 3 * cols + p * cols
                up_ref[at, first : first + cols] = ref[j].astype(F32)
                whole_ref[j, at, :] = ref[4 + j].astype(F32)
        down_ref[p * cols : (p + 1) * cols, :] = whole_ref[...].reshape(4 * quarter, cols).T


def collect_qkv_kernel(*refs, quarter):
    parts, (out_ref, qkv_ref) = refs[:4], refs[4:]
    half = quarter // 2
    y = lax.axis_index("rep") & 1
    cols = parts[0].shape[2]
    for which in range(2):
        at = pl.ds(pl.multiple_of((y if which == 0 else 1 - y) * half, half), half)
        first, second = parts[which], parts[2 + which]
        for b in range(3):
            out_ref[at, b * cols : (b + 1) * cols] = first[3 + b].astype(F32)
        for a in range(3):
            for g, block in enumerate((first[a], second[a], second[3 + a])):
                qkv_ref[at, (3 * a + g) * cols : (3 * a + g + 1) * cols] = block.astype(F32)


def shards(
    states,
    cotangent,
    norm1_gain,
    norm1_bias,
    qkv_weight,
    qkv_bias,
    out_weight,
    out_bias,
    norm2_gain,
    norm2_bias,
    up_weight,
    up_bias,
    down_weight,
    down_bias,
    slots,
    parents,
):
    n_shard = lax.axis_size("shard")
    n_branch = n_shard // 4
    pos_dev, width = states.shape[1], states.shape[2]
    ff = up_weight.shape[1]
    rows = 2 * pos_dev
    n_far = n_branch + 1
    keys = rows + n_far * pos_dev
    relative = n_shard == 4 and lax.axis_size("rep") == 8
    quarter = width // 4
    cols = ff // 12
    quad = 2 * PAIR
    me = lax.axis_index("shard")
    sizes = dict(n_shard=n_shard, n_branch=n_branch, pos_dev=pos_dev)
    bound = functools.partial
    shape = jax.ShapeDtypeStruct
    vectors = (norm1_gain, norm1_bias, qkv_bias, out_bias, norm2_gain, norm2_bias, up_bias, down_bias)

    freq = jnp.exp(-jnp.log(10000.0) * jnp.arange(32, dtype=F32) / 32)
    freq = jnp.tile(freq, 4).reshape(1, PAIR)
    table = pl.pallas_call(
        bound(table_kernel, **sizes),
        out_shape=shape(((1 + n_far) * pos_dev, 2 * PAIR), F32),
        grid=(1,),
        in_specs=[SMEM, SMEM, whole((1, PAIR))],
        out_specs=whole(((1 + n_far) * pos_dev, 2 * PAIR)),
        compiler_params=params(),
        cost_estimate=cost(3.5),
        name="rotary_table",
    )(slots, parents, freq)

    natural = [(k, "whole") for k in range(4)]
    if relative:
        half = quarter // 2
        rest = 4 * half + 3 * (cols // 2)
        pack_shapes = [
            shape((pos_dev + 16, width), BF16),
            shape((rest + 3 * half, cols), BF16),
            shape((rest, cols), BF16),
            shape((rest, cols), BF16),
        ]
        packed = pl.pallas_call(
            bound(pack_kernel, quarter=quarter, width=width, cols=cols),
            out_shape=pack_shapes,
            grid=(1,),
            in_specs=[whole(item.shape) for item in vectors] + [ANY] * 4,
            out_specs=[whole(item.shape) for item in pack_shapes],
            scratch_shapes=[pltpu.VMEM((16, width), F32), pltpu.SemaphoreType.DMA((32,))],
            compiler_params=params(),
            cost_estimate=cost(2),
            name="pack",
        )
        q_two = across(qkv_weight)
        q_one = core(qkv_weight)
        x_own, *b_half = packed(*vectors, states, out_weight, up_weight, down_weight)
        x_one = core(x_own)
        x_two = across(x_own)
        x_two, _ = lax.optimization_barrier((x_two, table))
        x_far = [x_own, x_one, x_two, core(x_two)]
        w_qkv = [qkv_weight, q_one, q_two, core(q_two)]
        how_qkv = natural
        how_out = [(0, "whole"), (1, "whole"), (2, "direct"), (2, "via"), (3, "direct"), (3, "via")]
        o_one, u_one, d_one = core(out_weight), core(up_weight), core(down_weight)
        b_two = [across(tie(b_half[0], x_two, q_two))]
        vec, b_up = pl.pallas_call(
            bound(unpack_kernel, sizes=[item.shape[0] for item in vectors], pos_dev=pos_dev, cols=cols),
            out_shape=[shape((8, ff), F32), shape((12, cols), F32)],
            grid=(1,),
            in_specs=[ANY] * 4,
            out_specs=[whole((8, ff)), whole((12, cols))],
            scratch_shapes=[pltpu.VMEM((4, 16, width), BF16), pltpu.SemaphoreType.DMA((4,))],
            compiler_params=params(),
            cost_estimate=cost(2),
            name="unpack",
        )(*x_far)
    else:
        gather = lambda item: lax.all_gather(item, "shard", axis=0, tiled=True)
        rows_of = lambda item: [item[j * quarter : (j + 1) * quarter] for j in range(4)]
        w_qkv, how_qkv = rows_of(gather(qkv_weight)), natural
        x_far = [gather(states[1][None])]
        w_out, how_out = rows_of(gather(out_weight)), natural
        ups, downs = rows_of(gather(up_weight)), gather(down_weight)
        pieces = []
        for k in range(4):
            pieces += [ups[k], downs[k * width : (k + 1) * width]]
        w_ff, how_ff = [pieces] * 3, natural
        small = lax.all_gather(jnp.concatenate(vectors), "shard", axis=0)
        lines, at = [], 0
        for item in vectors:
            n = item.shape[0]
            line = small[:, at : at + n].reshape(1, n_shard * n).astype(F32)
            lines.append(jnp.pad(line, ((0, 0), (0, ff - n_shard * n))))
            at += n
        vec = jnp.concatenate(lines, axis=0)
        b_up = vec[6].reshape(12, cols)

    each = lambda i: (i, 0)
    n1t, q, k, v, x_seen = pl.pallas_call(
        bound(qkv_kernel, n_far=len(x_far), hows=how_qkv, relative=relative, **sizes),
        out_shape=[
            shape((width, keys), BF16),
            shape((rows, width), BF16),
            shape((keys, width), BF16),
            shape((keys, width), BF16),
            shape((n_far * pos_dev, width), BF16),
        ],
        grid=(3,),
        in_specs=[SMEM, SMEM, whole((2, pos_dev, width))]
        + [ANY] * (len(x_far) + len(how_qkv))
        + [whole((8, ff)), whole(((1 + n_far) * pos_dev, 2 * PAIR))],
        out_specs=[
            whole((width, keys)),
            pl.BlockSpec((rows, quad), lambda i: (0, i)),
            pl.BlockSpec((keys, quad), lambda i: (0, i)),
            pl.BlockSpec((keys, quad), lambda i: (0, i)),
            whole((n_far * pos_dev, width)),
        ],
        scratch_shapes=[
            pltpu.VMEM((3, width, 3 * quad), BF16),
            pltpu.VMEM((keys, width), BF16),
            pltpu.SemaphoreType.DMA((3,)),
            pltpu.SemaphoreType.DMA((n_far,)),
        ],
        compiler_params=params(),
        cost_estimate=cost(11),
        name="norm_qkv",
    )(slots, parents, states, *x_far, *w_qkv, vec, table)

    if relative:
        b_two[0] = tie(b_two[0], q)
        b_two += [across(tie(b_half[p], b_two[0])) for p in (1, 2)]
        b_via = [swap(b_two[0], "rep", 1)]
        b_three = [core(b_two[0])]

    pair = lambda i: (0, i)
    n_pair = width // PAIR
    e, attended, linv = pl.pallas_call(
        bound(attend_kernel, **sizes),
        out_shape=[
            shape((HEADS, keys, rows), BF16),
            shape((rows, width), BF16),
            shape((rows, width), F32),
        ],
        grid=(n_pair,),
        in_specs=[
            SMEM,
            SMEM,
            pl.BlockSpec((rows, PAIR), pair),
            pl.BlockSpec((keys, PAIR), pair),
            pl.BlockSpec((keys, PAIR), pair),
        ],
        out_specs=[
            pl.BlockSpec((2, keys, rows), lambda i: (i, 0, 0)),
            pl.BlockSpec((rows, PAIR), pair),
            pl.BlockSpec((rows, PAIR), pair),
        ],
        scratch_shapes=[pltpu.VMEM((keys, PAIR), BF16), pltpu.VMEM((rows, PAIR), BF16)],
        compiler_params=params(),
        cost_estimate=cost(17),
        name="attend",
    )(slots, parents, tie(q, b_two[0]) if relative else q, k, v)

    if relative:
        b_last = [core(tie(b_via[0], attended))]
        b_two[1:] = [tie(item, attended) for item in b_two[1:]]
        b_via += [swap(item, "rep", 1) for item in b_two[1:]]
        b_three += [core(item) for item in b_two[1:]]
        attended = tie(attended, b_last[0], *b_two[1:])
        w_out = [out_weight, o_one, b_two[0], b_via[0], b_three[0], b_last[0]]
        how_ff = how_out
        w_ff = [[up_weight, down_weight, u_one, d_one, b_two[0], b_via[0], b_three[0], b_last[0]]]

    x_rows = states.reshape(rows, width)
    g_rows = cotangent.reshape(rows, width)
    wide, low, turned = shape((rows, width), F32), shape((rows, width), BF16), shape((width, rows), BF16)

    def feed(part, ins, outs, scratch, vmem_out=()):
        weights = ([] if part == 1 else w_out) + w_ff[part]
        vm = lambda item: pltpu.VMEM(item.shape, item.dtype)
        outs = outs + list(vmem_out) + [shape((4, cols), F32)]
        grads = [shape((4, quarter, cols), BF16)] * 4 + [shape((8, quarter, cols), BF16)] * 2
        n_any = len(outs) - len(vmem_out) - 1
        result = pl.pallas_call(
            bound(ff_kernel, part=part, hows_o=how_out, hows=how_ff, relative=relative),
            out_shape=outs + grads,
            grid=(1,),
            in_specs=[ANY] * len(weights) + [whole((8, ff)), whole((12, cols))] + [ANY] * (1 + len(ins)),
            out_specs=[ANY] * n_any + [whole(item.shape) for item in outs[n_any:]] + [ANY] * 6,
            scratch_shapes=[
                pltpu.VMEM((width, 4 * cols), BF16),
                pltpu.VMEM((4 * cols, width), BF16),
                vm(low),
                vm(turned),
                vm(low),
                vm(turned),
                pltpu.VMEM((rows, 4 * cols), BF16),
                pltpu.VMEM((rows, 4 * cols), BF16),
                vm(wide),
                vm(wide),
                pltpu.VMEM((3, rows, width), BF16),
                pltpu.VMEM((4, 8, quarter, cols), BF16),
                pltpu.SemaphoreType.DMA((3,)),
                pltpu.SemaphoreType.DMA((8,)),
                pltpu.SemaphoreType.DMA((12,)),
            ]
            + scratch,
            compiler_params=params(),
            cost_estimate=cost(13),
            name=("feed_first", "feed_second", "feed_third")[part],
        )(*weights, vec, b_up, g_rows, *ins)
        return result[:-6], result[-6:]

    square = pltpu.VMEM((width, width), BF16)
    (mid, n2, n2t, attt, *parts, bug0), chunk0 = feed(
        0, (x_rows, attended), [wide, low, turned, turned, low, low],
        [square, pltpu.VMEM((rows, width), F32)] + [pltpu.VMEM((rows, width), BF16)] * 2 + [pltpu.VMEM((width, rows), BF16)],
    )
    if relative:
        sum0 = Reduction(chunk0)
        b_via[1:] = [tie(item, bug0) for item in b_via[1:]]
        b_last += [core(item) for item in b_via[1:]]
        w_ff += [
            [up_weight, down_weight, u_one, d_one, b_two[p], b_via[p], b_three[p], b_last[p]] for p in (1, 2)
        ]
        n2 = tie(n2, sum0.go(*b_via[1:]))
    (*more, bug1), chunk1 = feed(1, (n2, n2t), [low, low], [])
    if relative:
        sum1 = Reduction(chunk1)
        n2 = tie(n2, sum1.go(sum0.go(bug1)))
    (output, branch, d_att, small2, bug2), chunk2 = feed(
        2, (n2, n2t, *parts, *more, mid), [low, low, low],
        [square, pltpu.VMEM((rows, width), F32), pltpu.VMEM((4, rows, width), BF16)], [shape((8, width), F32)],
    )
    if relative:
        sum2 = Reduction(chunk2)

    def back(g, d_att, *more):
        here = lambda i: (0, 2 * g + i)
        grads = [shape((3, quarter, quad), BF16)] * 4
        if g == 0:
            grads += [shape((6, quarter, quad), BF16)] * 2
        outs = [shape((n, quad), t) for n, t in ((rows, BF16), (keys, BF16), (keys, BF16), (8, F32))]
        scratch = [
            pltpu.VMEM((width, keys), BF16),
            pltpu.VMEM((4, 6 if g == 0 else 3, quarter, quad), BF16),
            pltpu.SemaphoreType.DMA((3,)),
            pltpu.SemaphoreType.DMA((6,)),
        ] + [pltpu.VMEM(item.shape, item.dtype) for item in more]
        return pl.pallas_call(
            bound(attend_back_kernel, pos_dev=pos_dev, group=g),
            out_shape=outs + grads,
            grid=(2,),
            in_specs=[
                pl.BlockSpec((rows, PAIR), here),
                pl.BlockSpec((keys, PAIR), here),
                pl.BlockSpec((keys, PAIR), here),
                pl.BlockSpec((rows, PAIR), here),
                pl.BlockSpec((rows, PAIR), here),
                pl.BlockSpec((rows, PAIR), here),
                pl.BlockSpec((2, keys, rows), lambda i: (2 * g + i, 0, 0)),
                whole(((1 + n_far) * pos_dev, 2 * PAIR)),
                ANY,
            ]
            + [ANY] * len(more),
            out_specs=[whole(item.shape) for item in outs] + [ANY] * len(grads),
            scratch_shapes=scratch,
            compiler_params=params(40),
            cost_estimate=cost(11),
            name=f"attend_back_{g}",
        )(q, k, v, d_att, attended, linv, e, table, n1t, *more)

    def turns(last, *items):
        for item in items:
            last = item.go(last)
        return last

    backs = []
    for g in range(3):
        if relative:
            if g == 0:
                last = turns(small2, sum0, sum1, sum2)
            elif g == 1:
                last = turns(backs[0][3], sum0, sum1, sum2, sum3)
            else:
                last = turns(backs[1][3], sum0, sum1, sum2, sum3)
            d_att = tie(d_att, last)
        backs.append(back(g, d_att, *((attt, branch) if g == 0 else ())))
        if relative and g == 0:
            sum3 = Reduction(backs[0][4:])
        if relative and g == 1:
            sum4 = Reduction(backs[1][4:])
        if relative and g == 2:
            sum4.more(backs[2][4:])
    d_all = [backs[g][a] for a in range(3) for g in range(3)]
    small_qkv = jnp.concatenate([item[3][:3] for item in backs], axis=1)
    if relative:
        last = turns(backs[2][3], sum3, sum0, sum1, sum2, sum4)
        d_all[0] = tie(d_all[0], last)

    far_shapes = (
        [shape((pos_dev, width), BF16)] * 3
        if relative
        else [shape((n_shard, pos_dev, width), BF16)]
    )
    dn1, small1, *far = pl.pallas_call(
        bound(input_back_kernel, relative=relative, hows=how_qkv, **sizes),
        out_shape=[shape((rows, width), F32), shape((8, width), F32), *far_shapes],
        grid=(1,),
        in_specs=[SMEM, SMEM, whole((2, pos_dev, width)), whole((n_far * pos_dev, width))]
        + [ANY] * (9 + len(how_qkv))
        + [whole((8, ff))],
        out_specs=[whole((rows, width)), whole((8, width))] + [whole(item.shape) for item in far_shapes],
        scratch_shapes=[
            pltpu.VMEM((3, width, width), BF16),
            pltpu.VMEM((3, keys, width), BF16),
            pltpu.VMEM((keys, width), F32),
            pltpu.SemaphoreType.DMA((3,)),
            pltpu.SemaphoreType.DMA((3,)),
        ],
        compiler_params=params(40),
        cost_estimate=cost(10),
        name="input_back",
    )(slots, parents, states, x_seen, *d_all, *w_qkv, vec)

    collect = pl.pallas_call(
        bound(collect_kernel, quarter=quarter),
        out_shape=[shape((quarter, ff), F32), shape((ff // 4, width), F32)],
        scratch_shapes=[pltpu.VMEM((4, quarter, cols), F32)],
        compiler_params=params(40),
        cost_estimate=cost(4),
        name="collect",
    )
    vectors_grad = jnp.concatenate([small1[:2], small_qkv, small2[:4], jnp.concatenate([bug0, bug1, bug2], axis=1)], axis=0)
    if relative:
        far_sum = FarGrad(*far)
        small_sum = SmallSum(vectors_grad)
        order = [
            (sum0,), sum2, sum4, sum3, far_sum, small_sum, small_sum, sum1, sum4, small_sum, sum2, sum3, sum4, small_sum, sum3,
            sum4, far_sum, sum4, small_sum, None,
        ]
        last = small1
        for item in order:
            if isinstance(item, tuple):
                item[0].got, last = lax.optimization_barrier((item[0].got, last))
            elif item is None:
                halves = [half for part in (sum0, sum1, sum2) for half in (part.part, part.got)]
                grad_up, grad_down = collect(tie(halves[0], last), *halves[1:])
                last = grad_down
            else:
                last = item.go(last)
        counts = [item.step for item in (sum0, sum1, sum2, sum3, sum4)]
        assert counts == [6] * 5, counts
        got, total = far_sum.part, small_sum.part
    else:
        got = lax.psum_scatter(far[0], "shard", scatter_dimension=0)
        total = lax.psum(vectors_grad, ("rep", "shard"))
    states_grad = pl.pallas_call(
        final_kernel,
        out_shape=shape((2, pos_dev, width), BF16),
        grid=(2,),
        in_specs=[
            pl.BlockSpec((1, pos_dev, width), lambda i: (i, 0, 0)),
            pl.BlockSpec((pos_dev, width), each),
            pl.BlockSpec((pos_dev, width), each),
            whole((pos_dev, width)),
            whole((8, ff)),
        ],
        out_specs=pl.BlockSpec((1, pos_dev, width), lambda i: (i, 0, 0)),
        compiler_params=params(40),
        cost_estimate=cost(4),
        name="states_back",
    )(states, branch, dn1, got, vec)

    def up_of(parts):
        return jnp.stack([item[:4] for item in parts]).transpose(2, 1, 0, 3).reshape(-1, ff)

    def down_of(parts):
        return jnp.stack([item[4:8] for item in parts]).transpose(0, 3, 1, 2).reshape(3, -1, width)

    def out_of(part):
        return part[3:].transpose(1, 0, 2).reshape(-1, width)

    def qkv_of(parts):
        return jnp.stack(parts).transpose(2, 1, 0, 3).reshape(-1, 3 * width)

    if relative:
        grad_out, grad_qkv = pl.pallas_call(
            bound(collect_qkv_kernel, quarter=quarter),
            out_shape=[shape((quarter, width), F32), shape((quarter, 3 * width), F32)],
            compiler_params=params(40),
            cost_estimate=cost(2),
            name="collect_qkv",
        )(sum3.part, sum3.got, sum4.part, sum4.got)
    else:

        def natural_order(chunk):
            *send, two, zero = chunk
            n = len(send) // 2
            return [zero, jnp.concatenate(send[n:]), two, jnp.concatenate(send[:n])]

        parts = list(zip(*(natural_order(chunk) for chunk in (chunk0, chunk1, chunk2))))
        quads = list(zip(*(natural_order(item[4:]) for item in backs)))
        ups = jnp.concatenate([up_of(item) for item in parts], axis=0)
        downs = jnp.concatenate([down_of(item).reshape(-1, width) for item in parts], axis=0)
        outs = jnp.concatenate([out_of(item[0]) for item in quads], axis=0)
        qkvs = jnp.concatenate([qkv_of((a[:3], b, c)) for a, b, c in quads], axis=0)

        def reduced(item):
            part = lax.psum_scatter(item, "shard", scatter_dimension=0, tiled=True)
            return lax.psum(part, "rep").astype(F32)

        grad_up, grad_down, grad_out, grad_qkv = (reduced(item) for item in (ups, downs, outs, qkvs))

    def own_rows(first, count):
        line = total[first : first + count].reshape(-1)
        n = line.shape[0] // n_shard
        return lax.dynamic_slice_in_dim(line, me * n, n)

    return (
        output.reshape(2, pos_dev, width),
        states_grad,
        own_rows(0, 1),
        own_rows(1, 1),
        grad_qkv,
        own_rows(2, 3),
        grad_out,
        own_rows(5, 1),
        own_rows(6, 1),
        own_rows(7, 1),
        grad_up,
        own_rows(9, 4),
        grad_down,
        own_rows(8, 1),
    )


def solution(mesh):
    in_specs = (
        P(None, ("rep", "shard"), None),
        P(None, ("rep", "shard"), None),
        P("shard"),
        P("shard"),
        P("shard", None),
        P("shard"),
        P("shard", None),
        P("shard"),
        P("shard"),
        P("shard"),
        P("shard", None),
        P("shard"),
        P("shard", None),
        P("shard"),
        P("rep", None),
        P("rep", None),
    )
    out_specs = (
        P(None, ("rep", "shard"), None),
        P(None, ("rep", "shard"), None),
        P("shard"),
        P("shard"),
        P("shard", None),
        P("shard"),
        P("shard", None),
        P("shard"),
        P("shard"),
        P("shard"),
        P("shard", None),
        P("shard"),
        P("shard", None),
        P("shard"),
    )
    return jax.shard_map(shards, mesh=mesh, in_specs=in_specs, out_specs=out_specs, check_vma=False)
```

```python
import functools
import math

import jax
import jax.numpy as jnp
from jax import lax
from jax.experimental import pallas as pl
from jax.experimental.pallas import tpu as pltpu
from jax.sharding import PartitionSpec as P

HEADS = 12
BLOCK = 16
NEG = -1e30
PAIR = 128
F32 = jnp.float32
BF16 = jnp.bfloat16
ANY = pl.BlockSpec(memory_space=pltpu.HBM)


SMEM = pl.BlockSpec(memory_space=pltpu.SMEM)


def params(mib=58):
    return pltpu.CompilerParams(vmem_limit_bytes=mib * 2**20)


def cost(us):
    return pl.CostEstimate(flops=int(us * 1.15e9), bytes_accessed=0, transcendentals=0)


def whole(shape):
    return pl.BlockSpec(shape, lambda *_: (0,) * len(shape))


def place(rel):
    return jnp.where(rel == 3, 0, jnp.where(rel == 0, 3, rel))


ORDER = (3, 1, 2, 0)


def dot(a, b):
    return lax.dot_general(a, b, (((1,), (0,)), ((), ())), preferred_element_type=F32)


def dot_t(a, b):
    return lax.dot_general(a, b, (((1,), (1,)), ((), ())), preferred_element_type=F32)


def t_dot(a, b):
    return lax.dot_general(a, b, (((0,), (0,)), ((), ())), preferred_element_type=F32)


def normed(x):
    spread = x - jnp.mean(x, axis=-1, keepdims=True)
    inv = lax.rsqrt(jnp.mean(spread * spread, axis=-1, keepdims=True) + 1e-05)
    return spread * inv, inv


def norm_back(d, n, inv, gain):
    e = d * gain
    return inv * (
        e - jnp.mean(e, axis=-1, keepdims=True) - n * jnp.mean(e * n, axis=-1, keepdims=True)
    )


def lanes(shape):
    return lax.broadcasted_iota(jnp.int32, shape, len(shape) - 1)


def swap_halves(t):
    return jnp.where((lanes(t.shape) & 63) < 32, pltpu.roll(t, 96, 1), pltpu.roll(t, 32, 1))

def chosen_pieces(slots, parents, n_shard, n_branch, pos_dev):
    me = lax.axis_index("shard")
    mine = slots[0, me]
    seg = jnp.where(mine < n_branch, 0, mine - n_branch + 1)
    parent = parents[0, seg]

    def holder(piece):
        found = me
        for j in range(n_shard):
            found = jnp.where(slots[0, j] == piece, j, found)
        return found

    out = []
    for run in range(n_branch):
        valid = jnp.where(seg > 0, 1, jnp.where(mine > run, 1, 0))
        out.append((holder(run), valid, run * pos_dev))
    has = jnp.where(parent > 0, 1, 0)
    out.append((holder(jnp.where(parent > 0, n_branch + parent - 1, -1)), has, n_branch * pos_dev))
    start = jnp.where(
        mine < n_branch,
        mine * pos_dev,
        jnp.where(mine < 2 * n_branch, n_branch * pos_dev, (n_branch + 1) * pos_dev),
    )
    return out, start


def relative_to(relative):
    return lax.axis_index("shard") if relative else jnp.zeros((), jnp.int32)


def half_of(how):
    y = lax.axis_index("rep") & 1
    return y if how == "direct" else 1 - y


def row_block(k, rel, quarter, how, chunk=None):
    first = (k ^ rel) * quarter
    if how == "whole":
        return pl.ds(pl.multiple_of(first, 16), quarter)
    first = first + half_of(how) * (quarter // 2)
    if chunk is None:
        return pl.ds(pl.multiple_of(first, 16), quarter // 2)
    return pl.ds(pl.multiple_of(first + chunk * (quarter // 4), 16), quarter // 4)


def pack_kernel(*refs, quarter, width, cols):
    vectors, refs = refs[:8], refs[8:]
    states, w_out, w_up, w_down, s_out, *refs = refs
    b_outs, (small, sem) = refs[:3], refs[3:]
    half = quarter // 2
    y = lax.axis_index("rep") & 1
    at = pl.ds(pl.multiple_of(y * half, half), half)
    pos_dev = states.shape[1]
    copies = [(states.at[1], s_out.at[0:pos_dev])]
    for p in range(3):
        for j in range(4):
            source = w_up.at[at, j * width + p * cols : j * width + (p + 1) * cols]
            copies.append((source, b_outs[p].at[j * half : (j + 1) * half]))
        rows = pl.ds(pl.multiple_of(p * cols + y * (cols // 2), cols // 2), cols // 2)
        for b in range(3):
            first = 4 * half + b * (cols // 2)
            copies.append((w_down.at[rows, b * cols : (b + 1) * cols], b_outs[p].at[first : first + cols // 2]))
    for b in range(3):
        first = 4 * half + 3 * (cols // 2) + b * half
        copies.append((w_out.at[at, b * cols : (b + 1) * cols], b_outs[0].at[first : first + half]))
    copies = [pltpu.make_async_copy(a, b, sem.at[i]) for i, (a, b) in enumerate(copies)]
    for copy in copies:
        copy.start()
    small[...] = jnp.zeros_like(small)
    for r, ref in enumerate(vectors):
        small[r : r + 1, : ref.shape[0]] = ref[...].astype(F32).reshape(1, -1)
    s_out[pos_dev:, :] = small[...].astype(BF16)
    for copy in copies:
        copy.wait()


def unpack_kernel(a, b, c, d, vec_ref, up_ref, held, sem, *, sizes, pos_dev, cols):
    rel = lax.axis_index("shard")
    copies = [
        pltpu.make_async_copy(ref.at[pos_dev : pos_dev + 16], held.at[k ^ rel], sem.at[k])
        for k, ref in enumerate((a, b, c, d))
    ]
    for copy in copies:
        copy.start()
    for copy in copies:
        copy.wait()
    for j in range(4):
        part = held[j].astype(F32)
        for r, size in enumerate(sizes):
            vec_ref[r : r + 1, j * size : (j + 1) * size] = part[r : r + 1, :size]
        for p in range(3):
            up_ref[j * 3 + p : j * 3 + p + 1, :] = part[6:7, p * cols : (p + 1) * cols]


def table_kernel(slots, parents, freq_ref, out_ref, *, n_shard, n_branch, pos_dev):
    out, start = chosen_pieces(slots, parents, n_shard, n_branch, pos_dev)
    starts = [start] + [item[2] for item in out]
    shape = (pos_dev, PAIR)
    sign = jnp.where((lanes(shape) & 63) < 32, -1.0, 1.0)
    for i, first in enumerate(starts):
        pos = (lax.broadcasted_iota(jnp.int32, shape, 0) + first).astype(F32)
        angle = pos * freq_ref[...]
        out_ref[i * pos_dev : (i + 1) * pos_dev, :PAIR] = jnp.cos(angle)
        out_ref[i * pos_dev : (i + 1) * pos_dev, PAIR:] = jnp.sin(angle) * sign


def qkv_kernel(slots, parents, x_ref, *refs, n_shard, n_branch, pos_dev, n_far, hows, relative):
    far_refs, refs = refs[:n_far], refs[n_far:]
    w_refs, refs = refs[: len(hows)], refs[len(hows) :]
    vec, tab, n1t_ref, q_ref, k_ref, v_ref, xr_ref, w, n1, w_sem, far_sem = refs
    i = pl.program_id(0)
    rel = relative_to(relative)
    width = x_ref.shape[-1]
    quarter = width // 4
    quad = 2 * PAIR
    rows = 2 * pos_dev
    chosen, _ = chosen_pieces(slots, parents, n_shard, n_branch, pos_dev)

    def w_copies(g):
        out = []
        for ref, (k, how) in zip(w_refs, hows):
            for a in range(3):
                source = ref.at[:, a * width + g * quad : a * width + (g + 1) * quad]
                target = w.at[g, row_block(k, rel, quarter, how), a * quad : (a + 1) * quad]
                out.append(pltpu.make_async_copy(source, target, w_sem.at[g]))
        return out

    def far_copy(t, ref):
        return pltpu.make_async_copy(ref, xr_ref.at[t * pos_dev : (t + 1) * pos_dev], far_sem.at[t])

    @pl.when(i == 0)
    def _():
        for t, (holder, _, _) in enumerate(chosen):
            if n_far == 1:
                far_copy(t, far_refs[0].at[holder]).start()
            else:
                for k in range(n_far):

                    @pl.when(holder ^ rel == k)
                    def _(t=t, k=k):
                        far_copy(t, far_refs[k].at[0:pos_dev]).start()
        for g in range(3):
            for copy in w_copies(g):
                copy.start()
        for t in range(2 + len(chosen)):
            if t >= 2:
                far_copy(t - 2, far_refs[0].at[0:pos_dev] if n_far > 1 else far_refs[0].at[0]).wait()
            x = x_ref[t] if t < 2 else xr_ref[(t - 2) * pos_dev : (t - 1) * pos_dev]
            n, _ = normed(x.astype(F32))
            part = (n * vec[0:1, :width] + vec[1:2, :width]).astype(BF16)
            n1[t * pos_dev : (t + 1) * pos_dev] = part
            turned = part.T
            for j in range(4):
                at = pl.ds(pl.multiple_of(place(j ^ rel) * quarter, quarter), quarter)
                n1t_ref[at, t * pos_dev : (t + 1) * pos_dev] = turned[j * quarter : (j + 1) * quarter, :]

    for g in range(3):

        @pl.when(i == g)
        def _(g=g):
            for copy in w_copies(g):
                copy.wait()

            def product(a, n):
                bias = vec[2:3, a * width + g * quad : a * width + (g + 1) * quad]
                return dot(n1[:n], w[g, :, a * quad : (a + 1) * quad]) + bias

            def turn(y, ref, scale):
                for t in range(y.shape[0] // pos_dev):
                    first = max(t - 1, 0) * pos_dev
                    cosine, sine = tab[first : first + pos_dev, :PAIR], tab[first : first + pos_dev, PAIR:]
                    for h in range(2):
                        part = y[t * pos_dev : (t + 1) * pos_dev, h * PAIR : (h + 1) * PAIR]
                        out = part * cosine + swap_halves(part) * sine
                        ref[t * pos_dev : (t + 1) * pos_dev, h * PAIR : (h + 1) * PAIR] = (out * scale).astype(BF16)

            turn(product(0, rows), q_ref, 1.0 / math.sqrt(width // HEADS))
            turn(product(1, n1.shape[0]), k_ref, 1.0)
            v_ref[...] = product(2, n1.shape[0]).astype(BF16)


def attend_kernel(slots, parents, q_ref, k_ref, v_ref, e_ref, o_ref, linv_ref, k_aug, q_aug, *, n_shard, n_branch, pos_dev):
    rows, keys = q_ref.shape[0], k_ref.shape[0]
    blocks = pos_dev // BLOCK

    @pl.when(pl.program_id(0) == 0)
    def _():
        chosen, _ = chosen_pieces(slots, parents, n_shard, n_branch, pos_dev)
        shape = (pos_dev, PAIR)
        lane = lanes(shape) & 63
        block = lax.broadcasted_iota(jnp.int32, shape, 0) // BLOCK
        k_aug[:pos_dev] = jnp.where(lane - 32 == block, 1.0, 0.0).astype(BF16)
        k_aug[pos_dev : 2 * pos_dev] = jnp.where(lane == block, 1.0, 0.0).astype(BF16)
        for t, (_, valid, _) in enumerate(chosen):
            first = (2 + t) * pos_dev
            shut = jnp.where(valid > 0, 0.0, NEG)
            k_aug[first : first + pos_dev] = jnp.where(lane == 16, shut, 0.0).astype(BF16)
        for copy in range(2):
            clean = jnp.where((lane < blocks) & (lane >= block + copy), NEG, 0.0)
            noisy = (lane >= 32) & (lane < 32 + blocks)
            if copy == 0:
                noisy = noisy & (lane - 32 != block)
            out = jnp.where(noisy, NEG, clean)
            out = jnp.where(lane == 16, 1.0, out)
            q_aug[copy * pos_dev : (copy + 1) * pos_dev] = out.astype(BF16)

    low_q = lanes((rows, PAIR)) < 64
    low_k = lanes((keys, PAIR)) < 64
    q, k, v = q_ref[...], k_ref[...], v_ref[...]
    ones = jnp.ones_like(v)
    q_h = [jnp.where(low_q, q, q_aug[...]), jnp.where(low_q, q_aug[...], q)]
    k_h = [jnp.where(low_k, k, k_aug[...]), jnp.where(low_k, k_aug[...], k)]
    v_t = [jnp.where(low_k, v, ones).T, jnp.where(low_k, ones, v).T]
    chunks = [slice(c * pos_dev, (c + 1) * pos_dev) for c in range(keys // pos_dev)]

    def peak(scores):
        return functools.reduce(jnp.maximum, [jnp.max(item, axis=0, keepdims=True) for item in scores])

    def weigh(h, at, scores, top):
        e = jnp.exp(scores - top).astype(BF16)
        e_ref[h, at] = e
        return e

    scores = [[dot_t(k_h[0][at], q_h[0]) for at in chunks], []]
    weights = [[], []]
    outs = [jnp.zeros((PAIR, rows), F32) for _ in range(2)]
    top = peak(scores[0])
    for c, at in enumerate(chunks):
        scores[1].append(dot_t(k_h[1][at], q_h[1]))
        weights[0].append(weigh(0, at, scores[0][c], top))
    top = peak(scores[1])
    for c, at in enumerate(chunks):
        outs[0] = outs[0] + dot(v_t[0][:, at], weights[0][c])
        weights[1].append(weigh(1, at, scores[1][c], top))
    for c, at in enumerate(chunks):
        outs[1] = outs[1] + dot(v_t[1][:, at], weights[1][c])
    outs = [item.T for item in outs]
    total = jnp.where(low_q, pltpu.roll(outs[0], 64, 1), pltpu.roll(outs[1], 64, 1))
    inv = 1.0 / total
    linv_ref[...] = inv
    o_ref[...] = (jnp.where(low_q, outs[0], outs[1]) * inv).astype(BF16)


def ff_kernel(*refs, part, hows_o, hows, relative):
    first, last = part == 0, part == 2
    wo_refs, refs = (refs[: len(hows_o)], refs[len(hows_o) :]) if part != 1 else ((), refs)
    count = sum(2 if how == "whole" else 1 for _, how in hows)
    w_refs, refs = refs[:count], refs[count:]
    vec, bup, g_in, *refs = refs
    if first:
        x_in, att_in, mid_out, n2_out, n2t_out, attt_out, acc_out, dn2_out, *refs = refs
    elif not last:
        n2_in, n2t_in, acc_out, dn2_out, *refs = refs
    else:
        n2_in, n2t_in, *refs = refs
        parts_in, mid_in, out_out, branch_out, datt_out, small_ref, *refs = refs[:4], *refs[4:]
    bug_ref, *refs = refs
    g_refs, refs = refs[:6], refs[6:]
    wu, wd, g, gt, n2, n2t, hid, dup, acc, dn2, low, stage, w_sem, in_sem, out_sem, *refs = refs
    if first:
        wo, mid, x, att, attt = refs
    elif last:
        wo, mid, parts = refs
    rel = relative_to(relative)
    rows, width = g.shape
    quarter = width // 4
    cols = wu.shape[1] // 4
    half = quarter // 2
    out_copies = []

    def put(source, target):
        copy = pltpu.make_async_copy(source, target, out_sem.at[len(out_copies)])
        copy.start()
        out_copies.append(copy)

    def spread(ref, value):
        for j in range(4):
            at = pl.ds(pl.multiple_of(place(j ^ rel) * quarter, quarter), quarter)
            ref[at, :] = value[j * quarter : (j + 1) * quarter, :]

    o_copies = []
    for a, ref in enumerate(wo_refs):
        k, how = hows_o[a]
        at = row_block(k, rel, quarter, how)
        if how == "whole":
            o_copies.append(pltpu.make_async_copy(ref, wo.at[at], w_sem.at[0]))
        else:
            for b in range(3):
                line = 4 * half + 3 * (cols // 2) + b * half
                source = ref.at[line : line + half]
                o_copies.append(pltpu.make_async_copy(source, wo.at[at, b * cols : (b + 1) * cols], w_sem.at[0]))
    up_copies, down_copies = [], []
    at_ref = 0
    for k, how in hows:
        at = row_block(k, rel, quarter, how)
        if how == "whole":
            up_source, down_source = w_refs[at_ref], w_refs[at_ref + 1]
            at_ref += 2
        else:
            up_source = down_source = w_refs[at_ref]
            at_ref += 1
        for p in range(4):
            there = slice(p * cols, (p + 1) * cols)
            j = ORDER[p] ^ rel
            if how == "whole":
                source = up_source.at[:, pl.ds(pl.multiple_of(j * width + part * cols, cols), cols)]
            else:
                source = up_source.at[pl.ds(pl.multiple_of(j * half, half), half)]
            up_copies.append(pltpu.make_async_copy(source, wu.at[at, there], w_sem.at[1]))
        p = ORDER.index(k)
        spot, sem = p * cols, w_sem.at[2]
        if how == "whole":
            source = down_source.at[part * cols : (part + 1) * cols]
            down_copies.append(pltpu.make_async_copy(source, wd.at[spot : spot + cols], sem))
        else:
            there = pl.ds(pl.multiple_of(spot + half_of(how) * (cols // 2), cols // 2), cols // 2)
            for b in range(3):
                line = 4 * half + b * (cols // 2)
                source = down_source.at[line : line + cols // 2]
                target = wd.at[there, b * cols : (b + 1) * cols]
                down_copies.append(pltpu.make_async_copy(source, target, sem))

    if first:
        pairs = [(x_in, x), (att_in, att), (g_in, g)]
    else:
        pairs = [(n2_in, n2), (g_in, g), (n2t_in, n2t)]
    if last:
        pairs += [(mid_in, mid)] + [(ref, parts.at[i]) for i, ref in enumerate(parts_in)]
    in_copies = [pltpu.make_async_copy(a, b, in_sem.at[i]) for i, (a, b) in enumerate(pairs)]
    if first:
        starts = in_copies[:2] + o_copies + up_copies + in_copies[2:] + down_copies
    else:
        starts = in_copies[:1] + up_copies + in_copies[1:2] + down_copies + in_copies[2:3]
    starts += o_copies + in_copies[3:] if last else []
    for copy in starts:
        copy.start()

    if first:
        for copy in (*in_copies[:2], *o_copies):
            copy.wait()
        mid[...] = x[...].astype(F32) + dot(att[...], wo[...]) + vec[3:4, :width]
        put(mid, mid_out)
        n, _ = normed(mid[...])
        n2[...] = (n * vec[4:5, :width] + vec[5:6, :width]).astype(BF16)
        put(n2, n2_out)
        spread(n2t, n2[...].T)
        put(n2t, n2t_out)
        spread(attt, att[...].T)
        put(attt, attt_out)
    else:
        in_copies[0].wait()

    bias = jnp.concatenate([bup[pl.ds((k ^ rel) * 3 + part, 1), :] for k in ORDER], axis=1)
    for copy in up_copies:
        copy.wait()
    up = dot(n2[...], wu[...]) + bias
    in_copies[2 if first else 1].wait()
    for copy in down_copies:
        copy.wait()
    d_hidden = dot_t(g[...], wd[...])
    cube = 0.044715 * up * up
    th = jnp.tanh(0.7978845608028654 * (up + cube * up))
    left = 0.5 * (1.0 + th)
    hid[...] = (up * left).astype(BF16)
    slope = left + (0.5 * 0.7978845608028654) * up * (1.0 - th * th) * (1.0 + 3.0 * cube)
    d_up = d_hidden * slope
    sums = jnp.sum(d_up, axis=0, keepdims=True)
    dup[...] = d_up.astype(BF16)
    gt[...] = g[...].T
    grad_down = dot(gt[...], hid[...])
    for p in range(4):
        bug_ref[pl.ds(ORDER[p] ^ rel, 1), :] = sums[:, p * cols : (p + 1) * cols]
        for r in range(4):
            block = slice(r * quarter, (r + 1) * quarter)
            stage[p, 4 + r] = grad_down[block, p * cols : (p + 1) * cols].astype(BF16)
    put(stage.at[0, 4:8], g_refs[1])
    put(stage.at[1, 4:8], g_refs[3])
    more, d_more = dot(hid[...], wd[...]), dot_t(dup[...], wu[...])
    if last:
        acc[...] = more
        dn2[...] = d_more
    else:
        low[0] = more.astype(BF16)
        low[1] = d_more.astype(BF16)
        put(low.at[0], acc_out)
        put(low.at[1], dn2_out)
    if not first:
        in_copies[2].wait()
    grad_up = dot(n2t[...], dup[...])
    for p in range(4):
        for r in range(4):
            block = slice(r * quarter, (r + 1) * quarter)
            stage[r, ORDER[p] ^ rel] = grad_up[block, p * cols : (p + 1) * cols].astype(BF16)
    put(stage.at[0, 0:4], g_refs[0])
    put(stage.at[1, 0:4], g_refs[2])
    put(stage.at[2], g_refs[4])
    put(stage.at[3], g_refs[5])

    if last:
        for copy in (*in_copies[3:], *o_copies):
            copy.wait()
        base = mid[...]
        n, inv = normed(base)
        d = dn2[...] + parts[1].astype(F32) + parts[3].astype(F32)
        ct = g[...].astype(F32)
        branch = (ct + norm_back(d, n, inv, vec[4:5, :width])).astype(BF16)
        low[0] = branch
        put(low.at[0], branch_out)
        hid2 = dot_t(branch, wo[...])
        for a, item in enumerate((branch.astype(F32), d * n, d, ct)):
            small_ref[a : a + 1, :] = jnp.sum(item, axis=0, keepdims=True)
        low[1] = hid2.astype(BF16)
        put(low.at[1], datt_out)
        total = base + acc[...] + parts[0].astype(F32) + parts[2].astype(F32) + vec[7:8, :width]
        low[2] = total.astype(BF16)
        put(low.at[2], out_out)
    for copy in out_copies:
        copy.wait()


def attend_back_kernel(q_ref, k_ref, v_ref, do_ref, o_ref, linv_ref, e_ref, tab, n1t_in, *refs, pos_dev, group):
    if group == 0:
        attt_in, branch_in, *refs = refs
    dq_ref, dk_ref, dv_ref, bias_ref, *refs = refs
    g_refs, refs = refs[: 6 if group == 0 else 4], refs[6 if group == 0 else 4 :]
    n1t, stage, in_sem, out_sem, *refs = refs
    if group == 0:
        attt, branch = refs
    rows, keys = q_ref.shape[0], k_ref.shape[0]
    quad = 2 * PAIR
    quarter = n1t_in.shape[0] // 4
    scale = 1.0 / 8.0
    i = pl.program_id(0)
    low_q, low_k = lanes((rows, PAIR)) < 64, lanes((keys, PAIR)) < 64
    pairs = [(n1t_in, n1t)] + ([(attt_in, attt), (branch_in, branch)] if group == 0 else [])
    in_copies = [pltpu.make_async_copy(a, b, in_sem.at[n]) for n, (a, b) in enumerate(pairs)]

    @pl.when(i == 0)
    def _():
        for copy in in_copies:
            copy.start()

    def unturn(t, first):
        parts = []
        for n in range(t.shape[0] // pos_dev):
            at = first[n] * pos_dev
            cosine, sine = tab[at : at + pos_dev, :PAIR], tab[at : at + pos_dev, PAIR:]
            part = t[n * pos_dev : (n + 1) * pos_dev]
            parts.append(part * cosine - swap_halves(part) * sine)
        return jnp.concatenate(parts, axis=0)

    def pair(at):
        q, k, v = q_ref[...], k_ref[...], v_ref[...]
        do = do_ref[...].astype(F32) * linv_ref[...]
        product = do * o_ref[...].astype(F32)
        do_b = do.astype(BF16)
        k_t = k.T
        do_h, v_h = [], []
        for h in range(2):
            here_q, here_k = (low_q, low_k) if h == 0 else (~low_q, ~low_k)
            free = 64 * (1 - h)
            delta = -jnp.sum(jnp.where(here_q, product, 0.0), axis=1, keepdims=True)
            high = delta.astype(BF16).astype(F32)
            lane_q, lane_k = lanes((rows, PAIR)), lanes((keys, PAIR))
            extra = jnp.where(lane_q == free, high, jnp.where(lane_q == free + 1, delta - high, 0.0))
            do_h.append(jnp.where(here_q, do, extra).astype(BF16))
            ones = jnp.where((lane_k == free) | (lane_k == free + 1), 1.0, 0.0).astype(BF16)
            v_h.append(jnp.where(here_k, v, ones))
        chunks = [slice(c * pos_dev, (c + 1) * pos_dev) for c in range(keys // pos_dev)]
        d_q = [jnp.zeros((PAIR, rows), F32) for _ in range(2)]
        d_k, d_v = [[], []], [[], []]
        steps = [(c, h) for c in chunks for h in range(2)]
        d_probs = dot_t(v_h[0][chunks[0]], do_h[0])
        for n, (c, h) in enumerate(steps):
            if n + 1 < len(steps):
                c_next, h_next = steps[n + 1]
                coming = dot_t(v_h[h_next][c_next], do_h[h_next])
            e = e_ref[h, c]
            d_scores = (d_probs * e.astype(F32)).astype(BF16)
            d_v[h].append(dot(e, do_b))
            d_k[h].append(dot(d_scores, q))
            d_q[h] = d_q[h] + dot(k_t[:, c], d_scores)
            d_probs = coming
        d_k, d_v = ([jnp.concatenate(item, axis=0) for item in both] for both in (d_k, d_v))
        d_q = [item.T for item in d_q]
        dv = jnp.where(low_k, d_v[0], d_v[1])
        dk = unturn(jnp.where(low_k, d_k[0], d_k[1]), [0, 0] + list(range(1, keys // pos_dev - 1)))
        dq = unturn(jnp.where(low_q, d_q[0], d_q[1]) * scale, [0, 0])
        dv_ref[:, at] = dv.astype(BF16)
        dk_ref[:, at] = dk.astype(BF16)
        dq_ref[:, at] = dq.astype(BF16)

    for a in range(2):

        @pl.when(i == a)
        def _(a=a):
            pair(slice(a * PAIR, (a + 1) * PAIR))

    def put(unit, grad):
        for r in range(4):
            stage[r, unit] = grad[r * quarter : (r + 1) * quarter].astype(BF16)

    if group == 0:

        @pl.when(i == 0)
        def _():
            in_copies[1].wait()
            in_copies[2].wait()
            for b in range(3):
                put(3 + b, dot(attt[...], branch[:, b * quad : (b + 1) * quad]))

    @pl.when(i == 1)
    def _():
        mine = (dq_ref, dk_ref, dv_ref)
        for a, ref in enumerate(mine):
            bias_ref[a : a + 1, :] = jnp.sum(ref[...].astype(F32), axis=0, keepdims=True)
        in_copies[0].wait()
        for a, ref in enumerate(mine):
            put(a, dot(n1t[:, : ref.shape[0]], ref[...]))
        if group == 0:
            sources = [stage.at[r, u : u + 3] for r in range(2) for u in (0, 3)] + [stage.at[2], stage.at[3]]
        else:
            sources = [stage.at[r] for r in range(4)]
        copies = [pltpu.make_async_copy(a, b, out_sem.at[n]) for n, (a, b) in enumerate(zip(sources, g_refs))]
        for copy in copies:
            copy.start()
        for copy in copies:
            copy.wait()


def input_back_kernel(slots, parents, x_ref, xr_ref, *refs, n_shard, n_branch, pos_dev, relative, hows):
    grads, refs = refs[:9], refs[9:]
    w_refs, refs = refs[: len(hows)], refs[len(hows) :]
    vec, dn1_ref, small_ref, *refs = refs
    outs, (w, d_in, acc, w_sem, d_sem) = refs[: 3 if relative else 1], refs[3 if relative else 1 :]
    rel = relative_to(relative)
    width = x_ref.shape[-1]
    quarter = width // 4
    quad = 2 * PAIR
    rows, keys = dn1_ref.shape[0], acc.shape[0]
    chosen, _ = chosen_pieces(slots, parents, n_shard, n_branch, pos_dev)

    def copies(a):
        out = []
        for ref, (k, how) in zip(w_refs, hows):
            source = ref.at[:, a * width : (a + 1) * width]
            out.append(pltpu.make_async_copy(source, w.at[a, row_block(k, rel, quarter, how)], w_sem.at[a]))
        n = rows if a == 0 else keys
        for g in range(3):
            target = d_in.at[a, 0:n, g * quad : (g + 1) * quad]
            out.append(pltpu.make_async_copy(grads[3 * a + g], target, d_sem.at[a]))
        return out

    for a in (1, 2, 0):
        for copy in copies(a):
            copy.start()
    for a in (1, 2, 0):
        for copy in copies(a):
            copy.wait()
        n = rows if a == 0 else keys
        more = dot_t(d_in[a, :n], w[a])
        if a == 1:
            acc[...] = more
        else:
            acc[:n] = acc[:n] + more
    total, plain = jnp.zeros((1, width), F32), jnp.zeros((1, width), F32)
    for t in range(keys // pos_dev):
        d = acc[t * pos_dev : (t + 1) * pos_dev]
        x = x_ref[t] if t < 2 else xr_ref[(t - 2) * pos_dev : (t - 1) * pos_dev]
        n, _ = normed(x.astype(F32))
        total = total + jnp.sum(d * n, axis=0, keepdims=True)
        plain = plain + jnp.sum(d, axis=0, keepdims=True)
        if t < 2:
            dn1_ref[t * pos_dev : (t + 1) * pos_dev] = d
    small_ref[0:1, :] = total
    small_ref[1:2, :] = plain
    if relative:
        parts = [acc[(2 + t) * pos_dev : (3 + t) * pos_dev] for t in range(len(chosen))]
        for k, ref in zip((3, 1, 2), outs):
            ref[...] = sum(
                jnp.where(holder ^ rel == k, 1.0, 0.0) * part for (holder, _, _), part in zip(chosen, parts)
            ).astype(BF16)
    else:
        outs[0][...] = jnp.zeros_like(outs[0])
        for t, (holder, _, _) in enumerate(chosen):
            part = acc[(2 + t) * pos_dev : (3 + t) * pos_dev]
            outs[0][holder] = (outs[0][holder].astype(F32) + part).astype(BF16)


def final_kernel(x_ref, branch_ref, dn1_ref, got_ref, vec, out_ref):
    i = pl.program_id(0)
    d = dn1_ref[...] + jnp.where(i == 1, 1.0, 0.0) * got_ref[...].astype(F32)
    n, inv = normed(x_ref[0].astype(F32))
    back = norm_back(d, n, inv, vec[0:1, : d.shape[1]])
    out_ref[0] = (branch_ref[...].astype(F32) + back).astype(BF16)


def swap(x, axis, bit):
    n = lax.axis_size(axis)
    return lax.ppermute(x, axis, [(i, i ^ bit) for i in range(n)])


def core(x):
    return swap(x, "shard", 1)


def across(x):
    return swap(x, "shard", 2)


def tie(x, *others):
    return lax.optimization_barrier((x, *others))[0]


def select_bit(bit, a, b):
    return jnp.where(bit == 1, b, a)


class Reduction:
    def __init__(self, chunk):
        *send, two, zero = chunk
        self.near = [(two, zero, len(send) // 2)]
        self.got = [core(item) for item in send]
        self.step = 0

    def more(self, chunk):
        *send, two, zero = chunk
        self.near.append((two, zero, len(send) // 2))
        self.got += [core(item) for item in send]

    def go(self, *after):
        got = tie(self.got, *after)
        r = lax.axis_index("rep")
        if self.step == 0:
            parts, kept = [], []
            for two, zero, n in self.near:
                parts.append(two + jnp.concatenate(got[:n], axis=0))
                kept.append(zero + jnp.concatenate(got[n : 2 * n], axis=0))
                got = got[2 * n :]
            self.part, self.kept = jnp.concatenate(parts, axis=0), jnp.concatenate(kept, axis=0)
            self.got = across(self.part)
        elif self.step in (1, 2):
            bit = self.step
            total = self.kept + got
            size = total.shape[1] // 2
            here = (r // bit) & 1
            self.kept = lax.dynamic_slice_in_dim(total, here * size, size, 1)
            self.part = lax.dynamic_slice_in_dim(total, (1 - here) * size, size, 1)
            self.got = swap(self.part, "rep", bit)
        elif self.step == 3:
            self.part = self.kept + got
            self.got = swap(self.part, "rep", 4)
        elif self.step == 4:
            self.part = self.part + got
            self.got = swap(self.part, "rep", 2)
        else:
            here = (r // 2) & 1
            self.part = jnp.concatenate(
                [select_bit(here, self.part, got), select_bit(here, got, self.part)], axis=1
            )
            self.got = swap(self.part, "rep", 1)
        self.step += 1
        return self.part


class SmallSum:
    LINKS = (("shard", 1), ("shard", 2), ("rep", 1), ("rep", 2), ("rep", 4))

    def __init__(self, x):
        self.part, self.step = x, 0
        self.got = swap(x, *self.LINKS[0])

    def go(self, *after):
        self.part = self.part + tie(self.got, *after)
        self.step += 1
        if self.step < 5:
            self.got = swap(self.part, *self.LINKS[self.step])
        return self.part


class FarGrad:
    def __init__(self, three, one, two):
        self.two, self.got, self.step = two, [core(three), core(one)], 0

    def go(self, *after):
        got = tie(self.got, *after)
        if self.step == 0:
            self.own = got[1]
            self.part = self.two + got[0]
            self.got = across(self.part)
        else:
            self.part = self.own + got
        self.step += 1
        return self.part


def collect_kernel(*refs, quarter):
    parts, (up_ref, down_ref, whole_ref) = refs[:6], refs[6:]
    half = quarter // 2
    y = lax.axis_index("rep") & 1
    cols = parts[0].shape[2]
    for p in range(3):
        for which in range(2):
            at = pl.ds(pl.multiple_of((y if which == 0 else 1 - y) * half, half), half)
            ref = parts[2 * p + which]
            for j in range(4):
                first = j * 3 * cols + p * cols
                up_ref[at, first : first + cols] = ref[j].astype(F32)
                whole_ref[j, at, :] = ref[4 + j].astype(F32)
        down_ref[p * cols : (p + 1) * cols, :] = whole_ref[...].reshape(4 * quarter, cols).T


def collect_qkv_kernel(*refs, quarter):
    parts, (out_ref, qkv_ref) = refs[:4], refs[4:]
    half = quarter // 2
    y = lax.axis_index("rep") & 1
    cols = parts[0].shape[2]
    for which in range(2):
        at = pl.ds(pl.multiple_of((y if which == 0 else 1 - y) * half, half), half)
        first, second = parts[which], parts[2 + which]
        for b in range(3):
            out_ref[at, b * cols : (b + 1) * cols] = first[3 + b].astype(F32)
        for a in range(3):
            for g, block in enumerate((first[a], second[a], second[3 + a])):
                qkv_ref[at, (3 * a + g) * cols : (3 * a + g + 1) * cols] = block.astype(F32)


def shards(
    states,
    cotangent,
    norm1_gain,
    norm1_bias,
    qkv_weight,
    qkv_bias,
    out_weight,
    out_bias,
    norm2_gain,
    norm2_bias,
    up_weight,
    up_bias,
    down_weight,
    down_bias,
    slots,
    parents,
):
    n_shard = lax.axis_size("shard")
    n_branch = n_shard // 4
    pos_dev, width = states.shape[1], states.shape[2]
    ff = up_weight.shape[1]
    rows = 2 * pos_dev
    n_far = n_branch + 1
    keys = rows + n_far * pos_dev
    relative = n_shard == 4 and lax.axis_size("rep") == 8
    quarter = width // 4
    cols = ff // 12
    quad = 2 * PAIR
    me = lax.axis_index("shard")
    sizes = dict(n_shard=n_shard, n_branch=n_branch, pos_dev=pos_dev)
    bound = functools.partial
    shape = jax.ShapeDtypeStruct
    vectors = (norm1_gain, norm1_bias, qkv_bias, out_bias, norm2_gain, norm2_bias, up_bias, down_bias)

    freq = jnp.exp(-jnp.log(10000.0) * jnp.arange(32, dtype=F32) / 32)
    freq = jnp.tile(freq, 4).reshape(1, PAIR)
    table = pl.pallas_call(
        bound(table_kernel, **sizes),
        out_shape=shape(((1 + n_far) * pos_dev, 2 * PAIR), F32),
        grid=(1,),
        in_specs=[SMEM, SMEM, whole((1, PAIR))],
        out_specs=whole(((1 + n_far) * pos_dev, 2 * PAIR)),
        compiler_params=params(),
        cost_estimate=cost(3.5),
        name="rotary_table",
    )(slots, parents, freq)

    natural = [(k, "whole") for k in range(4)]
    if relative:
        half = quarter // 2
        rest = 4 * half + 3 * (cols // 2)
        pack_shapes = [
            shape((pos_dev + 16, width), BF16),
            shape((rest + 3 * half, cols), BF16),
            shape((rest, cols), BF16),
            shape((rest, cols), BF16),
        ]
        packed = pl.pallas_call(
            bound(pack_kernel, quarter=quarter, width=width, cols=cols),
            out_shape=pack_shapes,
            grid=(1,),
            in_specs=[whole(item.shape) for item in vectors] + [ANY] * 4,
            out_specs=[whole(item.shape) for item in pack_shapes],
            scratch_shapes=[pltpu.VMEM((16, width), F32), pltpu.SemaphoreType.DMA((32,))],
            compiler_params=params(),
            cost_estimate=cost(2),
            name="pack",
        )
        q_two = across(qkv_weight)
        q_one = core(qkv_weight)
        x_own, *b_half = packed(*vectors, states, out_weight, up_weight, down_weight)
        x_one = core(x_own)
        x_two = across(x_own)
        x_two, _ = lax.optimization_barrier((x_two, table))
        x_far = [x_own, x_one, x_two, core(x_two)]
        w_qkv = [qkv_weight, q_one, q_two, core(q_two)]
        how_qkv = natural
        how_out = [(0, "whole"), (1, "whole"), (2, "direct"), (2, "via"), (3, "direct"), (3, "via")]
        o_one, u_one, d_one = core(out_weight), core(up_weight), core(down_weight)
        b_two = [across(tie(b_half[0], x_two, q_two))]
        vec, b_up = pl.pallas_call(
            bound(unpack_kernel, sizes=[item.shape[0] for item in vectors], pos_dev=pos_dev, cols=cols),
            out_shape=[shape((8, ff), F32), shape((12, cols), F32)],
            grid=(1,),
            in_specs=[ANY] * 4,
            out_specs=[whole((8, ff)), whole((12, cols))],
            scratch_shapes=[pltpu.VMEM((4, 16, width), BF16), pltpu.SemaphoreType.DMA((4,))],
            compiler_params=params(),
            cost_estimate=cost(2),
            name="unpack",
        )(*x_far)
    else:
        gather = lambda item: lax.all_gather(item, "shard", axis=0, tiled=True)
        rows_of = lambda item: [item[j * quarter : (j + 1) * quarter] for j in range(4)]
        w_qkv, how_qkv = rows_of(gather(qkv_weight)), natural
        x_far = [gather(states[1][None])]
        w_out, how_out = rows_of(gather(out_weight)), natural
        ups, downs = rows_of(gather(up_weight)), gather(down_weight)
        pieces = []
        for k in range(4):
            pieces += [ups[k], downs[k * width : (k + 1) * width]]
        w_ff, how_ff = [pieces] * 3, natural
        small = lax.all_gather(jnp.concatenate(vectors), "shard", axis=0)
        lines, at = [], 0
        for item in vectors:
            n = item.shape[0]
            line = small[:, at : at + n].reshape(1, n_shard * n).astype(F32)
            lines.append(jnp.pad(line, ((0, 0), (0, ff - n_shard * n))))
            at += n
        vec = jnp.concatenate(lines, axis=0)
        b_up = vec[6].reshape(12, cols)

    each = lambda i: (i, 0)
    n1t, q, k, v, x_seen = pl.pallas_call(
        bound(qkv_kernel, n_far=len(x_far), hows=how_qkv, relative=relative, **sizes),
        out_shape=[
            shape((width, keys), BF16),
            shape((rows, width), BF16),
            shape((keys, width), BF16),
            shape((keys, width), BF16),
            shape((n_far * pos_dev, width), BF16),
        ],
        grid=(3,),
        in_specs=[SMEM, SMEM, whole((2, pos_dev, width))]
        + [ANY] * (len(x_far) + len(how_qkv))
        + [whole((8, ff)), whole(((1 + n_far) * pos_dev, 2 * PAIR))],
        out_specs=[
            whole((width, keys)),
            pl.BlockSpec((rows, quad), lambda i: (0, i)),
            pl.BlockSpec((keys, quad), lambda i: (0, i)),
            pl.BlockSpec((keys, quad), lambda i: (0, i)),
            whole((n_far * pos_dev, width)),
        ],
        scratch_shapes=[
            pltpu.VMEM((3, width, 3 * quad), BF16),
            pltpu.VMEM((keys, width), BF16),
            pltpu.SemaphoreType.DMA((3,)),
            pltpu.SemaphoreType.DMA((n_far,)),
        ],
        compiler_params=params(),
        cost_estimate=cost(4),
        name="norm_qkv",
    )(slots, parents, states, *x_far, *w_qkv, vec, table)

    if relative:
        b_two[0] = tie(b_two[0], q)
        b_two += [across(tie(b_half[p], b_two[0])) for p in (1, 2)]
        b_via = [swap(b_two[0], "rep", 1)]
        b_three = [core(b_two[0])]

    pair = lambda i: (0, i)
    n_pair = width // PAIR
    e, attended, linv = pl.pallas_call(
        bound(attend_kernel, **sizes),
        out_shape=[
            shape((HEADS, keys, rows), BF16),
            shape((rows, width), BF16),
            shape((rows, width), F32),
        ],
        grid=(n_pair,),
        in_specs=[
            SMEM,
            SMEM,
            pl.BlockSpec((rows, PAIR), pair),
            pl.BlockSpec((keys, PAIR), pair),
            pl.BlockSpec((keys, PAIR), pair),
        ],
        out_specs=[
            pl.BlockSpec((2, keys, rows), lambda i: (i, 0, 0)),
            pl.BlockSpec((rows, PAIR), pair),
            pl.BlockSpec((rows, PAIR), pair),
        ],
        scratch_shapes=[pltpu.VMEM((keys, PAIR), BF16), pltpu.VMEM((rows, PAIR), BF16)],
        compiler_params=params(),
        cost_estimate=cost(17),
        name="attend",
    )(slots, parents, tie(q, b_two[0]) if relative else q, k, v)

    if relative:
        b_last = [core(tie(b_via[0], attended))]
        b_two[1:] = [tie(item, attended) for item in b_two[1:]]
        b_via += [swap(item, "rep", 1) for item in b_two[1:]]
        b_three += [core(item) for item in b_two[1:]]
        attended = tie(attended, b_last[0], *b_two[1:])
        w_out = [out_weight, o_one, b_two[0], b_via[0], b_three[0], b_last[0]]
        how_ff = how_out
        w_ff = [[up_weight, down_weight, u_one, d_one, b_two[0], b_via[0], b_three[0], b_last[0]]]

    x_rows = states.reshape(rows, width)
    g_rows = cotangent.reshape(rows, width)
    wide, low, turned = shape((rows, width), F32), shape((rows, width), BF16), shape((width, rows), BF16)

    def feed(part, ins, outs, scratch, vmem_out=()):
        weights = ([] if part == 1 else w_out) + w_ff[part]
        vm = lambda item: pltpu.VMEM(item.shape, item.dtype)
        outs = outs + list(vmem_out) + [shape((4, cols), F32)]
        grads = [shape((4, quarter, cols), BF16)] * 4 + [shape((8, quarter, cols), BF16)] * 2
        n_any = len(outs) - len(vmem_out) - 1
        result = pl.pallas_call(
            bound(ff_kernel, part=part, hows_o=how_out, hows=how_ff, relative=relative),
            out_shape=outs + grads,
            grid=(1,),
            in_specs=[ANY] * len(weights) + [whole((8, ff)), whole((12, cols))] + [ANY] * (1 + len(ins)),
            out_specs=[ANY] * n_any + [whole(item.shape) for item in outs[n_any:]] + [ANY] * 6,
            scratch_shapes=[
                pltpu.VMEM((width, 4 * cols), BF16),
                pltpu.VMEM((4 * cols, width), BF16),
                vm(low),
                vm(turned),
                vm(low),
                vm(turned),
                pltpu.VMEM((rows, 4 * cols), BF16),
                pltpu.VMEM((rows, 4 * cols), BF16),
                vm(wide),
                vm(wide),
                pltpu.VMEM((3, rows, width), BF16),
                pltpu.VMEM((4, 8, quarter, cols), BF16),
                pltpu.SemaphoreType.DMA((3,)),
                pltpu.SemaphoreType.DMA((8,)),
                pltpu.SemaphoreType.DMA((12,)),
            ]
            + scratch,
            compiler_params=params(),
            cost_estimate=cost(13),
            name=("feed_first", "feed_second", "feed_third")[part],
        )(*weights, vec, b_up, g_rows, *ins)
        return result[:-6], result[-6:]

    square = pltpu.VMEM((width, width), BF16)
    (mid, n2, n2t, attt, *parts, bug0), chunk0 = feed(
        0, (x_rows, attended), [wide, low, turned, turned, low, low],
        [square, pltpu.VMEM((rows, width), F32)] + [pltpu.VMEM((rows, width), BF16)] * 2 + [pltpu.VMEM((width, rows), BF16)],
    )
    if relative:
        sum0 = Reduction(chunk0)
        b_via[1:] = [tie(item, bug0) for item in b_via[1:]]
        b_last += [core(item) for item in b_via[1:]]
        w_ff += [
            [up_weight, down_weight, u_one, d_one, b_two[p], b_via[p], b_three[p], b_last[p]] for p in (1, 2)
        ]
        n2 = tie(n2, sum0.go(*b_via[1:]))
    (*more, bug1), chunk1 = feed(1, (n2, n2t), [low, low], [])
    if relative:
        sum1 = Reduction(chunk1)
        n2 = tie(n2, sum1.go(sum0.go(bug1)))
    (output, branch, d_att, small2, bug2), chunk2 = feed(
        2, (n2, n2t, *parts, *more, mid), [low, low, low],
        [square, pltpu.VMEM((rows, width), F32), pltpu.VMEM((4, rows, width), BF16)], [shape((8, width), F32)],
    )
    if relative:
        sum2 = Reduction(chunk2)

    def back(g, d_att, *more):
        here = lambda i: (0, 2 * g + i)
        grads = [shape((3, quarter, quad), BF16)] * 4
        if g == 0:
            grads += [shape((6, quarter, quad), BF16)] * 2
        outs = [shape((n, quad), t) for n, t in ((rows, BF16), (keys, BF16), (keys, BF16), (8, F32))]
        scratch = [
            pltpu.VMEM((width, keys), BF16),
            pltpu.VMEM((4, 6 if g == 0 else 3, quarter, quad), BF16),
            pltpu.SemaphoreType.DMA((3,)),
            pltpu.SemaphoreType.DMA((6,)),
        ] + [pltpu.VMEM(item.shape, item.dtype) for item in more]
        return pl.pallas_call(
            bound(attend_back_kernel, pos_dev=pos_dev, group=g),
            out_shape=outs + grads,
            grid=(2,),
            in_specs=[
                pl.BlockSpec((rows, PAIR), here),
                pl.BlockSpec((keys, PAIR), here),
                pl.BlockSpec((keys, PAIR), here),
                pl.BlockSpec((rows, PAIR), here),
                pl.BlockSpec((rows, PAIR), here),
                pl.BlockSpec((rows, PAIR), here),
                pl.BlockSpec((2, keys, rows), lambda i: (2 * g + i, 0, 0)),
                whole(((1 + n_far) * pos_dev, 2 * PAIR)),
                ANY,
            ]
            + [ANY] * len(more),
            out_specs=[whole(item.shape) for item in outs] + [ANY] * len(grads),
            scratch_shapes=scratch,
            compiler_params=params(40),
            cost_estimate=cost(11),
            name=f"attend_back_{g}",
        )(q, k, v, d_att, attended, linv, e, table, n1t, *more)

    def turns(last, *items):
        for item in items:
            last = item.go(last)
        return last

    backs = []
    for g in range(3):
        if relative:
            if g == 0:
                last = turns(small2, sum0, sum1, sum2)
            elif g == 1:
                last = turns(backs[0][3], sum0, sum1, sum2, sum3)
            else:
                last = turns(backs[1][3], sum0, sum1, sum2, sum3)
            d_att = tie(d_att, last)
        backs.append(back(g, d_att, *((attt, branch) if g == 0 else ())))
        if relative and g == 0:
            sum3 = Reduction(backs[0][4:])
        if relative and g == 1:
            sum4 = Reduction(backs[1][4:])
        if relative and g == 2:
            sum4.more(backs[2][4:])
    d_all = [backs[g][a] for a in range(3) for g in range(3)]
    small_qkv = jnp.concatenate([item[3][:3] for item in backs], axis=1)
    if relative:
        last = turns(backs[2][3], sum3, sum0, sum1, sum2, sum4)
        d_all[0] = tie(d_all[0], last)

    far_shapes = (
        [shape((pos_dev, width), BF16)] * 3
        if relative
        else [shape((n_shard, pos_dev, width), BF16)]
    )
    dn1, small1, *far = pl.pallas_call(
        bound(input_back_kernel, relative=relative, hows=how_qkv, **sizes),
        out_shape=[shape((rows, width), F32), shape((8, width), F32), *far_shapes],
        grid=(1,),
        in_specs=[SMEM, SMEM, whole((2, pos_dev, width)), whole((n_far * pos_dev, width))]
        + [ANY] * (9 + len(how_qkv))
        + [whole((8, ff))],
        out_specs=[whole((rows, width)), whole((8, width))] + [whole(item.shape) for item in far_shapes],
        scratch_shapes=[
            pltpu.VMEM((3, width, width), BF16),
            pltpu.VMEM((3, keys, width), BF16),
            pltpu.VMEM((keys, width), F32),
            pltpu.SemaphoreType.DMA((3,)),
            pltpu.SemaphoreType.DMA((3,)),
        ],
        compiler_params=params(40),
        cost_estimate=cost(10),
        name="input_back",
    )(slots, parents, states, x_seen, *d_all, *w_qkv, vec)

    collect = pl.pallas_call(
        bound(collect_kernel, quarter=quarter),
        out_shape=[shape((quarter, ff), F32), shape((ff // 4, width), F32)],
        scratch_shapes=[pltpu.VMEM((4, quarter, cols), F32)],
        compiler_params=params(40),
        cost_estimate=cost(4),
        name="collect",
    )
    vectors_grad = jnp.concatenate([small1[:2], small_qkv, small2[:4], jnp.concatenate([bug0, bug1, bug2], axis=1)], axis=0)
    if relative:
        far_sum = FarGrad(*far)
        small_sum = SmallSum(vectors_grad)
        order = [
            (sum0,), sum2, sum4, sum3, far_sum, small_sum, small_sum, sum1, sum4, small_sum, sum2, sum3, sum4, small_sum, sum3,
            sum4, far_sum, sum4, small_sum, None,
        ]
        last = small1
        for item in order:
            if isinstance(item, tuple):
                item[0].got, last = lax.optimization_barrier((item[0].got, last))
            elif item is None:
                halves = [half for part in (sum0, sum1, sum2) for half in (part.part, part.got)]
                grad_up, grad_down = collect(tie(halves[0], last), *halves[1:])
                last = grad_down
            else:
                last = item.go(last)
        counts = [item.step for item in (sum0, sum1, sum2, sum3, sum4)]
        assert counts == [6] * 5, counts
        got, total = far_sum.part, small_sum.part
    else:
        got = lax.psum_scatter(far[0], "shard", scatter_dimension=0)
        total = lax.psum(vectors_grad, ("rep", "shard"))
    states_grad = pl.pallas_call(
        final_kernel,
        out_shape=shape((2, pos_dev, width), BF16),
        grid=(2,),
        in_specs=[
            pl.BlockSpec((1, pos_dev, width), lambda i: (i, 0, 0)),
            pl.BlockSpec((pos_dev, width), each),
            pl.BlockSpec((pos_dev, width), each),
            whole((pos_dev, width)),
            whole((8, ff)),
        ],
        out_specs=pl.BlockSpec((1, pos_dev, width), lambda i: (i, 0, 0)),
        compiler_params=params(40),
        cost_estimate=cost(4),
        name="states_back",
    )(states, branch, dn1, got, vec)

    def up_of(parts):
        return jnp.stack([item[:4] for item in parts]).transpose(2, 1, 0, 3).reshape(-1, ff)

    def down_of(parts):
        return jnp.stack([item[4:8] for item in parts]).transpose(0, 3, 1, 2).reshape(3, -1, width)

    def out_of(part):
        return part[3:].transpose(1, 0, 2).reshape(-1, width)

    def qkv_of(parts):
        return jnp.stack(parts).transpose(2, 1, 0, 3).reshape(-1, 3 * width)

    if relative:
        grad_out, grad_qkv = pl.pallas_call(
            bound(collect_qkv_kernel, quarter=quarter),
            out_shape=[shape((quarter, width), F32), shape((quarter, 3 * width), F32)],
            compiler_params=params(40),
            cost_estimate=cost(2),
            name="collect_qkv",
        )(sum3.part, sum3.got, sum4.part, sum4.got)
    else:

        def natural_order(chunk):
            *send, two, zero = chunk
            n = len(send) // 2
            return [zero, jnp.concatenate(send[n:]), two, jnp.concatenate(send[:n])]

        parts = list(zip(*(natural_order(chunk) for chunk in (chunk0, chunk1, chunk2))))
        quads = list(zip(*(natural_order(item[4:]) for item in backs)))
        ups = jnp.concatenate([up_of(item) for item in parts], axis=0)
        downs = jnp.concatenate([down_of(item).reshape(-1, width) for item in parts], axis=0)
        outs = jnp.concatenate([out_of(item[0]) for item in quads], axis=0)
        qkvs = jnp.concatenate([qkv_of((a[:3], b, c)) for a, b, c in quads], axis=0)

        def reduced(item):
            part = lax.psum_scatter(item, "shard", scatter_dimension=0, tiled=True)
            return lax.psum(part, "rep").astype(F32)

        grad_up, grad_down, grad_out, grad_qkv = (reduced(item) for item in (ups, downs, outs, qkvs))

    def own_rows(first, count):
        line = total[first : first + count].reshape(-1)
        n = line.shape[0] // n_shard
        return lax.dynamic_slice_in_dim(line, me * n, n)

    return (
        output.reshape(2, pos_dev, width),
        states_grad,
        own_rows(0, 1),
        own_rows(1, 1),
        grad_qkv,
        own_rows(2, 3),
        grad_out,
        own_rows(5, 1),
        own_rows(6, 1),
        own_rows(7, 1),
        grad_up,
        own_rows(9, 4),
        grad_down,
        own_rows(8, 1),
    )


def solution(mesh):
    in_specs = (
        P(None, ("rep", "shard"), None),
        P(None, ("rep", "shard"), None),
        P("shard"),
        P("shard"),
        P("shard", None),
        P("shard"),
        P("shard", None),
        P("shard"),
        P("shard"),
        P("shard"),
        P("shard", None),
        P("shard"),
        P("shard", None),
        P("shard"),
        P("rep", None),
        P("rep", None),
    )
    out_specs = (
        P(None, ("rep", "shard"), None),
        P(None, ("rep", "shard"), None),
        P("shard"),
        P("shard"),
        P("shard", None),
        P("shard"),
        P("shard", None),
        P("shard"),
        P("shard"),
        P("shard"),
        P("shard", None),
        P("shard"),
        P("shard", None),
        P("shard"),
    )
    return jax.shard_map(shards, mesh=mesh, in_specs=in_specs, out_specs=out_specs, check_vma=False)
```

```python
import functools
import math

import jax
import jax.numpy as jnp
from jax import lax
from jax.experimental import pallas as pl
from jax.experimental.pallas import tpu as pltpu
from jax.sharding import PartitionSpec as P

HEADS = 12
BLOCK = 16
NEG = -1e30
PAIR = 128
F32 = jnp.float32
BF16 = jnp.bfloat16
ANY = pl.BlockSpec(memory_space=pltpu.HBM)


SMEM = pl.BlockSpec(memory_space=pltpu.SMEM)


def params(mib=58):
    return pltpu.CompilerParams(vmem_limit_bytes=mib * 2**20)


def cost(us):
    return pl.CostEstimate(flops=int(us * 1.15e9), bytes_accessed=0, transcendentals=0)


def whole(shape):
    return pl.BlockSpec(shape, lambda *_: (0,) * len(shape))


def place(rel):
    return jnp.where(rel == 3, 0, jnp.where(rel == 0, 3, rel))


ORDER = (3, 1, 2, 0)


def dot(a, b):
    return lax.dot_general(a, b, (((1,), (0,)), ((), ())), preferred_element_type=F32)


def dot_t(a, b):
    return lax.dot_general(a, b, (((1,), (1,)), ((), ())), preferred_element_type=F32)


def t_dot(a, b):
    return lax.dot_general(a, b, (((0,), (0,)), ((), ())), preferred_element_type=F32)


def normed(x):
    spread = x - jnp.mean(x, axis=-1, keepdims=True)
    inv = lax.rsqrt(jnp.mean(spread * spread, axis=-1, keepdims=True) + 1e-05)
    return spread * inv, inv


def norm_back(d, n, inv, gain):
    e = d * gain
    return inv * (
        e - jnp.mean(e, axis=-1, keepdims=True) - n * jnp.mean(e * n, axis=-1, keepdims=True)
    )


def lanes(shape):
    return lax.broadcasted_iota(jnp.int32, shape, len(shape) - 1)


def swap_halves(t):
    return jnp.where((lanes(t.shape) & 63) < 32, pltpu.roll(t, 96, 1), pltpu.roll(t, 32, 1))

def chosen_pieces(slots, parents, n_shard, n_branch, pos_dev):
    me = lax.axis_index("shard")
    mine = slots[0, me]
    seg = jnp.where(mine < n_branch, 0, mine - n_branch + 1)
    parent = parents[0, seg]

    def holder(piece):
        found = me
        for j in range(n_shard):
            found = jnp.where(slots[0, j] == piece, j, found)
        return found

    out = []
    for run in range(n_branch):
        valid = jnp.where(seg > 0, 1, jnp.where(mine > run, 1, 0))
        out.append((holder(run), valid, run * pos_dev))
    has = jnp.where(parent > 0, 1, 0)
    out.append((holder(jnp.where(parent > 0, n_branch + parent - 1, -1)), has, n_branch * pos_dev))
    start = jnp.where(
        mine < n_branch,
        mine * pos_dev,
        jnp.where(mine < 2 * n_branch, n_branch * pos_dev, (n_branch + 1) * pos_dev),
    )
    return out, start


def relative_to(relative):
    return lax.axis_index("shard") if relative else jnp.zeros((), jnp.int32)


def half_of(how):
    y = lax.axis_index("rep") & 1
    return y if how == "direct" else 1 - y


def row_block(k, rel, quarter, how, chunk=None):
    first = (k ^ rel) * quarter
    if how == "whole":
        return pl.ds(pl.multiple_of(first, 16), quarter)
    first = first + half_of(how) * (quarter // 2)
    if chunk is None:
        return pl.ds(pl.multiple_of(first, 16), quarter // 2)
    return pl.ds(pl.multiple_of(first + chunk * (quarter // 4), 16), quarter // 4)


def pack_kernel(*refs, quarter, width, cols):
    vectors, refs = refs[:8], refs[8:]
    states, w_out, w_up, w_down, s_out, *refs = refs
    b_outs, (small, sem) = refs[:3], refs[3:]
    half = quarter // 2
    y = lax.axis_index("rep") & 1
    at = pl.ds(pl.multiple_of(y * half, half), half)
    pos_dev = states.shape[1]
    copies = [(states.at[1], s_out.at[0:pos_dev])]
    for p in range(3):
        for j in range(4):
            source = w_up.at[at, j * width + p * cols : j * width + (p + 1) * cols]
            copies.append((source, b_outs[p].at[j * half : (j + 1) * half]))
        rows = pl.ds(pl.multiple_of(p * cols + y * (cols // 2), cols // 2), cols // 2)
        for b in range(3):
            first = 4 * half + b * (cols // 2)
            copies.append((w_down.at[rows, b * cols : (b + 1) * cols], b_outs[p].at[first : first + cols // 2]))
    for b in range(3):
        first = 4 * half + 3 * (cols // 2) + b * half
        copies.append((w_out.at[at, b * cols : (b + 1) * cols], b_outs[0].at[first : first + half]))
    copies = [pltpu.make_async_copy(a, b, sem.at[i]) for i, (a, b) in enumerate(copies)]
    for copy in copies:
        copy.start()
    small[...] = jnp.zeros_like(small)
    for r, ref in enumerate(vectors):
        small[r : r + 1, : ref.shape[0]] = ref[...].astype(F32).reshape(1, -1)
    s_out[pos_dev:, :] = small[...].astype(BF16)
    for copy in copies:
        copy.wait()


def unpack_kernel(a, b, c, d, vec_ref, up_ref, held, sem, *, sizes, pos_dev, cols):
    rel = lax.axis_index("shard")
    copies = [
        pltpu.make_async_copy(ref.at[pos_dev : pos_dev + 16], held.at[k ^ rel], sem.at[k])
        for k, ref in enumerate((a, b, c, d))
    ]
    for copy in copies:
        copy.start()
    for copy in copies:
        copy.wait()
    for j in range(4):
        part = held[j].astype(F32)
        for r, size in enumerate(sizes):
            vec_ref[r : r + 1, j * size : (j + 1) * size] = part[r : r + 1, :size]
        for p in range(3):
            up_ref[j * 3 + p : j * 3 + p + 1, :] = part[6:7, p * cols : (p + 1) * cols]


def table_kernel(slots, parents, freq_ref, out_ref, *, n_shard, n_branch, pos_dev):
    out, start = chosen_pieces(slots, parents, n_shard, n_branch, pos_dev)
    starts = [start] + [item[2] for item in out]
    shape = (pos_dev, PAIR)
    sign = jnp.where((lanes(shape) & 63) < 32, -1.0, 1.0)
    for i, first in enumerate(starts):
        pos = (lax.broadcasted_iota(jnp.int32, shape, 0) + first).astype(F32)
        angle = pos * freq_ref[...]
        out_ref[i * pos_dev : (i + 1) * pos_dev, :PAIR] = jnp.cos(angle)
        out_ref[i * pos_dev : (i + 1) * pos_dev, PAIR:] = jnp.sin(angle) * sign


def qkv_kernel(slots, parents, x_ref, *refs, n_shard, n_branch, pos_dev, n_far, hows, relative):
    far_refs, refs = refs[:n_far], refs[n_far:]
    w_refs, refs = refs[: len(hows)], refs[len(hows) :]
    vec, tab, n1t_ref, q_ref, k_ref, v_ref, xr_ref, w, n1, w_sem, far_sem = refs
    i = pl.program_id(0)
    rel = relative_to(relative)
    width = x_ref.shape[-1]
    quarter = width // 4
    quad = 2 * PAIR
    rows = 2 * pos_dev
    chosen, _ = chosen_pieces(slots, parents, n_shard, n_branch, pos_dev)

    def w_copies(g):
        out = []
        for ref, (k, how) in zip(w_refs, hows):
            for a in range(3):
                source = ref.at[:, a * width + g * quad : a * width + (g + 1) * quad]
                target = w.at[g, row_block(k, rel, quarter, how), a * quad : (a + 1) * quad]
                out.append(pltpu.make_async_copy(source, target, w_sem.at[g]))
        return out

    def far_copy(t, ref):
        return pltpu.make_async_copy(ref, xr_ref.at[t * pos_dev : (t + 1) * pos_dev], far_sem.at[t])

    @pl.when(i == 0)
    def _():
        for t, (holder, _, _) in enumerate(chosen):
            if n_far == 1:
                far_copy(t, far_refs[0].at[holder]).start()
            else:
                for k in range(n_far):

                    @pl.when(holder ^ rel == k)
                    def _(t=t, k=k):
                        far_copy(t, far_refs[k].at[0:pos_dev]).start()
        for g in range(3):
            for copy in w_copies(g):
                copy.start()
        for t in range(2 + len(chosen)):
            if t >= 2:
                far_copy(t - 2, far_refs[0].at[0:pos_dev] if n_far > 1 else far_refs[0].at[0]).wait()
            x = x_ref[t] if t < 2 else xr_ref[(t - 2) * pos_dev : (t - 1) * pos_dev]
            n, _ = normed(x.astype(F32))
            part = (n * vec[0:1, :width] + vec[1:2, :width]).astype(BF16)
            n1[t * pos_dev : (t + 1) * pos_dev] = part
            turned = part.T
            for j in range(4):
                at = pl.ds(pl.multiple_of(place(j ^ rel) * quarter, quarter), quarter)
                n1t_ref[at, t * pos_dev : (t + 1) * pos_dev] = turned[j * quarter : (j + 1) * quarter, :]

    for g in range(3):

        @pl.when(i == g)
        def _(g=g):
            for copy in w_copies(g):
                copy.wait()

            def product(a, n):
                bias = vec[2:3, a * width + g * quad : a * width + (g + 1) * quad]
                return dot(n1[:n], w[g, :, a * quad : (a + 1) * quad]) + bias

            def turn(y, ref, scale):
                for t in range(y.shape[0] // pos_dev):
                    first = max(t - 1, 0) * pos_dev
                    cosine, sine = tab[first : first + pos_dev, :PAIR], tab[first : first + pos_dev, PAIR:]
                    for h in range(2):
                        part = y[t * pos_dev : (t + 1) * pos_dev, h * PAIR : (h + 1) * PAIR]
                        out = part * cosine + swap_halves(part) * sine
                        ref[t * pos_dev : (t + 1) * pos_dev, h * PAIR : (h + 1) * PAIR] = (out * scale).astype(BF16)

            turn(product(0, rows), q_ref, 1.0 / math.sqrt(width // HEADS))
            turn(product(1, n1.shape[0]), k_ref, 1.0)
            v_ref[...] = product(2, n1.shape[0]).astype(BF16)


def attend_kernel(slots, parents, q_ref, k_ref, v_ref, e_ref, o_ref, linv_ref, k_aug, q_aug, *, n_shard, n_branch, pos_dev):
    rows, keys = q_ref.shape[0], k_ref.shape[0]
    blocks = pos_dev // BLOCK

    @pl.when(pl.program_id(0) == 0)
    def _():
        chosen, _ = chosen_pieces(slots, parents, n_shard, n_branch, pos_dev)
        shape = (pos_dev, PAIR)
        lane = lanes(shape) & 63
        block = lax.broadcasted_iota(jnp.int32, shape, 0) // BLOCK
        k_aug[:pos_dev] = jnp.where(lane - 32 == block, 1.0, 0.0).astype(BF16)
        k_aug[pos_dev : 2 * pos_dev] = jnp.where(lane == block, 1.0, 0.0).astype(BF16)
        for t, (_, valid, _) in enumerate(chosen):
            first = (2 + t) * pos_dev
            shut = jnp.where(valid > 0, 0.0, NEG)
            k_aug[first : first + pos_dev] = jnp.where(lane == 16, shut, 0.0).astype(BF16)
        for copy in range(2):
            clean = jnp.where((lane < blocks) & (lane >= block + copy), NEG, 0.0)
            noisy = (lane >= 32) & (lane < 32 + blocks)
            if copy == 0:
                noisy = noisy & (lane - 32 != block)
            out = jnp.where(noisy, NEG, clean)
            out = jnp.where(lane == 16, 1.0, out)
            q_aug[copy * pos_dev : (copy + 1) * pos_dev] = out.astype(BF16)

    low_q = lanes((rows, PAIR)) < 64
    low_k = lanes((keys, PAIR)) < 64
    q, k, v = q_ref[...], k_ref[...], v_ref[...]
    ones = jnp.ones_like(v)
    q_h = [jnp.where(low_q, q, q_aug[...]), jnp.where(low_q, q_aug[...], q)]
    k_h = [jnp.where(low_k, k, k_aug[...]), jnp.where(low_k, k_aug[...], k)]
    v_t = [jnp.where(low_k, v, ones).T, jnp.where(low_k, ones, v).T]
    chunks = [slice(c * pos_dev, (c + 1) * pos_dev) for c in range(keys // pos_dev)]

    def peak(scores):
        return functools.reduce(jnp.maximum, [jnp.max(item, axis=0, keepdims=True) for item in scores])

    def weigh(h, at, scores, top):
        e = jnp.exp(scores - top).astype(BF16)
        e_ref[h, at] = e
        return e

    scores = [[dot_t(k_h[0][at], q_h[0]) for at in chunks], []]
    weights = [[], []]
    outs = [jnp.zeros((PAIR, rows), F32) for _ in range(2)]
    top = peak(scores[0])
    for c, at in enumerate(chunks):
        scores[1].append(dot_t(k_h[1][at], q_h[1]))
        weights[0].append(weigh(0, at, scores[0][c], top))
    top = peak(scores[1])
    for c, at in enumerate(chunks):
        outs[0] = outs[0] + dot(v_t[0][:, at], weights[0][c])
        weights[1].append(weigh(1, at, scores[1][c], top))
    for c, at in enumerate(chunks):
        outs[1] = outs[1] + dot(v_t[1][:, at], weights[1][c])
    outs = [item.T for item in outs]
    total = jnp.where(low_q, pltpu.roll(outs[0], 64, 1), pltpu.roll(outs[1], 64, 1))
    inv = 1.0 / total
    linv_ref[...] = inv
    o_ref[...] = (jnp.where(low_q, outs[0], outs[1]) * inv).astype(BF16)


def ff_kernel(*refs, part, hows_o, hows, relative):
    first, last = part == 0, part == 2
    wo_refs, refs = (refs[: len(hows_o)], refs[len(hows_o) :]) if part != 1 else ((), refs)
    count = sum(2 if how == "whole" else 1 for _, how in hows)
    w_refs, refs = refs[:count], refs[count:]
    vec, bup, g_in, *refs = refs
    if first:
        x_in, att_in, mid_out, n2_out, n2t_out, attt_out, acc_out, dn2_out, *refs = refs
    elif not last:
        n2_in, n2t_in, acc_out, dn2_out, *refs = refs
    else:
        n2_in, n2t_in, *refs = refs
        parts_in, mid_in, out_out, branch_out, datt_out, small_ref, *refs = refs[:4], *refs[4:]
    bug_ref, *refs = refs
    g_refs, refs = refs[:6], refs[6:]
    wu, wd, g, gt, n2, n2t, hid, dup, acc, dn2, low, stage, w_sem, in_sem, out_sem, *refs = refs
    if first:
        wo, mid, x, att, attt = refs
    elif last:
        wo, mid, parts = refs
    rel = relative_to(relative)
    rows, width = g.shape
    quarter = width // 4
    cols = wu.shape[1] // 4
    half = quarter // 2
    out_copies = []

    def put(source, target):
        copy = pltpu.make_async_copy(source, target, out_sem.at[len(out_copies)])
        copy.start()
        out_copies.append(copy)

    def spread(ref, value):
        for j in range(4):
            at = pl.ds(pl.multiple_of(place(j ^ rel) * quarter, quarter), quarter)
            ref[at, :] = value[j * quarter : (j + 1) * quarter, :]

    o_copies = []
    for a, ref in enumerate(wo_refs):
        k, how = hows_o[a]
        at = row_block(k, rel, quarter, how)
        if how == "whole":
            o_copies.append(pltpu.make_async_copy(ref, wo.at[at], w_sem.at[0]))
        else:
            for b in range(3):
                line = 4 * half + 3 * (cols // 2) + b * half
                source = ref.at[line : line + half]
                o_copies.append(pltpu.make_async_copy(source, wo.at[at, b * cols : (b + 1) * cols], w_sem.at[0]))
    up_copies, down_copies = [], []
    at_ref = 0
    for k, how in hows:
        at = row_block(k, rel, quarter, how)
        if how == "whole":
            up_source, down_source = w_refs[at_ref], w_refs[at_ref + 1]
            at_ref += 2
        else:
            up_source = down_source = w_refs[at_ref]
            at_ref += 1
        for p in range(4):
            there = slice(p * cols, (p + 1) * cols)
            j = ORDER[p] ^ rel
            if how == "whole":
                source = up_source.at[:, pl.ds(pl.multiple_of(j * width + part * cols, cols), cols)]
            else:
                source = up_source.at[pl.ds(pl.multiple_of(j * half, half), half)]
            up_copies.append(pltpu.make_async_copy(source, wu.at[at, there], w_sem.at[1]))
        p = ORDER.index(k)
        spot, sem = p * cols, w_sem.at[2]
        if how == "whole":
            source = down_source.at[part * cols : (part + 1) * cols]
            down_copies.append(pltpu.make_async_copy(source, wd.at[spot : spot + cols], sem))
        else:
            there = pl.ds(pl.multiple_of(spot + half_of(how) * (cols // 2), cols // 2), cols // 2)
            for b in range(3):
                line = 4 * half + b * (cols // 2)
                source = down_source.at[line : line + cols // 2]
                target = wd.at[there, b * cols : (b + 1) * cols]
                down_copies.append(pltpu.make_async_copy(source, target, sem))

    if first:
        pairs = [(x_in, x), (att_in, att), (g_in, g)]
    else:
        pairs = [(n2_in, n2), (g_in, g), (n2t_in, n2t)]
    if last:
        pairs += [(mid_in, mid)] + [(ref, parts.at[i]) for i, ref in enumerate(parts_in)]
    in_copies = [pltpu.make_async_copy(a, b, in_sem.at[i]) for i, (a, b) in enumerate(pairs)]
    if first:
        starts = in_copies[:2] + o_copies + up_copies + in_copies[2:] + down_copies
    else:
        starts = in_copies[:1] + up_copies + in_copies[1:2] + down_copies + in_copies[2:3]
    starts += o_copies + in_copies[3:] if last else []
    for copy in starts:
        copy.start()

    if first:
        for copy in (*in_copies[:2], *o_copies):
            copy.wait()
        mid[...] = x[...].astype(F32) + dot(att[...], wo[...]) + vec[3:4, :width]
        put(mid, mid_out)
        n, _ = normed(mid[...])
        n2[...] = (n * vec[4:5, :width] + vec[5:6, :width]).astype(BF16)
        put(n2, n2_out)
        spread(n2t, n2[...].T)
        put(n2t, n2t_out)
        spread(attt, att[...].T)
        put(attt, attt_out)
    else:
        in_copies[0].wait()

    bias = jnp.concatenate([bup[pl.ds((k ^ rel) * 3 + part, 1), :] for k in ORDER], axis=1)
    for copy in up_copies:
        copy.wait()
    up = dot(n2[...], wu[...]) + bias
    in_copies[2 if first else 1].wait()
    for copy in down_copies:
        copy.wait()
    d_hidden = dot_t(g[...], wd[...])
    cube = 0.044715 * up * up
    th = jnp.tanh(0.7978845608028654 * (up + cube * up))
    left = 0.5 * (1.0 + th)
    hid[...] = (up * left).astype(BF16)
    slope = left + (0.5 * 0.7978845608028654) * up * (1.0 - th * th) * (1.0 + 3.0 * cube)
    d_up = d_hidden * slope
    sums = jnp.sum(d_up, axis=0, keepdims=True)
    dup[...] = d_up.astype(BF16)
    gt[...] = g[...].T
    grad_down = dot(gt[...], hid[...])
    for p in range(4):
        bug_ref[pl.ds(ORDER[p] ^ rel, 1), :] = sums[:, p * cols : (p + 1) * cols]
        for r in range(4):
            block = slice(r * quarter, (r + 1) * quarter)
            stage[p, 4 + r] = grad_down[block, p * cols : (p + 1) * cols].astype(BF16)
    put(stage.at[0, 4:8], g_refs[1])
    put(stage.at[1, 4:8], g_refs[3])
    more, d_more = dot(hid[...], wd[...]), dot_t(dup[...], wu[...])
    if last:
        acc[...] = more
        dn2[...] = d_more
    else:
        low[0] = more.astype(BF16)
        low[1] = d_more.astype(BF16)
        put(low.at[0], acc_out)
        put(low.at[1], dn2_out)
    if not first:
        in_copies[2].wait()
    grad_up = dot(n2t[...], dup[...])
    for p in range(4):
        for r in range(4):
            block = slice(r * quarter, (r + 1) * quarter)
            stage[r, ORDER[p] ^ rel] = grad_up[block, p * cols : (p + 1) * cols].astype(BF16)
    put(stage.at[0, 0:4], g_refs[0])
    put(stage.at[1, 0:4], g_refs[2])
    put(stage.at[2], g_refs[4])
    put(stage.at[3], g_refs[5])

    if last:
        for copy in (*in_copies[3:], *o_copies):
            copy.wait()
        base = mid[...]
        n, inv = normed(base)
        d = dn2[...] + parts[1].astype(F32) + parts[3].astype(F32)
        ct = g[...].astype(F32)
        branch = (ct + norm_back(d, n, inv, vec[4:5, :width])).astype(BF16)
        low[0] = branch
        put(low.at[0], branch_out)
        hid2 = dot_t(branch, wo[...])
        for a, item in enumerate((branch.astype(F32), d * n, d, ct)):
            small_ref[a : a + 1, :] = jnp.sum(item, axis=0, keepdims=True)
        low[1] = hid2.astype(BF16)
        put(low.at[1], datt_out)
        total = base + acc[...] + parts[0].astype(F32) + parts[2].astype(F32) + vec[7:8, :width]
        low[2] = total.astype(BF16)
        put(low.at[2], out_out)
    for copy in out_copies:
        copy.wait()


def attend_back_kernel(q_ref, k_ref, v_ref, do_ref, o_ref, linv_ref, e_ref, tab, n1t_in, *refs, pos_dev, group):
    if group == 0:
        attt_in, branch_in, *refs = refs
    dq_ref, dk_ref, dv_ref, bias_ref, *refs = refs
    g_refs, refs = refs[: 6 if group == 0 else 4], refs[6 if group == 0 else 4 :]
    n1t, stage, in_sem, out_sem, *refs = refs
    if group == 0:
        attt, branch = refs
    rows, keys = q_ref.shape[0], k_ref.shape[0]
    quad = 2 * PAIR
    quarter = n1t_in.shape[0] // 4
    scale = 1.0 / 8.0
    i = pl.program_id(0)
    low_q, low_k = lanes((rows, PAIR)) < 64, lanes((keys, PAIR)) < 64
    pairs = [(n1t_in, n1t)] + ([(attt_in, attt), (branch_in, branch)] if group == 0 else [])
    in_copies = [pltpu.make_async_copy(a, b, in_sem.at[n]) for n, (a, b) in enumerate(pairs)]

    @pl.when(i == 0)
    def _():
        for copy in in_copies:
            copy.start()

    def unturn(t, first):
        parts = []
        for n in range(t.shape[0] // pos_dev):
            at = first[n] * pos_dev
            cosine, sine = tab[at : at + pos_dev, :PAIR], tab[at : at + pos_dev, PAIR:]
            part = t[n * pos_dev : (n + 1) * pos_dev]
            parts.append(part * cosine - swap_halves(part) * sine)
        return jnp.concatenate(parts, axis=0)

    def pair(at):
        q, k, v = q_ref[...], k_ref[...], v_ref[...]
        do = do_ref[...].astype(F32) * linv_ref[...]
        product = do * o_ref[...].astype(F32)
        do_b = do.astype(BF16)
        k_t = k.T
        do_h, v_h = [], []
        for h in range(2):
            here_q, here_k = (low_q, low_k) if h == 0 else (~low_q, ~low_k)
            free = 64 * (1 - h)
            delta = -jnp.sum(jnp.where(here_q, product, 0.0), axis=1, keepdims=True)
            high = delta.astype(BF16).astype(F32)
            lane_q, lane_k = lanes((rows, PAIR)), lanes((keys, PAIR))
            extra = jnp.where(lane_q == free, high, jnp.where(lane_q == free + 1, delta - high, 0.0))
            do_h.append(jnp.where(here_q, do, extra).astype(BF16))
            ones = jnp.where((lane_k == free) | (lane_k == free + 1), 1.0, 0.0).astype(BF16)
            v_h.append(jnp.where(here_k, v, ones))
        chunks = [slice(c * pos_dev, (c + 1) * pos_dev) for c in range(keys // pos_dev)]
        d_q = [jnp.zeros((PAIR, rows), F32) for _ in range(2)]
        d_k, d_v = [[], []], [[], []]
        steps = [(c, h) for c in chunks for h in range(2)]
        d_probs = dot_t(v_h[0][chunks[0]], do_h[0])
        for n, (c, h) in enumerate(steps):
            if n + 1 < len(steps):
                c_next, h_next = steps[n + 1]
                coming = dot_t(v_h[h_next][c_next], do_h[h_next])
            e = e_ref[h, c]
            d_scores = (d_probs * e.astype(F32)).astype(BF16)
            d_v[h].append(dot(e, do_b))
            d_k[h].append(dot(d_scores, q))
            d_q[h] = d_q[h] + dot(k_t[:, c], d_scores)
            d_probs = coming
        d_k, d_v = ([jnp.concatenate(item, axis=0) for item in both] for both in (d_k, d_v))
        d_q = [item.T for item in d_q]
        dv = jnp.where(low_k, d_v[0], d_v[1])
        dk = unturn(jnp.where(low_k, d_k[0], d_k[1]), [0, 0] + list(range(1, keys // pos_dev - 1)))
        dq = unturn(jnp.where(low_q, d_q[0], d_q[1]) * scale, [0, 0])
        dv_ref[:, at] = dv.astype(BF16)
        dk_ref[:, at] = dk.astype(BF16)
        dq_ref[:, at] = dq.astype(BF16)

    for a in range(2):

        @pl.when(i == a)
        def _(a=a):
            pair(slice(a * PAIR, (a + 1) * PAIR))

    def put(unit, grad):
        for r in range(4):
            stage[r, unit] = grad[r * quarter : (r + 1) * quarter].astype(BF16)

    if group == 0:

        @pl.when(i == 0)
        def _():
            in_copies[1].wait()
            in_copies[2].wait()
            for b in range(3):
                put(3 + b, dot(attt[...], branch[:, b * quad : (b + 1) * quad]))

    @pl.when(i == 1)
    def _():
        mine = (dq_ref, dk_ref, dv_ref)
        for a, ref in enumerate(mine):
            bias_ref[a : a + 1, :] = jnp.sum(ref[...].astype(F32), axis=0, keepdims=True)
        in_copies[0].wait()
        for a, ref in enumerate(mine):
            put(a, dot(n1t[:, : ref.shape[0]], ref[...]))
        if group == 0:
            sources = [stage.at[r, u : u + 3] for r in range(2) for u in (0, 3)] + [stage.at[2], stage.at[3]]
        else:
            sources = [stage.at[r] for r in range(4)]
        copies = [pltpu.make_async_copy(a, b, out_sem.at[n]) for n, (a, b) in enumerate(zip(sources, g_refs))]
        for copy in copies:
            copy.start()
        for copy in copies:
            copy.wait()


def input_back_kernel(slots, parents, x_ref, xr_ref, *refs, n_shard, n_branch, pos_dev, relative, hows):
    grads, refs = refs[:9], refs[9:]
    w_refs, refs = refs[: len(hows)], refs[len(hows) :]
    vec, dn1_ref, small_ref, *refs = refs
    outs, (w, d_in, acc, w_sem, d_sem) = refs[: 3 if relative else 1], refs[3 if relative else 1 :]
    rel = relative_to(relative)
    width = x_ref.shape[-1]
    quarter = width // 4
    quad = 2 * PAIR
    rows, keys = dn1_ref.shape[0], acc.shape[0]
    chosen, _ = chosen_pieces(slots, parents, n_shard, n_branch, pos_dev)

    def copies(a):
        out = []
        for ref, (k, how) in zip(w_refs, hows):
            source = ref.at[:, a * width : (a + 1) * width]
            out.append(pltpu.make_async_copy(source, w.at[a, row_block(k, rel, quarter, how)], w_sem.at[a]))
        n = rows if a == 0 else keys
        for g in range(3):
            target = d_in.at[a, 0:n, g * quad : (g + 1) * quad]
            out.append(pltpu.make_async_copy(grads[3 * a + g], target, d_sem.at[a]))
        return out

    for a in (1, 2, 0):
        for copy in copies(a):
            copy.start()
    for a in (1, 2, 0):
        for copy in copies(a):
            copy.wait()
        n = rows if a == 0 else keys
        more = dot_t(d_in[a, :n], w[a])
        if a == 1:
            acc[...] = more
        else:
            acc[:n] = acc[:n] + more
    total, plain = jnp.zeros((1, width), F32), jnp.zeros((1, width), F32)
    for t in range(keys // pos_dev):
        d = acc[t * pos_dev : (t + 1) * pos_dev]
        x = x_ref[t] if t < 2 else xr_ref[(t - 2) * pos_dev : (t - 1) * pos_dev]
        n, _ = normed(x.astype(F32))
        total = total + jnp.sum(d * n, axis=0, keepdims=True)
        plain = plain + jnp.sum(d, axis=0, keepdims=True)
        if t < 2:
            dn1_ref[t * pos_dev : (t + 1) * pos_dev] = d
    small_ref[0:1, :] = total
    small_ref[1:2, :] = plain
    if relative:
        parts = [acc[(2 + t) * pos_dev : (3 + t) * pos_dev] for t in range(len(chosen))]
        for k, ref in zip((3, 1, 2), outs):
            ref[...] = sum(
                jnp.where(holder ^ rel == k, 1.0, 0.0) * part for (holder, _, _), part in zip(chosen, parts)
            ).astype(BF16)
    else:
        outs[0][...] = jnp.zeros_like(outs[0])
        for t, (holder, _, _) in enumerate(chosen):
            part = acc[(2 + t) * pos_dev : (3 + t) * pos_dev]
            outs[0][holder] = (outs[0][holder].astype(F32) + part).astype(BF16)


def final_kernel(x_ref, branch_ref, dn1_ref, got_ref, vec, out_ref):
    i = pl.program_id(0)
    d = dn1_ref[...] + jnp.where(i == 1, 1.0, 0.0) * got_ref[...].astype(F32)
    n, inv = normed(x_ref[0].astype(F32))
    back = norm_back(d, n, inv, vec[0:1, : d.shape[1]])
    out_ref[0] = (branch_ref[...].astype(F32) + back).astype(BF16)


def swap(x, axis, bit):
    n = lax.axis_size(axis)
    return lax.ppermute(x, axis, [(i, i ^ bit) for i in range(n)])


def core(x):
    return swap(x, "shard", 1)


def across(x):
    return swap(x, "shard", 2)


def tie(x, *others):
    return lax.optimization_barrier((x, *others))[0]


def select_bit(bit, a, b):
    return jnp.where(bit == 1, b, a)


class Reduction:
    def __init__(self, chunk):
        *send, two, zero = chunk
        self.near = [(two, zero, len(send) // 2)]
        self.got = [core(item) for item in send]
        self.step = 0

    def more(self, chunk):
        *send, two, zero = chunk
        self.near.append((two, zero, len(send) // 2))
        self.got += [core(item) for item in send]

    def go(self, *after):
        got = tie(self.got, *after)
        r = lax.axis_index("rep")
        if self.step == 0:
            parts, kept = [], []
            for two, zero, n in self.near:
                parts.append(two + jnp.concatenate(got[:n], axis=0))
                kept.append(zero + jnp.concatenate(got[n : 2 * n], axis=0))
                got = got[2 * n :]
            self.part, self.kept = jnp.concatenate(parts, axis=0), jnp.concatenate(kept, axis=0)
            self.got = across(self.part)
        elif self.step in (1, 2):
            bit = self.step
            total = self.kept + got
            size = total.shape[1] // 2
            here = (r // bit) & 1
            self.kept = lax.dynamic_slice_in_dim(total, here * size, size, 1)
            self.part = lax.dynamic_slice_in_dim(total, (1 - here) * size, size, 1)
            self.got = swap(self.part, "rep", bit)
        elif self.step == 3:
            self.part = self.kept + got
            self.got = swap(self.part, "rep", 4)
        elif self.step == 4:
            self.part = self.part + got
            self.got = swap(self.part, "rep", 2)
        else:
            here = (r // 2) & 1
            self.part = jnp.concatenate(
                [select_bit(here, self.part, got), select_bit(here, got, self.part)], axis=1
            )
            self.got = swap(self.part, "rep", 1)
        self.step += 1
        return self.part


class SmallSum:
    LINKS = (("shard", 1), ("shard", 2), ("rep", 1), ("rep", 2), ("rep", 4))

    def __init__(self, x):
        self.part, self.step = x, 0
        self.got = swap(x, *self.LINKS[0])

    def go(self, *after):
        self.part = self.part + tie(self.got, *after)
        self.step += 1
        if self.step < 5:
            self.got = swap(self.part, *self.LINKS[self.step])
        return self.part


class FarGrad:
    def __init__(self, three, one, two):
        self.two, self.got, self.step = two, [core(three), core(one)], 0

    def go(self, *after):
        got = tie(self.got, *after)
        if self.step == 0:
            self.own = got[1]
            self.part = self.two + got[0]
            self.got = across(self.part)
        else:
            self.part = self.own + got
        self.step += 1
        return self.part


def collect_kernel(*refs, quarter):
    parts, (up_ref, down_ref, whole_ref) = refs[:6], refs[6:]
    half = quarter // 2
    y = lax.axis_index("rep") & 1
    cols = parts[0].shape[2]
    for p in range(3):
        for which in range(2):
            at = pl.ds(pl.multiple_of((y if which == 0 else 1 - y) * half, half), half)
            ref = parts[2 * p + which]
            for j in range(4):
                first = j * 3 * cols + p * cols
                up_ref[at, first : first + cols] = ref[j].astype(F32)
                whole_ref[j, at, :] = ref[4 + j].astype(F32)
        down_ref[p * cols : (p + 1) * cols, :] = whole_ref[...].reshape(4 * quarter, cols).T


def collect_qkv_kernel(*refs, quarter):
    parts, (out_ref, qkv_ref) = refs[:4], refs[4:]
    half = quarter // 2
    y = lax.axis_index("rep") & 1
    cols = parts[0].shape[2]
    for which in range(2):
        at = pl.ds(pl.multiple_of((y if which == 0 else 1 - y) * half, half), half)
        first, second = parts[which], parts[2 + which]
        for b in range(3):
            out_ref[at, b * cols : (b + 1) * cols] = first[3 + b].astype(F32)
        for a in range(3):
            for g, block in enumerate((first[a], second[a], second[3 + a])):
                qkv_ref[at, (3 * a + g) * cols : (3 * a + g + 1) * cols] = block.astype(F32)


def shards(
    states,
    cotangent,
    norm1_gain,
    norm1_bias,
    qkv_weight,
    qkv_bias,
    out_weight,
    out_bias,
    norm2_gain,
    norm2_bias,
    up_weight,
    up_bias,
    down_weight,
    down_bias,
    slots,
    parents,
):
    n_shard = lax.axis_size("shard")
    n_branch = n_shard // 4
    pos_dev, width = states.shape[1], states.shape[2]
    ff = up_weight.shape[1]
    rows = 2 * pos_dev
    n_far = n_branch + 1
    keys = rows + n_far * pos_dev
    relative = n_shard == 4 and lax.axis_size("rep") == 8
    quarter = width // 4
    cols = ff // 12
    quad = 2 * PAIR
    me = lax.axis_index("shard")
    sizes = dict(n_shard=n_shard, n_branch=n_branch, pos_dev=pos_dev)
    bound = functools.partial
    shape = jax.ShapeDtypeStruct
    vectors = (norm1_gain, norm1_bias, qkv_bias, out_bias, norm2_gain, norm2_bias, up_bias, down_bias)

    freq = jnp.exp(-jnp.log(10000.0) * jnp.arange(32, dtype=F32) / 32)
    freq = jnp.tile(freq, 4).reshape(1, PAIR)
    table = pl.pallas_call(
        bound(table_kernel, **sizes),
        out_shape=shape(((1 + n_far) * pos_dev, 2 * PAIR), F32),
        grid=(1,),
        in_specs=[SMEM, SMEM, whole((1, PAIR))],
        out_specs=whole(((1 + n_far) * pos_dev, 2 * PAIR)),
        compiler_params=params(),
        cost_estimate=cost(3.5),
        name="rotary_table",
    )(slots, parents, freq)

    natural = [(k, "whole") for k in range(4)]
    if relative:
        half = quarter // 2
        rest = 4 * half + 3 * (cols // 2)
        pack_shapes = [
            shape((pos_dev + 16, width), BF16),
            shape((rest + 3 * half, cols), BF16),
            shape((rest, cols), BF16),
            shape((rest, cols), BF16),
        ]
        packed = pl.pallas_call(
            bound(pack_kernel, quarter=quarter, width=width, cols=cols),
            out_shape=pack_shapes,
            grid=(1,),
            in_specs=[whole(item.shape) for item in vectors] + [ANY] * 4,
            out_specs=[whole(item.shape) for item in pack_shapes],
            scratch_shapes=[pltpu.VMEM((16, width), F32), pltpu.SemaphoreType.DMA((32,))],
            compiler_params=params(),
            cost_estimate=cost(2),
            name="pack",
        )
        q_two = across(qkv_weight)
        q_one = core(qkv_weight)
        x_own, *b_half = packed(*vectors, states, out_weight, up_weight, down_weight)
        x_one = core(x_own)
        x_two = across(x_own)
        x_two, _ = lax.optimization_barrier((x_two, table))
        x_far = [x_own, x_one, x_two, core(x_two)]
        w_qkv = [qkv_weight, q_one, q_two, core(q_two)]
        how_qkv = natural
        how_out = [(0, "whole"), (1, "whole"), (2, "direct"), (2, "via"), (3, "direct"), (3, "via")]
        o_one = core(out_weight)
        b_two = [across(tie(b_half[0], x_two, q_two))]
        vec, b_up = pl.pallas_call(
            bound(unpack_kernel, sizes=[item.shape[0] for item in vectors], pos_dev=pos_dev, cols=cols),
            out_shape=[shape((8, ff), F32), shape((12, cols), F32)],
            grid=(1,),
            in_specs=[ANY] * 4,
            out_specs=[whole((8, ff)), whole((12, cols))],
            scratch_shapes=[pltpu.VMEM((4, 16, width), BF16), pltpu.SemaphoreType.DMA((4,))],
            compiler_params=params(),
            cost_estimate=cost(2),
            name="unpack",
        )(*x_far)
    else:
        gather = lambda item: lax.all_gather(item, "shard", axis=0, tiled=True)
        rows_of = lambda item: [item[j * quarter : (j + 1) * quarter] for j in range(4)]
        w_qkv, how_qkv = rows_of(gather(qkv_weight)), natural
        x_far = [gather(states[1][None])]
        w_out, how_out = rows_of(gather(out_weight)), natural
        ups, downs = rows_of(gather(up_weight)), gather(down_weight)
        pieces = []
        for k in range(4):
            pieces += [ups[k], downs[k * width : (k + 1) * width]]
        w_ff, how_ff = [pieces] * 3, natural
        small = lax.all_gather(jnp.concatenate(vectors), "shard", axis=0)
        lines, at = [], 0
        for item in vectors:
            n = item.shape[0]
            line = small[:, at : at + n].reshape(1, n_shard * n).astype(F32)
            lines.append(jnp.pad(line, ((0, 0), (0, ff - n_shard * n))))
            at += n
        vec = jnp.concatenate(lines, axis=0)
        b_up = vec[6].reshape(12, cols)

    each = lambda i: (i, 0)
    n1t, q, k, v, x_seen = pl.pallas_call(
        bound(qkv_kernel, n_far=len(x_far), hows=how_qkv, relative=relative, **sizes),
        out_shape=[
            shape((width, keys), BF16),
            shape((rows, width), BF16),
            shape((keys, width), BF16),
            shape((keys, width), BF16),
            shape((n_far * pos_dev, width), BF16),
        ],
        grid=(3,),
        in_specs=[SMEM, SMEM, whole((2, pos_dev, width))]
        + [ANY] * (len(x_far) + len(how_qkv))
        + [whole((8, ff)), whole(((1 + n_far) * pos_dev, 2 * PAIR))],
        out_specs=[
            whole((width, keys)),
            pl.BlockSpec((rows, quad), lambda i: (0, i)),
            pl.BlockSpec((keys, quad), lambda i: (0, i)),
            pl.BlockSpec((keys, quad), lambda i: (0, i)),
            whole((n_far * pos_dev, width)),
        ],
        scratch_shapes=[
            pltpu.VMEM((3, width, 3 * quad), BF16),
            pltpu.VMEM((keys, width), BF16),
            pltpu.SemaphoreType.DMA((3,)),
            pltpu.SemaphoreType.DMA((n_far,)),
        ],
        compiler_params=params(),
        cost_estimate=cost(4),
        name="norm_qkv",
    )(slots, parents, states, *x_far, *w_qkv, vec, table)

    if relative:
        b_two[0] = tie(b_two[0], q)
        u_one, d_one = core(tie(up_weight, q)), core(tie(down_weight, q))
        b_two += [across(tie(b_half[p], b_two[0])) for p in (1, 2)]
        b_via = [swap(b_two[0], "rep", 1)]
        b_three = [core(b_two[0])]

    pair = lambda i: (0, i)
    n_pair = width // PAIR
    e, attended, linv = pl.pallas_call(
        bound(attend_kernel, **sizes),
        out_shape=[
            shape((HEADS, keys, rows), BF16),
            shape((rows, width), BF16),
            shape((rows, width), F32),
        ],
        grid=(n_pair,),
        in_specs=[
            SMEM,
            SMEM,
            pl.BlockSpec((rows, PAIR), pair),
            pl.BlockSpec((keys, PAIR), pair),
            pl.BlockSpec((keys, PAIR), pair),
        ],
        out_specs=[
            pl.BlockSpec((2, keys, rows), lambda i: (i, 0, 0)),
            pl.BlockSpec((rows, PAIR), pair),
            pl.BlockSpec((rows, PAIR), pair),
        ],
        scratch_shapes=[pltpu.VMEM((keys, PAIR), BF16), pltpu.VMEM((rows, PAIR), BF16)],
        compiler_params=params(),
        cost_estimate=cost(17),
        name="attend",
    )(slots, parents, tie(q, b_two[0]) if relative else q, k, v)

    if relative:
        b_last = [core(tie(b_via[0], attended))]
        b_two[1] = tie(b_two[1], attended)
        b_via.append(swap(b_two[1], "rep", 1))
        b_three.append(core(b_two[1]))
        attended = tie(attended, b_last[0], b_two[1])
        w_out = [out_weight, o_one, b_two[0], b_via[0], b_three[0], b_last[0]]
        how_ff = how_out
        w_ff = [[up_weight, down_weight, u_one, d_one, b_two[0], b_via[0], b_three[0], b_last[0]]]

    x_rows = states.reshape(rows, width)
    g_rows = cotangent.reshape(rows, width)
    wide, low, turned = shape((rows, width), F32), shape((rows, width), BF16), shape((width, rows), BF16)

    def feed(part, ins, outs, scratch, vmem_out=()):
        weights = ([] if part == 1 else w_out) + w_ff[part]
        vm = lambda item: pltpu.VMEM(item.shape, item.dtype)
        outs = outs + list(vmem_out) + [shape((4, cols), F32)]
        grads = [shape((4, quarter, cols), BF16)] * 4 + [shape((8, quarter, cols), BF16)] * 2
        n_any = len(outs) - len(vmem_out) - 1
        result = pl.pallas_call(
            bound(ff_kernel, part=part, hows_o=how_out, hows=how_ff, relative=relative),
            out_shape=outs + grads,
            grid=(1,),
            in_specs=[ANY] * len(weights) + [whole((8, ff)), whole((12, cols))] + [ANY] * (1 + len(ins)),
            out_specs=[ANY] * n_any + [whole(item.shape) for item in outs[n_any:]] + [ANY] * 6,
            scratch_shapes=[
                pltpu.VMEM((width, 4 * cols), BF16),
                pltpu.VMEM((4 * cols, width), BF16),
                vm(low),
                vm(turned),
                vm(low),
                vm(turned),
                pltpu.VMEM((rows, 4 * cols), BF16),
                pltpu.VMEM((rows, 4 * cols), BF16),
                vm(wide),
                vm(wide),
                pltpu.VMEM((3, rows, width), BF16),
                pltpu.VMEM((4, 8, quarter, cols), BF16),
                pltpu.SemaphoreType.DMA((3,)),
                pltpu.SemaphoreType.DMA((8,)),
                pltpu.SemaphoreType.DMA((12,)),
            ]
            + scratch,
            compiler_params=params(),
            cost_estimate=cost(13),
            name=("feed_first", "feed_second", "feed_third")[part],
        )(*weights, vec, b_up, g_rows, *ins)
        return result[:-6], result[-6:]

    square = pltpu.VMEM((width, width), BF16)
    (mid, n2, n2t, attt, *parts, bug0), chunk0 = feed(
        0, (x_rows, attended), [wide, low, turned, turned, low, low],
        [square, pltpu.VMEM((rows, width), F32)] + [pltpu.VMEM((rows, width), BF16)] * 2 + [pltpu.VMEM((width, rows), BF16)],
    )
    if relative:
        sum0 = Reduction(chunk0)
        b_via[1] = tie(b_via[1], bug0)
        b_last.append(core(b_via[1]))
        b_two[2] = tie(b_two[2], bug0)
        b_via.append(swap(b_two[2], "rep", 1))
        b_three.append(core(b_two[2]))
        w_ff.append([up_weight, down_weight, u_one, d_one, b_two[1], b_via[1], b_three[1], b_last[1]])
        n2 = tie(n2, sum0.go(b_via[1]), b_two[2])
    (*more, bug1), chunk1 = feed(1, (n2, n2t), [low, low], [])
    if relative:
        sum1 = Reduction(chunk1)
        b_via[2] = tie(b_via[2], bug1)
        b_last.append(core(b_via[2]))
        w_ff.append([up_weight, down_weight, u_one, d_one, b_two[2], b_via[2], b_three[2], b_last[2]])
        n2 = tie(n2, sum1.go(sum0.go(bug1)), b_via[2])
    (output, branch, d_att, small2, bug2), chunk2 = feed(
        2, (n2, n2t, *parts, *more, mid), [low, low, low],
        [square, pltpu.VMEM((rows, width), F32), pltpu.VMEM((4, rows, width), BF16)], [shape((8, width), F32)],
    )
    if relative:
        sum2 = Reduction(chunk2)

    def back(g, d_att, *more):
        here = lambda i: (0, 2 * g + i)
        grads = [shape((3, quarter, quad), BF16)] * 4
        if g == 0:
            grads += [shape((6, quarter, quad), BF16)] * 2
        outs = [shape((n, quad), t) for n, t in ((rows, BF16), (keys, BF16), (keys, BF16), (8, F32))]
        scratch = [
            pltpu.VMEM((width, keys), BF16),
            pltpu.VMEM((4, 6 if g == 0 else 3, quarter, quad), BF16),
            pltpu.SemaphoreType.DMA((3,)),
            pltpu.SemaphoreType.DMA((6,)),
        ] + [pltpu.VMEM(item.shape, item.dtype) for item in more]
        return pl.pallas_call(
            bound(attend_back_kernel, pos_dev=pos_dev, group=g),
            out_shape=outs + grads,
            grid=(2,),
            in_specs=[
                pl.BlockSpec((rows, PAIR), here),
                pl.BlockSpec((keys, PAIR), here),
                pl.BlockSpec((keys, PAIR), here),
                pl.BlockSpec((rows, PAIR), here),
                pl.BlockSpec((rows, PAIR), here),
                pl.BlockSpec((rows, PAIR), here),
                pl.BlockSpec((2, keys, rows), lambda i: (2 * g + i, 0, 0)),
                whole(((1 + n_far) * pos_dev, 2 * PAIR)),
                ANY,
            ]
            + [ANY] * len(more),
            out_specs=[whole(item.shape) for item in outs] + [ANY] * len(grads),
            scratch_shapes=scratch,
            compiler_params=params(40),
            cost_estimate=cost(11),
            name=f"attend_back_{g}",
        )(q, k, v, d_att, attended, linv, e, table, n1t, *more)

    def turns(last, *items):
        for item in items:
            last = item.go(last)
        return last

    backs = []
    for g in range(3):
        if relative:
            if g == 0:
                last = turns(small2, sum0, sum1, sum2)
            elif g == 1:
                last = turns(backs[0][3], sum0, sum1, sum2, sum3)
            else:
                last = turns(backs[1][3], sum0, sum1, sum2, sum3)
            d_att = tie(d_att, last)
        backs.append(back(g, d_att, *((attt, branch) if g == 0 else ())))
        if relative and g == 0:
            sum3 = Reduction(backs[0][4:])
        if relative and g == 1:
            sum4 = Reduction(backs[1][4:])
        if relative and g == 2:
            sum4.more(backs[2][4:])
    d_all = [backs[g][a] for a in range(3) for g in range(3)]
    small_qkv = jnp.concatenate([item[3][:3] for item in backs], axis=1)
    if relative:
        last = turns(backs[2][3], sum3, sum0, sum1, sum2, sum4)
        d_all[0] = tie(d_all[0], last)

    far_shapes = (
        [shape((pos_dev, width), BF16)] * 3
        if relative
        else [shape((n_shard, pos_dev, width), BF16)]
    )
    dn1, small1, *far = pl.pallas_call(
        bound(input_back_kernel, relative=relative, hows=how_qkv, **sizes),
        out_shape=[shape((rows, width), F32), shape((8, width), F32), *far_shapes],
        grid=(1,),
        in_specs=[SMEM, SMEM, whole((2, pos_dev, width)), whole((n_far * pos_dev, width))]
        + [ANY] * (9 + len(how_qkv))
        + [whole((8, ff))],
        out_specs=[whole((rows, width)), whole((8, width))] + [whole(item.shape) for item in far_shapes],
        scratch_shapes=[
            pltpu.VMEM((3, width, width), BF16),
            pltpu.VMEM((3, keys, width), BF16),
            pltpu.VMEM((keys, width), F32),
            pltpu.SemaphoreType.DMA((3,)),
            pltpu.SemaphoreType.DMA((3,)),
        ],
        compiler_params=params(40),
        cost_estimate=cost(10),
        name="input_back",
    )(slots, parents, states, x_seen, *d_all, *w_qkv, vec)

    collect = pl.pallas_call(
        bound(collect_kernel, quarter=quarter),
        out_shape=[shape((quarter, ff), F32), shape((ff // 4, width), F32)],
        scratch_shapes=[pltpu.VMEM((4, quarter, cols), F32)],
        compiler_params=params(40),
        cost_estimate=cost(4),
        name="collect",
    )
    vectors_grad = jnp.concatenate([small1[:2], small_qkv, small2[:4], jnp.concatenate([bug0, bug1, bug2], axis=1)], axis=0)
    if relative:
        far_sum = FarGrad(*far)
        small_sum = SmallSum(vectors_grad)
        order = [
            (sum0,), sum2, sum4, sum3, far_sum, small_sum, small_sum, sum1, sum4, small_sum, sum2, sum3, sum4, small_sum, sum3,
            sum4, far_sum, sum4, small_sum, None,
        ]
        last = small1
        for item in order:
            if isinstance(item, tuple):
                item[0].got, last = lax.optimization_barrier((item[0].got, last))
            elif item is None:
                halves = [half for part in (sum0, sum1, sum2) for half in (part.part, part.got)]
                grad_up, grad_down = collect(tie(halves[0], last), *halves[1:])
                last = grad_down
            else:
                last = item.go(last)
        counts = [item.step for item in (sum0, sum1, sum2, sum3, sum4)]
        assert counts == [6] * 5, counts
        got, total = far_sum.part, small_sum.part
    else:
        got = lax.psum_scatter(far[0], "shard", scatter_dimension=0)
        total = lax.psum(vectors_grad, ("rep", "shard"))
    states_grad = pl.pallas_call(
        final_kernel,
        out_shape=shape((2, pos_dev, width), BF16),
        grid=(2,),
        in_specs=[
            pl.BlockSpec((1, pos_dev, width), lambda i: (i, 0, 0)),
            pl.BlockSpec((pos_dev, width), each),
            pl.BlockSpec((pos_dev, width), each),
            whole((pos_dev, width)),
            whole((8, ff)),
        ],
        out_specs=pl.BlockSpec((1, pos_dev, width), lambda i: (i, 0, 0)),
        compiler_params=params(40),
        cost_estimate=cost(4),
        name="states_back",
    )(states, branch, dn1, got, vec)

    def up_of(parts):
        return jnp.stack([item[:4] for item in parts]).transpose(2, 1, 0, 3).reshape(-1, ff)

    def down_of(parts):
        return jnp.stack([item[4:8] for item in parts]).transpose(0, 3, 1, 2).reshape(3, -1, width)

    def out_of(part):
        return part[3:].transpose(1, 0, 2).reshape(-1, width)

    def qkv_of(parts):
        return jnp.stack(parts).transpose(2, 1, 0, 3).reshape(-1, 3 * width)

    if relative:
        grad_out, grad_qkv = pl.pallas_call(
            bound(collect_qkv_kernel, quarter=quarter),
            out_shape=[shape((quarter, width), F32), shape((quarter, 3 * width), F32)],
            compiler_params=params(40),
            cost_estimate=cost(2),
            name="collect_qkv",
        )(sum3.part, sum3.got, sum4.part, sum4.got)
    else:

        def natural_order(chunk):
            *send, two, zero = chunk
            n = len(send) // 2
            return [zero, jnp.concatenate(send[n:]), two, jnp.concatenate(send[:n])]

        parts = list(zip(*(natural_order(chunk) for chunk in (chunk0, chunk1, chunk2))))
        quads = list(zip(*(natural_order(item[4:]) for item in backs)))
        ups = jnp.concatenate([up_of(item) for item in parts], axis=0)
        downs = jnp.concatenate([down_of(item).reshape(-1, width) for item in parts], axis=0)
        outs = jnp.concatenate([out_of(item[0]) for item in quads], axis=0)
        qkvs = jnp.concatenate([qkv_of((a[:3], b, c)) for a, b, c in quads], axis=0)

        def reduced(item):
            part = lax.psum_scatter(item, "shard", scatter_dimension=0, tiled=True)
            return lax.psum(part, "rep").astype(F32)

        grad_up, grad_down, grad_out, grad_qkv = (reduced(item) for item in (ups, downs, outs, qkvs))

    def own_rows(first, count):
        line = total[first : first + count].reshape(-1)
        n = line.shape[0] // n_shard
        return lax.dynamic_slice_in_dim(line, me * n, n)

    return (
        output.reshape(2, pos_dev, width),
        states_grad,
        own_rows(0, 1),
        own_rows(1, 1),
        grad_qkv,
        own_rows(2, 3),
        grad_out,
        own_rows(5, 1),
        own_rows(6, 1),
        own_rows(7, 1),
        grad_up,
        own_rows(9, 4),
        grad_down,
        own_rows(8, 1),
    )


def solution(mesh):
    in_specs = (
        P(None, ("rep", "shard"), None),
        P(None, ("rep", "shard"), None),
        P("shard"),
        P("shard"),
        P("shard", None),
        P("shard"),
        P("shard", None),
        P("shard"),
        P("shard"),
        P("shard"),
        P("shard", None),
        P("shard"),
        P("shard", None),
        P("shard"),
        P("rep", None),
        P("rep", None),
    )
    out_specs = (
        P(None, ("rep", "shard"), None),
        P(None, ("rep", "shard"), None),
        P("shard"),
        P("shard"),
        P("shard", None),
        P("shard"),
        P("shard", None),
        P("shard"),
        P("shard"),
        P("shard"),
        P("shard", None),
        P("shard"),
        P("shard", None),
        P("shard"),
    )
    return jax.shard_map(shards, mesh=mesh, in_specs=in_specs, out_specs=out_specs, check_vma=False)
```
